32 devices in a mesh: dp: 8 (over z, y), mp: 4 (over x, core).
Axes of the slice: x: 2, y: 2, z: 4, core: 2. Of those that a mesh axis runs over, the one named last changes fastest.
Arguments:
- features: bfloat16 [9216, 1024], P('dp'), may hold values from -6 to 6
- stem_weight: bfloat16 [1024, 1024], P(None, 'mp'), may hold values from -0.1875 to 0.1875
- group_gain: float32 [1024], P('mp'), may hold values from 0.1 to 1.9
- group_bias: float32 [1024], P('mp'), may hold values from -3 to 3
- embed_weight: bfloat16 [1024, 768], P('mp'), may hold values from -0.1875 to 0.1875
- first_gain: float32 [768], replicated, may hold values from 0.1 to 1.9
- first_bias: float32 [768], replicated, may hold values from -2 to 2
- project_in: bfloat16 [768, 2304], P(None, 'mp'), may hold values from -0.21875 to 0.21875
- project_out: bfloat16 [768, 768], P('mp'), may hold values from -3 to 3
- second_gain: float32 [768], replicated, may hold values from 0.1 to 1.9
- second_bias: float32 [768], replicated, may hold values from -2 to 2
- up_weight: bfloat16 [768, 3072], P(None, 'mp'), may hold values from -0.21875 to 0.21875
- up_bias: float32 [3072], P('mp'), may hold values from -3 to 3
- down_weight: bfloat16 [3072, 768], P('mp'), may hold values from -0.109375 to 0.109375
- valid_mask: int32 [16, 576], replicated, may hold values from 0 to 1, as said below
- slot_slice: int32 [16], P('dp'), may hold values from 0 to 15, each once
- cotangent: bfloat16 [9216, 768], P(('dp', 'mp')), may hold values from -6 to 6
Outputs:
- block_out: bfloat16 [9216, 768], P(('dp', 'mp'))
- features_grad: float32 [9216, 1024], P(('dp', 'mp'))
- stem_weight_grad: float32 [1024, 1024], P(None, 'mp')
- group_gain_grad: float32 [1024], P('mp')
- group_bias_grad: float32 [1024], P('mp')
- embed_weight_grad: float32 [1024, 768], P('mp')
- first_gain_grad: float32 [768], replicated
- first_bias_grad: float32 [768], replicated
- project_in_grad: float32 [768, 2304], P(None, 'mp')
- project_out_grad: float32 [768, 768], P('mp')
- second_gain_grad: float32 [768], replicated
- second_bias_grad: float32 [768], replicated
- up_weight_grad: float32 [768, 3072], P(None, 'mp')
- up_bias_grad: float32 [3072], P('mp')
- down_weight_grad: float32 [3072, 768], P('mp')
The draws below stay inside these ranges and needn't reach their ends.
Inputs may be any that keep to these rules, and one draw needn't show every extreme that they name: `valid_mask`: row s is 1 at the positions below slice s's valid length, 196 or 576, and 0 after; half of the slices have each length. `slot_slice`: each slice stands in exactly one slot; slots j * 2 to (j + 1) * 2 - 1 are on index j of dp.
All inputs are finite; a program needn't handle non-finite values.
Results may differ from the reference program's by a relative error of at most 0.019.
Values may be sent and summed in bfloat16 or wider, within the bound.
A program may use at most 128 MiB of HBM per device.

```python
import jax
import jax.numpy as jnp
from jax import lax

D = 768
HEADS = 12
HEAD_DIM = 64
FF = 3072
CIN = 1024
GROUPS = 32
L = 576
SHORT = 196
SLICES = 16


def draw_valid_mask(key, part):
    shuffled = jax.random.permutation(key, SLICES)
    lengths = jnp.where(shuffled < SLICES // 2, SHORT, L).astype(jnp.int32)
    positions = jnp.arange(L, dtype=jnp.int32)
    return (positions[None, :] < lengths[:, None]).astype(jnp.int32)


def level_of(rng, extent, shards, smallest, largest):
    def one(position, blocks):
        steps = jax.random.uniform(jax.random.fold_in(jax.random.fold_in(rng, 6), position), (blocks,), jnp.float32, smallest / len(shards), largest / len(shards))
        return jnp.repeat(jnp.exp(steps), extent[position] // blocks).reshape((-1,) + (1,) * (len(extent) - position - 1))

    loudness = one(*shards[0])
    for cut in shards[1:]:
        loudness = loudness * one(*cut)
    return loudness


def noise(key, extent, deviation, most, cuts=(), kind=jnp.bfloat16):
    array = jax.random.normal(key, extent, jnp.float32) * deviation
    if len(cuts) > 0:
        array = level_of(key, extent, cuts, -0.22, 0.18) * array
    return jnp.clip(array, min=-most, max=most).astype(kind)


def setup_inputs(seed: int = 0) -> dict:
    key_list = jax.random.split(jax.random.key(seed), 18)
    return {
        "features": noise(key_list[0], (SLICES * L, CIN), 1.0, 6.0, ((0, 8),)),
        "stem_weight": noise(key_list[1], (CIN, CIN), CIN ** -0.5, 0.1875, ((1, 4),)),
        "group_gain": jnp.clip(1.0 + 0.18 * jax.random.normal(key_list[2], (CIN,), jnp.float32), 0.1, 1.9),
        "group_bias": noise(key_list[3], (CIN,), 0.5, 3.0, ((0, 4),), jnp.float32),
        "embed_weight": noise(key_list[4], (CIN, D), CIN ** -0.5, 0.1875, ((0, 4),)),
        "first_gain": jnp.clip(1.0 + 0.18 * jax.random.normal(key_list[5], (D,), jnp.float32), 0.1, 1.9),
        "first_bias": noise(key_list[6], (D,), 0.3, 2.0, (), jnp.float32),
        "project_in": noise(key_list[7], (D, 3 * D), D ** -0.5, 0.21875, ((1, 4),)),
        "project_out": noise(key_list[8], (D, D), (max(1, 3 * D // L)) ** -0.5, 3.0, ((0, 4),)),
        "second_gain": jnp.clip(1.0 + 0.18 * jax.random.normal(key_list[9], (D,), jnp.float32), 0.1, 1.9),
        "second_bias": noise(key_list[10], (D,), 0.3, 2.0, (), jnp.float32),
        "up_weight": noise(key_list[11], (D, FF), D ** -0.5, 0.21875, ((1, 4),)),
        "up_bias": noise(key_list[12], (FF,), 0.5, 3.0, ((0, 4),), jnp.float32),
        "down_weight": noise(key_list[13], (FF, D), FF ** -0.5, 0.109375, ((0, 4),)),
        "valid_mask": draw_valid_mask(jax.random.fold_in(key_list[17], 71), 0),
        "slot_slice": jax.random.permutation(key_list[15], SLICES).astype(jnp.int32),
        "cotangent": noise(key_list[16], (SLICES * L, D), 1.0, 6.0, ((0, 32),)),
    }


@jax.custom_vjp
def low(v):
    return lax.optimization_barrier(v.astype(jnp.bfloat16)).astype(jnp.float32)

@jax.custom_vjp
def low_back(v):
    return v

def low_keep(v):
    return (low(v), None)

def low_pass(kept, grad):
    return (grad,)

def back_keep(v):
    return (v, None)

def back_low(kept, grad):
    return (low(grad),)
low.defvjp(low_keep, low_pass)
low_back.defvjp(back_keep, back_low)

def product(left, right):
    return jnp.dot(left, right, precision=lax.Precision.HIGHEST, preferred_element_type=jnp.float32)

def gelu_exact(values):
    return jax.nn.gelu(values, approximate=False)

def layer_norm(values, norm_gain, norm_bias):
    average = lax.optimization_barrier(jnp.mean(values, axis=-1, keepdims=True))
    centered = values - average
    variance = lax.optimization_barrier(jnp.mean(centered * centered, axis=-1, keepdims=True))
    return centered * lax.rsqrt(variance + 1e-06) * norm_gain + norm_bias

def standardize(matrix):
    average = lax.optimization_barrier(jnp.mean(matrix, axis=0, keepdims=True))
    centered = matrix - average
    variance = lax.optimization_barrier(jnp.mean(centered * centered, axis=0, keepdims=True))
    return centered * lax.rsqrt(variance + 1e-05)

def group_norm(stem_out, valid, norm_gain, norm_bias):
    slices, length, channels = stem_out.shape
    group_size = CIN // GROUPS
    grouped = stem_out.reshape(slices, length, channels // group_size, group_size)
    weight = valid[:, :, None, None]
    counted = lax.optimization_barrier(jnp.sum(valid, axis=1))[:, None, None, None] * group_size
    average = lax.optimization_barrier(jnp.sum(grouped * weight, axis=(1, 3), keepdims=True)) / counted
    centered = grouped - average
    variance = lax.optimization_barrier(jnp.sum(centered * centered * weight, axis=(1, 3), keepdims=True)) / counted
    normed = (centered * lax.rsqrt(variance + 1e-05)).reshape(slices, length, channels)
    return normed * norm_gain + norm_bias

def layer_apply(parameters, features, valid):
    stem_weight, group_gain, group_bias, embed_weight, first_gain, first_bias, project_in, project_out, second_gain, second_bias, up_weight, up_bias, down_weight = parameters
    slices = valid.shape[0]
    tokens = slices * L
    standard = low(standardize(stem_weight))
    stem_out = low_back(product(features, standard))
    normed_stem = group_norm(stem_out.reshape(slices, L, CIN), valid, group_gain, group_bias)
    activated = low(gelu_exact(normed_stem).reshape(tokens, CIN))
    residual_first = low_back(product(activated, embed_weight))
    normed_one = low(layer_norm(residual_first, first_gain, first_bias))
    packed = low(low_back(product(normed_one, project_in))).reshape(slices, L, HEADS, 3, HEAD_DIM)
    queries = packed[:, :, :, 0]
    key_part = packed[:, :, :, 1]
    value_part = packed[:, :, :, 2]
    raw_scores = jnp.einsum('sqhd,skhd->shqk', queries, key_part, precision=lax.Precision.HIGHEST)
    scores = low_back(raw_scores * HEAD_DIM ** (-0.5))
    scores = jnp.where(valid[:, None, None, :] > 0.5, scores, -1000000000.0)
    weights = low(jax.nn.softmax(scores, axis=-1))
    mixed_raw = jnp.einsum('shqk,skhd->sqhd', weights, value_part, precision=lax.Precision.HIGHEST)
    mixed_out = low(low_back(mixed_raw)).reshape(tokens, D)
    residual_second = residual_first + low_back(product(mixed_out, project_out))
    normed_two = low(layer_norm(residual_second, second_gain, second_bias))
    hidden_pre = low_back(product(normed_two, up_weight) + up_bias)
    hidden = low(gelu_exact(hidden_pre))
    residual_third = residual_second + low_back(product(hidden, down_weight))
    return residual_third * valid.reshape(tokens)[:, None]

def reference(features, stem_weight, group_gain, group_bias, embed_weight, first_gain, first_bias, project_in, project_out, second_gain, second_bias, up_weight, up_bias, down_weight, valid_mask, slot_slice, cotangent):
    parameters = tuple((array_in.astype(jnp.float32) for array_in in (stem_weight, group_gain, group_bias, embed_weight, first_gain, first_bias, project_in, project_out, second_gain, second_bias, up_weight, up_bias, down_weight)))
    slot_valid = jnp.take(valid_mask, slot_slice, axis=0).astype(jnp.float32)
    group_count = SLICES // 4
    feature_blocks = features.astype(jnp.float32).reshape(group_count, 4 * L, CIN)
    valid_blocks = slot_valid.reshape(group_count, 4, L)
    grad_blocks = cotangent.astype(jnp.float32).reshape(group_count, 4 * L, D)

    def scan_step(totals, block_in):
        feature_block, valid_block, grad_block = block_in
        output, pull_back = jax.vjp(lambda params_in, inputs_in: layer_apply(params_in, inputs_in, valid_block), parameters, feature_block)
        param_grads, feature_grad = pull_back(grad_block)
        totals = jax.tree.map(lambda first_in, second_in: first_in + second_in, totals, param_grads)
        return (totals, (output.astype(jnp.bfloat16), feature_grad))
    initial = jax.tree.map(jnp.zeros_like, parameters)
    totals, (outputs, feature_grads) = lax.scan(scan_step, initial, (feature_blocks, valid_blocks, grad_blocks))
    return (outputs.reshape(SLICES * L, D), feature_grads.reshape(SLICES * L, CIN), totals[0], totals[1], totals[2], totals[3], totals[4], totals[5], totals[6], totals[7], totals[8], totals[9], totals[10], totals[11], totals[12])
```

```python
import functools

import jax
import jax.numpy as jnp
from jax import lax
from jax.experimental import pallas as pl
from jax.experimental.pallas import tpu as pltpu
from jax.sharding import PartitionSpec as P

MESH = pl.DeviceIdType.MESH
F32 = jnp.float32
BF16 = jnp.bfloat16
HEAD_DIM = 64
GROUP = 32
NEAR = 8


def dot(left, right, left_dim=1, right_dim=0, precision=None):
    return lax.dot_general(
        left,
        right,
        (((left_dim,), (right_dim,)), ((), ())),
        precision=precision,
        preferred_element_type=F32,
    )


def gelu_parts(z):
    cdf = 0.5 + 0.5 * lax.erf(z * 0.7071067811865476)
    return z * cdf, cdf + z * (jnp.exp(-0.5 * z * z) * 0.3989422804014327)


class Net:
    def __init__(self, send_sems, recv_sems, local_sems):
        self.send_sems, self.recv_sems, self.local_sems = send_sems, recv_sems, local_sems
        self.count, self.local_count, self.unsent = 0, 0, []

    def send(self, src, dst, device):
        copy = pltpu.make_async_remote_copy(
            src_ref=src,
            dst_ref=dst,
            send_sem=self.send_sems.at[self.count],
            recv_sem=self.recv_sems.at[self.count],
            device_id=device,
            device_id_type=MESH,
        )
        self.count += 1
        copy.start()
        self.unsent.append(copy)
        return copy

    def sent(self, copy):
        self.unsent = [one for one in self.unsent if one is not copy]
        copy.wait_send()

    def local(self, src, dst):
        copy = pltpu.make_async_copy(src, dst, self.local_sems.at[self.local_count])
        self.local_count += 1
        copy.start()
        return copy

    def finish(self):
        for copy in self.unsent:
            copy.wait_send()


class Summed:
    def __init__(self, net, place, grad, half_in, parts_in, piece, out):
        self.net, self.place = net, place
        self.grad, self.half_in, self.parts_in, self.piece, self.out = (
            grad,
            half_in,
            parts_in,
            piece,
            out,
        )
        self.rows = grad.shape[-2]
        self.part = self.rows // 4

    def start(self):
        y = self.place.y
        self.half = self.net.send(self.grad.at[1 - y], self.half_in, self.place.y_device)

    def spread(self):
        y, zi = self.place.y, self.place.zi
        self.half.wait_recv()
        for t in range(4):
            rows = pl.ds(t * self.part, self.part)
            self.grad[y, rows, :] = (
                self.grad[y, rows, :].astype(F32) + self.half_in[rows, :].astype(F32)
            ).astype(BF16)
        self.parts = []
        for k in range(1, 4):
            to = lax.rem(zi + k, 4)
            rows = pl.ds(pl.multiple_of(to * self.part, 16), self.part)
            self.parts.append(
                self.net.send(
                    self.grad.at[y, rows], self.parts_in.at[k - 1], self.place.z_device(k)
                )
            )

    def gather(self):
        y, zi = self.place.y, self.place.zi
        rows = pl.ds(pl.multiple_of(zi * self.part, 16), self.part)
        for copy in self.parts:
            copy.wait_recv()
        total = self.grad[y, rows, :].astype(F32)
        for k in range(3):
            total = total + self.parts_in[k].astype(F32)
        self.piece[...] = total.astype(BF16)
        target = self.out.at[y, rows]
        self.own = self.net.local(self.piece, target)
        self.pieces = [
            self.net.send(self.piece, target, self.place.z_device(k)) for k in range(1, 4)
        ]

    def share(self):
        y = self.place.y
        self.own.wait()
        for copy in self.pieces:
            copy.wait_recv()
        self.last = self.net.send(self.out.at[y], self.out.at[y], self.place.y_device)

    def done(self):
        self.last.wait_recv()


class Place:
    def __init__(self):
        self.d = lax.axis_index("dp")
        self.m = lax.axis_index("mp")
        self.x = lax.div(self.m, 2)
        self.c = lax.rem(self.m, 2)
        self.y = lax.rem(self.d, 2)
        self.zi = lax.div(lax.rem(self.d, NEAR), 2)
        self.base = self.d - lax.rem(self.d, NEAR)
        self.sib_m = self.m + 1 - 2 * self.c
        self.far_m = lax.rem(self.m + 2, 4)
        self.far_sib_m = lax.rem(self.sib_m + 2, 4)
        self.sib = (self.d, self.sib_m)
        self.far = (self.d, self.far_m)
        self.y_device = (self.d + 1 - 2 * self.y, self.m)

    def z_device(self, k):
        return (self.base + 2 * lax.rem(self.zi + k, 4) + self.y, self.m)


def kernel(in_names, out_names, scratch_names, *refs):
    names = in_names + out_names + scratch_names
    r = dict(zip(names, refs))
    run(**r)


def run(
    features, stem_weight, group_gain, group_bias, embed_weight, first_gain, first_bias,
    project_in, project_out, second_gain, second_bias, up_weight, up_bias, down_weight,
    valid_mask, slot_slice, cotangent,
    block_out, features_grad, o_stem, o_embed, o_pin, o_pout, o_up, o_down, o_small,
    feat, stem, std, wstat, embed, pin, pout, up, down, gvec, xhs, dgs, act, gst,
    sbuf, rbuf, res1, xh1, rs1, n1, q, k, v, probs, heads, mixed, res2, xh2, rs2,
    n2, hid, branch, preg, own, csend, crecv, xsend, xrecv, mb, pg, sg, gtmp,
    g_up, g_down, g_pin, g_pout, g_embed, g_stem,
    x_pin, x_pout, x_embed, x_stem,
    y_up, y_down, y_pin, y_pout, y_embed, y_stem,
    z_up, z_down, z_pin, z_pout, z_embed, z_stem,
    p_up, p_down, p_pin, p_pout, p_embed, p_stem,
    sm, smr, smz, send_sems, recv_sems, local_sems,
):
    place = Place()
    net = Net(send_sems, recv_sems, local_sems)
    x, c = place.x, place.c
    R = cotangent.shape[0]
    L = feat.shape[0]
    D = up.shape[0]
    own_rows = pl.multiple_of(c * R, 16)
    sib_rows = pl.multiple_of((1 - c) * R, 16)

    def block(m):
        return pl.ds(pl.multiple_of(m * R, 16), R)

    barrier = pltpu.get_barrier_semaphore()
    peers = [place.sib, place.far, place.y_device] + [place.z_device(i) for i in (1, 2, 3)]
    for peer in peers:
        pl.semaphore_signal(barrier, inc=1, device_id=peer, device_id_type=MESH)
    l_stem = net.local(stem_weight, stem.at[0])
    l_feat = net.local(features.at[pl.ds(pl.multiple_of(x * L, 16), L)], feat)
    l_embed = net.local(embed_weight, embed.at[0])
    l_cot = net.local(cotangent, branch.at[block(place.m)])
    l_pin = net.local(project_in, pin.at[0])
    l_pout = net.local(project_out, pout.at[0])
    l_up = net.local(up_weight, up)
    l_down = net.local(down_weight, down)
    gvec[0, 0:1, :] = group_gain[...].reshape(1, -1)
    gvec[0, 1:2, :] = group_bias[...].reshape(1, -1)
    pl.semaphore_wait(barrier, len(peers))

    c_gvec = net.send(gvec.at[0], gvec.at[1], place.far)
    c_stem = net.send(stem_weight, stem.at[1], place.far)

    slices = valid_mask.shape[0]
    lengths = jnp.sum(valid_mask[...].astype(F32), axis=1, keepdims=True)
    mine = lax.broadcasted_iota(jnp.int32, (slices, 1), 0) == slot_slice[x]
    length = jnp.sum(jnp.where(mine, lengths, 0.0), axis=0, keepdims=True)

    def valid_rows(start, count):
        at = (lax.broadcasted_iota(jnp.int32, (count, 1), 0) + start).astype(F32)
        return jnp.where(at < length, 1.0, 0.0)

    key_valid = jnp.where(
        lax.broadcasted_iota(jnp.int32, (1, L), 1).astype(F32) < length, 1.0, 0.0
    )
    score_scale = HEAD_DIM ** (-0.5)
    key_scale = key_valid * score_scale
    key_shift = (key_valid - 1.0) * 1e9

    channels = stem.shape[2]
    same = (
        lax.div(lax.broadcasted_iota(jnp.int32, (channels, channels), 0), GROUP)
        == lax.div(lax.broadcasted_iota(jnp.int32, (channels, channels), 1), GROUP)
    )
    same = jnp.where(same, 1.0, 0.0)

    def group_sum(values):
        wide = jnp.broadcast_to(values, (8, channels))
        return dot(wide, same, precision=lax.Precision.HIGHEST)[0:1]

    def standardize(j):
        w = stem[j].astype(F32)
        average = jnp.sum(w, axis=0, keepdims=True) * (1.0 / w.shape[0])
        w = w - average
        scale = lax.rsqrt(jnp.sum(w * w, axis=0, keepdims=True) * (1.0 / w.shape[0]) + 1e-5)
        std[j] = (w * scale).astype(BF16)
        wstat[j, 0:1, :] = average
        wstat[j, 1:2, :] = scale

    tile_rows = [(t * R, R) for t in range(L // R)]

    def stem_forward(j):
        count = 1.0 / (length * GROUP)
        total = jnp.zeros((1, channels), F32)
        for at, size in tile_rows:
            s = dot(feat[at : at + size, :], std[j])
            xhs[j, at : at + size, :] = s
            total = total + jnp.sum(s * valid_rows(at, size), axis=0, keepdims=True)
        average = group_sum(total) * count
        total = jnp.zeros((1, channels), F32)
        for at, size in tile_rows:
            s = xhs[j, at : at + size, :] - average
            total = total + jnp.sum(s * s * valid_rows(at, size), axis=0, keepdims=True)
        scale = lax.rsqrt(group_sum(total) * count + 1e-5)
        gst[j, 0:1, :] = scale
        for at, size in tile_rows:
            xh = (xhs[j, at : at + size, :] - average) * scale
            xhs[j, at : at + size, :] = xh
            value, slope = gelu_parts(xh * gvec[j, 0:1, :] + gvec[j, 1:2, :])
            act[j, at : at + size, :] = value.astype(BF16)
            dgs[j, at : at + size, :] = slope

    l_stem.wait()
    standardize(0)
    l_feat.wait()
    stem_forward(0)
    c_embed = net.send(embed_weight, embed.at[1], place.far)
    c_gvec.wait_recv()
    c_stem.wait_recv()
    standardize(1)
    c_pin = net.send(project_in, pin.at[1], place.far)
    stem_forward(1)
    l_embed.wait()
    c_embed.wait_recv()
    c_pout = net.send(project_out, pout.at[1], place.far)

    def core_sum(product):
        width = pl.ds(0, D)
        sbuf[:, width] = product(sib_rows)
        copy = net.send(sbuf.at[:, width], rbuf.at[:, width], place.sib)
        mine = product(own_rows)
        copy.wait_recv()
        net.sent(copy)
        return mine

    def embed_product(start):
        rows = pl.ds(start, R)
        return dot(act[0, rows, :], embed[0]) + dot(act[1, rows, :], embed[1])

    res1[...] = core_sum(embed_product)

    step = R // 3

    def layer_norm(res, other, add, gain, bias, xh_ref, scale_ref, out_ref, out_start):
        gain, bias = gain[...].reshape(1, -1), bias[...].reshape(1, -1)
        for t in range(3):
            rows = slice(t * step, (t + 1) * step)
            value = res[rows, :] + other[rows, 0:D]
            if add is not None:
                value = value + add[rows, :]
            res[rows, :] = value
            average = jnp.sum(value, axis=1, keepdims=True) * (1.0 / D)
            value = value - average
            scale = lax.rsqrt(jnp.sum(value * value, axis=1, keepdims=True) * (1.0 / D) + 1e-6)
            xh = value * scale
            xh_ref[rows, :] = xh
            scale_ref[rows, :] = scale
            out_ref[pl.ds(out_start + t * step, step), :] = (xh * gain + bias).astype(BF16)

    layer_norm(res1, rbuf, None, first_gain, first_bias, xh1, rs1, n1, own_rows)
    c_n1 = net.send(n1.at[pl.ds(own_rows, R)], n1.at[pl.ds(own_rows, R)], place.sib)
    l_pin.wait()
    c_n1.wait_recv()

    per_shard = pin.shape[2] // (3 * HEAD_DIM)

    def attend(j):
        for at, size in tile_rows:
            packed = dot(n1[at : at + size, :], pin[j]).astype(BF16)
            for h in range(per_shard):
                for i, ref in enumerate((q, k, v)):
                    lane = (3 * h + i) * HEAD_DIM
                    ref[per_shard * j + h, at : at + size, :] = packed[:, lane : lane + HEAD_DIM]

        def head(i, carry):
            h = per_shard * j + i
            for at, size in tile_rows:
                s = dot(q[h, at : at + size, :], k[h], 1, 1) * key_scale + key_shift
                s = jnp.exp(s - jnp.max(s, axis=1, keepdims=True))
                p = (s * (1.0 / jnp.sum(s, axis=1, keepdims=True))).astype(BF16)
                probs[h, at : at + size, :] = p
                heads[h, at : at + size, :] = dot(p, v[h]).astype(BF16)
            return carry

        lax.fori_loop(0, per_shard, head, 0)

    attend(0)
    c_pin.wait_recv()
    c_cot = [
        net.send(cotangent, branch.at[block(place.m)], device) for device in (place.far, place.sib)
    ]
    attend(1)

    def side_by_side(pieces, store):
        at = 0
        while at < len(pieces):
            pair = pieces[at : at + 2]
            value = pair[0] if len(pair) == 1 else jnp.concatenate(pair, axis=1)
            store(slice(at * HEAD_DIM, at * HEAD_DIM + value.shape[1]), value)
            at += 2

    def store_mixed(lanes, value):
        mixed[:, lanes] = value

    side_by_side([heads[h] for h in range(2 * per_shard)], store_mixed)
    l_pout.wait()
    c_pout.wait_recv()
    out_width = pout.shape[1]

    def out_product(start):
        rows = pl.ds(start, R)
        whole = jnp.concatenate([pout[0], pout[1]], axis=0)
        return dot(mixed[rows, :], whole)

    res2[...] = core_sum(out_product)
    layer_norm(
        res2, rbuf, res1, second_gain, second_bias, xh2, rs2, n2, pl.multiple_of(place.m * R, 16)
    )
    mine = block(place.m)
    c_n2 = [net.send(n2.at[mine], n2.at[mine], device) for device in (place.far, place.sib)]

    l_cot.wait()
    l_up.wait()
    l_down.wait()
    bias_sum = []

    def feed(m):
        rows = block(m)
        pre = dot(n2[rows, :], up[...]) + up_bias[...].reshape(1, -1)
        value, slope = gelu_parts(pre)
        hid[rows, :] = value.astype(BF16)
        grad = (dot(branch[rows, :], down[...], 1, 1) * slope).astype(BF16)
        preg[rows, :] = grad
        bias_sum.append(jnp.sum(grad.astype(F32), axis=0, keepdims=True))

    def back_part(m):
        return dot(preg[block(m), :], up[...], 1, 1)

    def out_part(m):
        return dot(hid[block(m), :], down[...])

    def mask_branch(m, own_slot):
        rows = block(m)
        start = lax.rem(m, 2) * R
        branch[rows, :] = (
            branch[rows, :].astype(F32) * valid_of(own_slot, start)
        ).astype(BF16)

    mine_far = lax.broadcasted_iota(jnp.int32, (slices, 1), 0) == slot_slice[1 - x]
    far_length = jnp.sum(jnp.where(mine_far, lengths, 0.0), axis=0, keepdims=True)

    def valid_of(own_slot, start):
        at = (lax.broadcasted_iota(jnp.int32, (R, 1), 0) + start).astype(F32)
        return jnp.where(at < (length if own_slot else far_length), 1.0, 0.0)

    c_cot[0].wait_recv()
    f_rows = block(place.far_m)
    c_cot_fwd = net.send(branch.at[f_rows], branch.at[f_rows], place.sib)
    mask_done = []

    mask_branch(place.m, True)
    feed(place.m)
    own[1] = back_part(place.m)
    c_cot[1].wait_recv()
    c_n2[1].wait_recv()
    mask_branch(place.sib_m, True)
    feed(place.sib_m)
    csend[1, 0] = back_part(place.sib_m).astype(BF16)
    c_core = {}
    c_core[1, 0] = net.send(csend.at[1, 0], crecv.at[1, 0], place.sib)
    c_n2[0].wait_recv()
    c_n2_fwd = net.send(n2.at[f_rows], n2.at[f_rows], place.sib)
    csend[0, 0] = out_part(place.sib_m).astype(BF16)
    c_core[0, 0] = net.send(csend.at[0, 0], crecv.at[0, 0], place.sib)
    own[0] = out_part(place.m)
    c_cot_fwd.wait_recv()
    c_n2_fwd.wait_recv()
    mask_branch(place.far_sib_m, False)
    feed(place.far_sib_m)
    csend[1, 1] = back_part(place.far_sib_m).astype(BF16)
    c_core[1, 1] = net.send(csend.at[1, 1], crecv.at[1, 1], place.sib)
    net.sent(c_cot_fwd)
    mask_branch(place.far_m, False)
    feed(place.far_m)
    sbuf[:, 0:D] = back_part(place.far_m)
    c_core[1, 1].wait_recv()
    xsend[1] = (sbuf[:, 0:D] + crecv[1, 1].astype(F32)).astype(BF16)
    c_far = {}
    c_far[1] = net.send(xsend.at[1], xrecv.at[1], place.far)
    csend[0, 1] = out_part(place.far_sib_m).astype(BF16)
    c_core[0, 1] = net.send(csend.at[0, 1], crecv.at[0, 1], place.sib)
    sbuf[:, 0:D] = out_part(place.far_m)
    c_core[0, 1].wait_recv()
    xsend[0] = (sbuf[:, 0:D] + crecv[0, 1].astype(F32)).astype(BF16)
    c_far[0] = net.send(xsend.at[0], xrecv.at[0], place.far)

    summed = {
        "down": Summed(net, place, g_down, y_down, z_down, p_down, o_down),
        "up": Summed(net, place, g_up, y_up, z_up, p_up, o_up),
        "pout": Summed(net, place, g_pout.at[0], y_pout, z_pout, p_pout, o_pout),
        "pin": Summed(net, place, g_pin.at[0], y_pin, z_pin, p_pin, o_pin),
        "embed": Summed(net, place, g_embed.at[0], y_embed, z_embed, p_embed, o_embed),
        "stem": Summed(net, place, g_stem.at[0], y_stem, z_stem, p_stem, o_stem),
    }

    half = D // 2
    for i in range(2):
        g_down[i] = dot(hid[:, i * half : (i + 1) * half], branch[...], 0, 0).astype(BF16)
    summed["down"].start()
    for i in range(2):
        g_up[i] = dot(n2[:, i * half : (i + 1) * half], preg[...], 0, 0).astype(BF16)
    summed["up"].start()
    sm[...] = jnp.zeros_like(sm)
    sm[4:5, :] = bias_sum[0] + bias_sum[1] + bias_sum[2] + bias_sum[3]

    def norm_back(grad_of, gain, xh_ref, scale_ref, keep, out_ref, out_start, row):
        gain = gain[...].reshape(1, -1)
        gain_sum = jnp.zeros((1, D), F32)
        bias_total = jnp.zeros((1, D), F32)
        for t in range(3):
            rows = slice(t * step, (t + 1) * step)
            dy, through = grad_of(rows)
            xh = xh_ref[rows, :]
            gain_sum = gain_sum + jnp.sum(dy * xh, axis=0, keepdims=True)
            bias_total = bias_total + jnp.sum(dy, axis=0, keepdims=True)
            dy = dy * gain
            mean_one = jnp.sum(dy, axis=1, keepdims=True) * (1.0 / D)
            mean_two = jnp.sum(dy * xh, axis=1, keepdims=True) * (1.0 / D)
            dx = through + scale_ref[rows, :] * (dy - mean_one - xh * mean_two)
            if keep is not None:
                keep[rows, :] = dx
            out_ref[pl.ds(out_start + t * step, step), :] = dx.astype(BF16)
        sm[row : row + 1, :] = gain_sum
        sm[row + 1 : row + 2, :] = bias_total

    sg2, eb = res1, mb
    c_core[1, 0].wait_recv()
    c_far[1].wait_recv()

    def second_grad_of(rows):
        dy = own[1, rows, :] + crecv[1, 0, rows, :].astype(F32) + xrecv[1, rows, :].astype(F32)
        at = pl.ds(pl.multiple_of(place.m * R, 16) + rows.start, step)
        return dy, branch[at, :].astype(F32)

    norm_back(second_grad_of, second_gain, xh2, rs2, sg2, mb, own_rows, 2)
    c_mb = net.send(mb.at[pl.ds(own_rows, R)], mb.at[pl.ds(own_rows, R)], place.sib)

    c_core[0, 0].wait_recv()
    c_far[0].wait_recv()
    net.sent(c_core[0, 0])
    for t in range(3):
        rows = slice(t * step, (t + 1) * step)
        value = (
            res2[rows, :]
            + own[0, rows, :]
            + crecv[0, 0, rows, :].astype(F32)
            + xrecv[0, rows, :].astype(F32)
        )
        csend[0, 0, rows, :] = (value * valid_rows(own_rows + t * step, step)).astype(BF16)
    l_bout = net.local(csend.at[0, 0], block_out)

    c_mb.wait_recv()
    grad = dot(mixed[...], mb[...], 0, 0)
    shard = pout.shape[1]
    wide = g_pout.shape[3]
    for j in (1, 0):
        for i in range(2):
            g_pout[j, i] = grad[j * shard : (j + 1) * shard, i * wide : (i + 1) * wide].astype(BF16)
    cx = {}
    cx["pout"] = net.send(g_pout.at[1], x_pout, place.far)
    whole_out = jnp.concatenate([pout[0], pout[1]], axis=0)
    for at, size in tile_rows:
        value = dot(mb[at : at + size, :], whole_out, 1, 1).astype(BF16)
        for h in range(2 * per_shard):
            heads[h, at : at + size, :] = value[:, h * HEAD_DIM : (h + 1) * HEAD_DIM]

    def head_back(h, carry):
        p = probs[h]
        dp = dot(heads[h], v[h], 1, 1)
        v[h] = dot(p, heads[h], 0, 0).astype(BF16)
        p = p.astype(F32)
        ds = (p * (dp - jnp.sum(p * dp, axis=1, keepdims=True))).astype(BF16)
        dq = (dot(ds, k[h]) * score_scale).astype(BF16)
        k[h] = (dot(ds, q[h], 0, 0) * score_scale).astype(BF16)
        q[h] = dq
        return carry

    lax.fori_loop(0, 2 * per_shard, head_back, 0)

    for j in (1, 0):

        def store_pg(lanes, value):
            pg[j, :, lanes] = value

        pieces = [ref[per_shard * j + h] for h in range(per_shard) for ref in (q, k, v)]
        side_by_side(pieces, store_pg)
    for j in (1, 0):
        for i in range(2):
            g_pin[j, i] = dot(n1[:, i * half : (i + 1) * half], pg[j], 0, 0).astype(BF16)
        if j == 1:
            cx["pin"] = net.send(g_pin.at[1], x_pin, place.far)

    def first_product(start):
        rows = pl.ds(start, R)
        return dot(pg[0, rows, :], pin[0], 1, 1) + dot(pg[1, rows, :], pin[1], 1, 1)

    own[0] = core_sum(first_product)

    def first_grad_of(rows):
        return own[0, rows, :] + rbuf[rows, 0:D], sg2[rows, :]

    net.sent(c_mb)
    norm_back(first_grad_of, first_gain, xh1, rs1, None, eb, own_rows, 0)
    c_eb = net.send(eb.at[pl.ds(own_rows, R)], eb.at[pl.ds(own_rows, R)], place.sib)

    def far_sum(name, grad, arrived):
        cx[name].wait_recv()
        for i in range(2):
            grad[0, i] = (grad[0, i].astype(F32) + arrived[i].astype(F32)).astype(BF16)
        summed[name].start()

    summed["down"].spread()
    far_sum("pout", g_pout, x_pout)
    c_eb.wait_recv()

    embed_half = embed.shape[1] // 2
    for j in (1, 0):
        grad = dot(act[j], eb[...], 0, 0)
        for i in range(2):
            g_embed[j, i] = grad[i * embed_half : (i + 1) * embed_half, :].astype(BF16)
        if j == 1:
            cx["embed"] = net.send(g_embed.at[1], x_embed, place.far)
    cin = feat.shape[1]
    for j in (1, 0):
        gain_sum = jnp.zeros((1, channels), F32)
        bias_total = jnp.zeros((1, channels), F32)
        for at, size in tile_rows:
            dz = dot(eb[at : at + size, :], embed[j], 1, 1) * dgs[j, at : at + size, :]
            dgs[j, at : at + size, :] = dz
            gain_sum = gain_sum + jnp.sum(dz * xhs[j, at : at + size, :], axis=0, keepdims=True)
            bias_total = bias_total + jnp.sum(dz, axis=0, keepdims=True)
        sm[5 + j : 6 + j, 0:channels] = gain_sum
        sm[5 + j : 6 + j, channels : 2 * channels] = bias_total
        gain = gvec[j, 0:1, :]
        count = 1.0 / (length * GROUP)
        mean_one = group_sum(bias_total * gain) * count
        mean_two = group_sum(gain_sum * gain) * count
        for at, size in tile_rows:
            part = dgs[j, at : at + size, :] * gain - valid_rows(at, size) * (
                mean_one + xhs[j, at : at + size, :] * mean_two
            )
            sg[j, at : at + size, :] = (part * gst[j, 0:1, :]).astype(BF16)
        average, scale = wstat[j, 0:1, :], wstat[j, 1:2, :]
        sum_one = jnp.zeros((1, channels), F32)
        sum_two = jnp.zeros((1, channels), F32)
        quarter = cin // 4
        for t in range(4):
            rows = slice(t * quarter, (t + 1) * quarter)
            grad = dot(feat[:, rows], sg[j], 0, 0)
            gtmp[rows, :] = grad
            xh = (stem[j, rows, :].astype(F32) - average) * scale
            sum_one = sum_one + jnp.sum(grad, axis=0, keepdims=True)
            sum_two = sum_two + jnp.sum(grad * xh, axis=0, keepdims=True)
        sum_one = sum_one * (1.0 / cin)
        sum_two = sum_two * (1.0 / cin)
        for t in range(4):
            rows = slice(t * quarter, (t + 1) * quarter)
            xh = (stem[j, rows, :].astype(F32) - average) * scale
            value = (gtmp[rows, :] - sum_one - xh * sum_two) * scale
            g_stem[j, t // 2, (t % 2) * quarter : (t % 2 + 1) * quarter, :] = value.astype(BF16)
        if j == 1:
            cx["stem"] = net.send(g_stem.at[1], x_stem, place.far)

    c_sm = net.send(sm, smr.at[0], place.sib)
    summed["up"].spread()
    summed["down"].gather()
    far_sum("pin", g_pin, x_pin)
    c_sm.wait_recv()
    net.sent(c_sm)
    sm[0:4, :] = sm[0:4, :] + smr[0, 0:4, :]
    c_sm = net.send(sm, smr.at[1], place.far)

    def feature_product(start):
        rows = pl.ds(start, R)
        return dot(sg[0, rows, :], std[0], 1, 1) + dot(sg[1, rows, :], std[1], 1, 1)

    sbuf[...] = feature_product(sib_rows)
    c_feat = net.send(sbuf, rbuf, place.sib)
    mine_feat = feature_product(own_rows)
    c_feat.wait_recv()
    net.sent(c_feat)
    sbuf[...] = mine_feat + rbuf[...]
    l_fgrad = net.local(sbuf, features_grad)

    far_sum("embed", g_embed, x_embed)
    c_sm.wait_recv()
    net.sent(c_sm)
    sm[0:4, :] = sm[0:4, :] + smr[1, 0:4, :]
    sm[5:6, :] = sm[5:6, :] + smr[1, 6:7, :]
    c_sm = net.send(sm, smr.at[2], place.y_device)
    summed["pout"].spread()
    summed["up"].gather()
    far_sum("stem", g_stem, x_stem)
    summed["down"].share()
    c_sm.wait_recv()
    net.sent(c_sm)
    smz[place.zi] = sm[...] + smr[2]
    c_smz = [
        net.send(smz.at[place.zi], smz.at[place.zi], place.z_device(i)) for i in (1, 2, 3)
    ]
    summed["pout"].gather()
    summed["pin"].spread()
    summed["up"].share()
    summed["embed"].spread()
    summed["pin"].gather()
    summed["pout"].share()
    summed["stem"].spread()
    for copy in c_smz:
        copy.wait_recv()
    o_small[...] = smz[0] + smz[1] + smz[2] + smz[3]
    summed["embed"].gather()
    summed["pin"].share()
    summed["stem"].gather()
    summed["embed"].share()
    summed["stem"].share()
    l_bout.wait()
    l_fgrad.wait()
    for one in summed.values():
        one.done()
    net.finish()


def body(
    features, stem_weight, group_gain, group_bias, embed_weight, first_gain, first_bias,
    project_in, project_out, second_gain, second_bias, up_weight, up_bias, down_weight,
    valid_mask, slot_slice, cotangent, *, dp,
):
    slots = slot_slice.shape[0]
    L = features.shape[0] // slots
    R = cotangent.shape[0]
    cin, channels = stem_weight.shape
    D = cotangent.shape[1]
    wide_in = project_in.shape[1]
    out_rows = project_out.shape[0]
    hidden = up_weight.shape[1]
    heads = 2 * wide_in // (3 * HEAD_DIM)
    hbm = pl.BlockSpec(memory_space=pl.ANY)
    vmem = pl.BlockSpec(memory_space=pltpu.VMEM)
    smem = pl.BlockSpec(memory_space=pltpu.SMEM)
    in_specs = dict(
        features=hbm, stem_weight=hbm, group_gain=vmem, group_bias=vmem, embed_weight=hbm,
        first_gain=vmem, first_bias=vmem, project_in=hbm, project_out=hbm, second_gain=vmem,
        second_bias=vmem, up_weight=hbm, up_bias=vmem, down_weight=hbm, valid_mask=vmem,
        slot_slice=smem, cotangent=hbm,
    )
    grads = dict(
        up=(D // 2, hidden),
        down=(hidden // 2, D),
        pin=(D // 2, wide_in),
        pout=(out_rows, D // 2),
        embed=(channels // 2, D),
        stem=(cin // 2, channels),
    )
    outs = dict(block_out=((R, D), BF16, hbm), features_grad=((R, cin), F32, hbm))
    for name in ("stem", "embed", "pin", "pout", "up", "down"):
        outs["o_" + name] = ((2,) + grads[name], BF16, hbm)
    outs["o_small"] = ((8, D), F32, vmem)
    scratch = dict(
        feat=((L, cin), BF16), stem=((2, cin, channels), BF16), std=((2, cin, channels), BF16),
        wstat=((2, 8, channels), F32), embed=((2, channels, D), BF16), pin=((2, D, wide_in), BF16),
        pout=((2, out_rows, D), BF16), up=((D, hidden), BF16), down=((hidden, D), BF16),
        gvec=((2, 8, channels), F32), xhs=((2, L, channels), F32), dgs=((2, L, channels), F32),
        act=((2, L, channels), BF16), gst=((2, 8, channels), F32),
        sbuf=((R, cin), F32), rbuf=((R, cin), F32), res1=((R, D), F32), xh1=((R, D), F32),
        rs1=((R, 1), F32), n1=((L, D), BF16), q=((heads, L, HEAD_DIM), BF16),
        k=((heads, L, HEAD_DIM), BF16), v=((heads, L, HEAD_DIM), BF16), probs=((heads, L, L), BF16),
        heads=((heads, L, HEAD_DIM), BF16), mixed=((L, heads * HEAD_DIM), BF16),
        res2=((R, D), F32), xh2=((R, D), F32), rs2=((R, 1), F32), n2=((4 * R, D), BF16),
        hid=((4 * R, hidden), BF16), branch=((4 * R, D), BF16), preg=((4 * R, hidden), BF16),
        own=((2, R, D), F32), csend=((2, 2, R, D), BF16),
        crecv=((2, 2, R, D), BF16), xsend=((2, R, D), BF16), xrecv=((2, R, D), BF16),
        mb=((L, D), BF16), pg=((2, L, wide_in), BF16),
        sg=((2, L, channels), BF16), gtmp=((cin, channels), F32),
    )
    for name in ("up", "down"):
        scratch["g_" + name] = ((2,) + grads[name], BF16)
    for name in ("pin", "pout", "embed", "stem"):
        scratch["g_" + name] = ((2, 2) + grads[name], BF16)
    for name in ("pin", "pout", "embed", "stem"):
        scratch["x_" + name] = ((2,) + grads[name], BF16)
    order = ("up", "down", "pin", "pout", "embed", "stem")
    for name in order:
        scratch["y_" + name] = (grads[name], BF16)
    for name in order:
        scratch["z_" + name] = ((3, grads[name][0] // 4, grads[name][1]), BF16)
    for name in order:
        scratch["p_" + name] = ((grads[name][0] // 4, grads[name][1]), BF16)
    scratch.update(sm=((8, D), F32), smr=((3, 8, D), F32), smz=((4, 8, D), F32))
    copies = 96
    shapes = [pltpu.VMEM(*one) for one in scratch.values()]
    shapes += [pltpu.SemaphoreType.DMA((copies,)) for _ in range(2)]
    shapes += [pltpu.SemaphoreType.DMA((24,))]
    names = tuple(scratch) + ("send_sems", "recv_sems", "local_sems")
    results = pl.pallas_call(
        functools.partial(kernel, tuple(in_specs), tuple(outs), names),
        out_shape=[jax.ShapeDtypeStruct(shape, kind) for shape, kind, _ in outs.values()],
        in_specs=list(in_specs.values()),
        out_specs=[spec for _, _, spec in outs.values()],
        scratch_shapes=shapes,
        compiler_params=pltpu.CompilerParams(
            collective_id=0, has_side_effects=True, vmem_limit_bytes=62 * 2**20
        ),
        name="layer",
    )(
        features, stem_weight, group_gain, group_bias, embed_weight, first_gain, first_bias,
        project_in, project_out, second_gain, second_bias, up_weight, up_bias, down_weight,
        valid_mask, slot_slice, cotangent,
    )
    out = dict(zip(outs, results))

    wide = {name: out["o_" + name].astype(F32) for name in order}
    small = out["o_small"]
    bit = NEAR
    while bit < dp:
        pairs = [(i, i ^ bit) for i in range(dp)]
        wide, small = jax.tree.map(
            lambda part: part + lax.ppermute(part, "dp", pairs), (wide, small)
        )
        bit *= 2

    def rows_of(name):
        return wide[name].reshape(-1, wide[name].shape[-1])

    project_out_grad = jnp.moveaxis(wide["pout"], 0, 1).reshape(out_rows, D)
    return (
        out["block_out"],
        out["features_grad"],
        rows_of("stem"),
        small[5, 0:channels],
        small[5, channels : 2 * channels],
        rows_of("embed"),
        small[0],
        small[1],
        rows_of("pin"),
        project_out_grad,
        small[2],
        small[3],
        rows_of("up"),
        small[4],
        rows_of("down"),
    )


def solution(mesh):
    return jax.shard_map(
        functools.partial(body, dp=mesh.shape["dp"]),
        mesh=mesh,
        in_specs=(
            P("dp", None), P(None, "mp"), P("mp"), P("mp"), P("mp", None), P(), P(),
            P(None, "mp"), P("mp", None), P(), P(), P(None, "mp"), P("mp"), P("mp", None),
            P(), P("dp"), P(("dp", "mp"), None),
        ),
        out_specs=(
            P(("dp", "mp"), None), P(("dp", "mp"), None), P(None, "mp"), P("mp"), P("mp"),
            P("mp", None), P(), P(), P(None, "mp"), P("mp", None), P(), P(), P(None, "mp"),
            P("mp"), P("mp", None),
        ),
        check_vma=False,
    )
```

```python
import functools

import jax
import jax.numpy as jnp
from jax import lax
from jax.experimental import pallas as pl
from jax.experimental.pallas import tpu as pltpu
from jax.sharding import PartitionSpec as P

MESH = pl.DeviceIdType.MESH
F32 = jnp.float32
BF16 = jnp.bfloat16
HEAD_DIM = 64
GROUP = 32
NEAR = 8


def dot(left, right, left_dim=1, right_dim=0, precision=None):
    return lax.dot_general(
        left,
        right,
        (((left_dim,), (right_dim,)), ((), ())),
        precision=precision,
        preferred_element_type=F32,
    )


def gelu_parts(z):
    cdf = 0.5 + 0.5 * lax.erf(z * 0.7071067811865476)
    return z * cdf, cdf + z * (jnp.exp(-0.5 * z * z) * 0.3989422804014327)


class Net:
    def __init__(self, send_sems, recv_sems, local_sems):
        self.send_sems, self.recv_sems, self.local_sems = send_sems, recv_sems, local_sems
        self.count, self.local_count, self.unsent = 0, 0, []

    def send(self, src, dst, device):
        copy = pltpu.make_async_remote_copy(
            src_ref=src,
            dst_ref=dst,
            send_sem=self.send_sems.at[self.count],
            recv_sem=self.recv_sems.at[self.count],
            device_id=device,
            device_id_type=MESH,
        )
        self.count += 1
        copy.start()
        self.unsent.append(copy)
        return copy

    def sent(self, copy):
        self.unsent = [one for one in self.unsent if one is not copy]
        copy.wait_send()

    def local(self, src, dst):
        copy = pltpu.make_async_copy(src, dst, self.local_sems.at[self.local_count])
        self.local_count += 1
        copy.start()
        return copy

    def finish(self):
        for copy in self.unsent:
            copy.wait_send()


class Summed:
    def __init__(self, net, place, order, grad, arrive, piece, out, far=None, far_in=None):
        self.net, self.place, self.order = net, place, order
        self.grad, self.arrive, self.piece, self.out = grad, arrive, piece, out
        self.far, self.far_in = far, far_in
        self.at, self.size, self.slot = 0, grad.shape[0], 0
        self.level, self.back = 0, False

    def send_far(self):
        self.copy = self.net.send(self.far, self.far_in, self.place.far)

    def add(self, at, source, count):
        for t in range(count):
            self.grad[at + t] = (
                self.grad[at + t].astype(F32) + source(t).astype(F32)
            ).astype(BF16)

    def start(self):
        bit, partner = self.place.partner(self.order[self.level])
        half = self.size // 2
        give = pl.ds(self.at + (1 - bit) * half, half)
        self.at = self.at + bit * half
        self.copy = self.net.send(
            self.grad.at[give], self.arrive.at[pl.ds(self.slot, half)], partner
        )

    def share(self):
        held = pl.ds(self.at, self.size)
        bit, partner = self.place.partner(self.order[self.level])
        self.copy = self.net.send(self.out.at[held], self.out.at[held], partner)
        self.at = self.at - bit * self.size

    def step(self):
        self.copy.wait_recv()
        if self.far is not None:
            self.far = None
            self.add(0, lambda t: self.far_in[t], self.size)
            self.start()
        elif not self.back:
            half = self.size // 2
            slot = self.slot
            self.size, self.slot = half, slot + half
            self.level += 1
            if self.level < len(self.order):
                self.add(self.at, lambda t: self.arrive[slot + t], half)
                self.start()
            else:
                self.back = True
                self.level -= 1
                self.piece[0] = (
                    self.grad[self.at].astype(F32) + self.arrive[slot].astype(F32)
                ).astype(BF16)
                held = pl.ds(self.at, 1)
                self.own = self.net.local(self.piece, self.out.at[held])
                bit, partner = self.place.partner(self.order[self.level])
                self.copy = self.net.send(self.piece, self.out.at[held], partner)
                self.at = self.at - bit
        else:
            if self.size == 1:
                self.own.wait()
            self.size *= 2
            self.level -= 1
            if self.level >= 0:
                self.share()
                return
            self.copy = None

    def step_all(self):
        while self.copy is not None:
            self.step()


class Place:
    def __init__(self):
        self.d = lax.axis_index("dp")
        self.m = lax.axis_index("mp")
        self.x = lax.div(self.m, 2)
        self.c = lax.rem(self.m, 2)
        self.y = lax.rem(self.d, 2)
        self.zi = lax.div(lax.rem(self.d, NEAR), 2)
        self.bits = {"y": (self.y, 1), "a": (lax.rem(self.zi, 2), 2), "b": (lax.div(self.zi, 2), 4)}
        self.sib_m = self.m + 1 - 2 * self.c
        self.far_m = lax.rem(self.m + 2, 4)
        self.far_sib_m = lax.rem(self.sib_m + 2, 4)
        self.sib = (self.d, self.sib_m)
        self.far = (self.d, self.far_m)
        self.y_device = (self.d + 1 - 2 * self.y, self.m)

    def partner(self, name):
        bit, stride = self.bits[name]
        return bit, (self.d + stride - 2 * stride * bit, self.m)


GRADS = ("up", "down", "pout", "pin0", "pin1", "pin2", "embed", "stem")
BY_SLOT = GRADS[2:]
KINDS = dict(g="grad", f="far", i="far_in", r="arrive", p="piece", o="out")
ORDER = (
    "norm2", "mixed_back", "heads_far", "down", "up", "heads_own", "norm1_send", "down", "up",
    "norm1", "pout", "stem_far", "stem_own", "down", "up", "features_send", "pin0", "pout",
    "features_sum", "small", "result", "down", "up", "pout", "pin0", "embed", "small", "down",
    "up", "pin0", "pout", "embed", "small", "stem", "pout", "pin0", "embed", "small", "stem",
    "pout", "pin0", "pin1", "small", "embed", "stem", "pin0", "pin1", "pin2", "embed", "stem",
    "pin1", "pin2", "embed", "stem", "pin1", "pin2", "stem", "pin1", "pin2", "stem", "pin1",
    "pin2", "pin1", "pin2",
)


def kernel(in_names, out_names, scratch_names, *refs):
    names = in_names + out_names + scratch_names
    r = dict(zip(names, refs))
    sums = {name: {} for name in GRADS}
    for name in names:
        kind, _, which = name.partition("_")
        if which in sums and kind in KINDS:
            sums[which][KINDS[kind]] = r.pop(name)
    run(sums=sums, **r)


def run(
    features, stem_weight, group_gain, group_bias, embed_weight, first_gain, first_bias,
    project_in, project_out, second_gain, second_bias, up_weight, up_bias, down_weight,
    valid_mask, slot_slice, cotangent,
    block_out, features_grad, o_small,
    feat, stem, std, wstat, embed, pin, pout, up, down, gvec, xhs, dgs, act, gst,
    sbuf, rbuf, res1, xh1, rs1, n1, q, k, v, probs, heads, mixed, res2, xh2, rs2,
    n2, hid, branch, preg, own, csend, crecv, xsend, xrecv, mb, pg, sg, gtmp,
    sm, smr, send_sems, recv_sems, local_sems, sums,
):
    place = Place()
    net = Net(send_sems, recv_sems, local_sems)
    x, c = place.x, place.c
    R = cotangent.shape[0]
    L = feat.shape[0]
    D = up.shape[0]
    own_rows = pl.multiple_of(c * R, 16)
    sib_rows = pl.multiple_of((1 - c) * R, 16)

    def block(m):
        return pl.ds(pl.multiple_of(m * R, 16), R)

    barrier = pltpu.get_barrier_semaphore()
    peers = [place.sib, place.far] + [place.partner(name)[1] for name in place.bits]
    for peer in peers:
        pl.semaphore_signal(barrier, inc=1, device_id=peer, device_id_type=MESH)
    l_stem = net.local(stem_weight, stem.at[0])
    l_feat = net.local(features.at[pl.ds(pl.multiple_of(x * L, 16), L)], feat)
    l_embed = net.local(embed_weight, embed.at[0])
    l_cot = net.local(cotangent, branch.at[block(place.m)])
    l_pin = net.local(project_in, pin.at[0])
    l_pout = net.local(project_out, pout.at[0])
    l_up = net.local(up_weight, up)
    l_down = net.local(down_weight, down)
    gvec[0, 0:1, :] = group_gain[...].reshape(1, -1)
    gvec[0, 1:2, :] = group_bias[...].reshape(1, -1)
    pl.semaphore_wait(barrier, len(peers))

    c_gvec = net.send(gvec.at[0], gvec.at[1], place.far)

    def halves(weight, kept, pieces):
        rows = weight.shape[0] // 2 // pieces
        for t in range(pieces):
            at = pl.ds(pl.multiple_of((place.y * pieces + t) * rows, 16), rows)
            yield kept.at[1, at], net.send(weight.at[at], kept.at[1, at], place.far)

    stem_half = list(halves(stem_weight, stem, 2))
    embed_half = list(halves(embed_weight, embed, 1))
    pin_half = list(halves(project_in, pin, 2))
    pout_half = list(halves(project_out, pout, 1))
    c_cot = [
        net.send(cotangent, branch.at[block(place.m)], device) for device in (place.far, place.sib)
    ]

    def pass_on(half):
        ref, copy = half
        copy.wait_recv()
        return net.send(ref, ref, place.y_device)

    slices = valid_mask.shape[0]
    lengths = jnp.sum(valid_mask[...].astype(F32), axis=1, keepdims=True)
    mine = lax.broadcasted_iota(jnp.int32, (slices, 1), 0) == slot_slice[x]
    length = jnp.sum(jnp.where(mine, lengths, 0.0), axis=0, keepdims=True)

    def valid_rows(start, count):
        at = (lax.broadcasted_iota(jnp.int32, (count, 1), 0) + start).astype(F32)
        return jnp.where(at < length, 1.0, 0.0)

    key_valid = jnp.where(
        lax.broadcasted_iota(jnp.int32, (1, L), 1).astype(F32) < length, 1.0, 0.0
    )
    score_scale = HEAD_DIM ** (-0.5)
    key_scale = key_valid * score_scale
    key_shift = (key_valid - 1.0) * 1e9

    channels = stem.shape[2]
    same = (
        lax.div(lax.broadcasted_iota(jnp.int32, (channels, channels), 0), GROUP)
        == lax.div(lax.broadcasted_iota(jnp.int32, (channels, channels), 1), GROUP)
    )
    same = jnp.where(same, 1.0, 0.0)

    def group_sum(values):
        wide = jnp.broadcast_to(values, (8, channels))
        return dot(wide, same, precision=lax.Precision.HIGHEST)[0:1]

    def standardize(j):
        w = stem[j].astype(F32)
        average = jnp.sum(w, axis=0, keepdims=True) * (1.0 / w.shape[0])
        w = w - average
        scale = lax.rsqrt(jnp.sum(w * w, axis=0, keepdims=True) * (1.0 / w.shape[0]) + 1e-5)
        std[j] = (w * scale).astype(BF16)
        wstat[j, 0:1, :] = average
        wstat[j, 1:2, :] = scale

    tile_rows = [(t * R, R) for t in range(L // R)]

    def stem_forward(j):
        count = 1.0 / (length * GROUP)
        total = jnp.zeros((1, channels), F32)
        for at, size in tile_rows:
            s = dot(feat[at : at + size, :], std[j])
            xhs[j, at : at + size, :] = s
            total = total + jnp.sum(s * valid_rows(at, size), axis=0, keepdims=True)
        average = group_sum(total) * count
        total = jnp.zeros((1, channels), F32)
        for at, size in tile_rows:
            s = xhs[j, at : at + size, :] - average
            total = total + jnp.sum(s * s * valid_rows(at, size), axis=0, keepdims=True)
        scale = lax.rsqrt(group_sum(total) * count + 1e-5)
        gst[j, 0:1, :] = scale
        for at, size in tile_rows:
            xh = (xhs[j, at : at + size, :] - average) * scale
            xhs[j, at : at + size, :] = xh
            value, slope = gelu_parts(xh * gvec[j, 0:1, :] + gvec[j, 1:2, :])
            act[j, at : at + size, :] = value.astype(BF16)
            dgs[j, at : at + size, :] = slope

    l_stem.wait()
    standardize(0)
    c_stem = [pass_on(stem_half[0])]
    l_feat.wait()
    stem_forward(0)
    c_stem.append(pass_on(stem_half[1]))
    c_gvec.wait_recv()
    c_embed = pass_on(embed_half[0])
    for copy in c_stem:
        copy.wait_recv()
    standardize(1)
    stem_forward(1)
    l_embed.wait()
    c_embed.wait_recv()

    def core_sum(product):
        width = pl.ds(0, D)
        sbuf[:, width] = product(sib_rows)
        copy = net.send(sbuf.at[:, width], rbuf.at[:, width], place.sib)
        mine = product(own_rows)
        copy.wait_recv()
        net.sent(copy)
        return mine

    def embed_product(start):
        rows = pl.ds(start, R)
        return dot(act[0, rows, :], embed[0]) + dot(act[1, rows, :], embed[1])

    res1[...] = core_sum(embed_product)

    step = R // 3

    def layer_norm(res, other, add, gain, bias, xh_ref, scale_ref, out_ref, out_start):
        gain, bias = gain[...].reshape(1, -1), bias[...].reshape(1, -1)
        for t in range(3):
            rows = slice(t * step, (t + 1) * step)
            value = res[rows, :] + other[rows, 0:D]
            if add is not None:
                value = value + add[rows, :]
            res[rows, :] = value
            average = jnp.sum(value, axis=1, keepdims=True) * (1.0 / D)
            value = value - average
            scale = lax.rsqrt(jnp.sum(value * value, axis=1, keepdims=True) * (1.0 / D) + 1e-6)
            xh = value * scale
            xh_ref[rows, :] = xh
            scale_ref[rows, :] = scale
            out_ref[pl.ds(out_start + t * step, step), :] = (xh * gain + bias).astype(BF16)

    c_pin = [pass_on(pin_half[0])]
    layer_norm(res1, rbuf, None, first_gain, first_bias, xh1, rs1, n1, own_rows)
    c_n1 = net.send(n1.at[pl.ds(own_rows, R)], n1.at[pl.ds(own_rows, R)], place.sib)
    l_pin.wait()
    c_n1.wait_recv()
    c_pin.append(pass_on(pin_half[1]))

    per_shard = pin.shape[1] // (3 * HEAD_DIM)

    def attend(j):
        for at, size in tile_rows:
            packed = dot(n1[at : at + size, :], pin[j], 1, 1).astype(BF16)
            for h in range(per_shard):
                for i, ref in enumerate((q, k, v)):
                    lane = (3 * h + i) * HEAD_DIM
                    ref[per_shard * j + h, at : at + size, :] = packed[:, lane : lane + HEAD_DIM]

        def head(i, carry):
            h = per_shard * j + i
            for at, size in tile_rows:
                s = dot(q[h, at : at + size, :], k[h], 1, 1) * key_scale + key_shift
                s = jnp.exp(s - jnp.max(s, axis=1, keepdims=True))
                p = (s * (1.0 / jnp.sum(s, axis=1, keepdims=True))).astype(BF16)
                probs[h, at : at + size, :] = p
                heads[h, at : at + size, :] = dot(p, v[h]).astype(BF16)
            return carry

        lax.fori_loop(0, per_shard, head, 0)

    attend(0)
    c_pout = pass_on(pout_half[0])
    for copy in c_pin:
        copy.wait_recv()
    attend(1)

    def side_by_side(pieces, store):
        at = 0
        while at < len(pieces):
            pair = pieces[at : at + 2]
            value = pair[0] if len(pair) == 1 else jnp.concatenate(pair, axis=1)
            store(slice(at * HEAD_DIM, at * HEAD_DIM + value.shape[1]), value)
            at += 2

    def store_mixed(lanes, value):
        mixed[:, lanes] = value

    side_by_side([heads[h] for h in range(2 * per_shard)], store_mixed)
    l_pout.wait()
    c_pout.wait_recv()
    out_width = pout.shape[1]

    def out_product(start):
        rows = pl.ds(start, R)
        whole = jnp.concatenate([pout[0], pout[1]], axis=0)
        return dot(mixed[rows, :], whole)

    res2[...] = core_sum(out_product)
    layer_norm(
        res2, rbuf, res1, second_gain, second_bias, xh2, rs2, n2, pl.multiple_of(place.m * R, 16)
    )
    mine = block(place.m)
    c_n2 = [net.send(n2.at[mine], n2.at[mine], device) for device in (place.far, place.sib)]

    l_cot.wait()
    l_up.wait()
    l_down.wait()
    bias_sum = []

    def feed(m):
        rows = block(m)
        pre = dot(n2[rows, :], up[...]) + up_bias[...].reshape(1, -1)
        value, slope = gelu_parts(pre)
        hid[rows, :] = value.astype(BF16)
        grad = (dot(branch[rows, :], down[...], 1, 1) * slope).astype(BF16)
        preg[rows, :] = grad
        bias_sum.append(jnp.sum(grad.astype(F32), axis=0, keepdims=True))

    def back_part(m):
        return dot(preg[block(m), :], up[...], 1, 1)

    def out_part(m):
        return dot(hid[block(m), :], down[...])

    def mask_branch(m, own_slot):
        rows = block(m)
        start = lax.rem(m, 2) * R
        branch[rows, :] = (
            branch[rows, :].astype(F32) * valid_of(own_slot, start)
        ).astype(BF16)

    mine_far = lax.broadcasted_iota(jnp.int32, (slices, 1), 0) == slot_slice[1 - x]
    far_length = jnp.sum(jnp.where(mine_far, lengths, 0.0), axis=0, keepdims=True)

    def valid_of(own_slot, start):
        at = (lax.broadcasted_iota(jnp.int32, (R, 1), 0) + start).astype(F32)
        return jnp.where(at < (length if own_slot else far_length), 1.0, 0.0)

    c_cot[0].wait_recv()
    f_rows = block(place.far_m)
    c_cot_fwd = net.send(branch.at[f_rows], branch.at[f_rows], place.sib)
    mask_done = []

    mask_branch(place.m, True)
    feed(place.m)
    own[1] = back_part(place.m)
    c_cot[1].wait_recv()
    c_n2[1].wait_recv()
    mask_branch(place.sib_m, True)
    feed(place.sib_m)
    csend[1, 0] = back_part(place.sib_m).astype(BF16)
    c_core = {}
    c_core[1, 0] = net.send(csend.at[1, 0], crecv.at[1, 0], place.sib)
    c_n2[0].wait_recv()
    c_n2_fwd = net.send(n2.at[f_rows], n2.at[f_rows], place.sib)
    csend[0, 0] = out_part(place.sib_m).astype(BF16)
    c_core[0, 0] = net.send(csend.at[0, 0], crecv.at[0, 0], place.sib)
    own[0] = out_part(place.m)
    c_cot_fwd.wait_recv()
    c_n2_fwd.wait_recv()
    mask_branch(place.far_sib_m, False)
    feed(place.far_sib_m)
    csend[1, 1] = back_part(place.far_sib_m).astype(BF16)
    c_core[1, 1] = net.send(csend.at[1, 1], crecv.at[1, 1], place.sib)
    net.sent(c_cot_fwd)
    mask_branch(place.far_m, False)
    feed(place.far_m)
    sbuf[:, 0:D] = back_part(place.far_m)
    c_core[1, 1].wait_recv()
    xsend[1] = (sbuf[:, 0:D] + crecv[1, 1].astype(F32)).astype(BF16)
    c_far = {}
    c_far[1] = net.send(xsend.at[1], xrecv.at[1], place.far)
    csend[0, 1] = out_part(place.far_sib_m).astype(BF16)
    c_core[0, 1] = net.send(csend.at[0, 1], crecv.at[0, 1], place.sib)
    sbuf[:, 0:D] = out_part(place.far_m)
    c_core[0, 1].wait_recv()
    xsend[0] = (sbuf[:, 0:D] + crecv[0, 1].astype(F32)).astype(BF16)
    c_far[0] = net.send(xsend.at[0], xrecv.at[0], place.far)

    def make(name, order):
        return Summed(net, place, order, **sums[name])

    summed = {name: make(name, "ayb" if name == "up" else "yab") for name in GRADS}

    def keep(name, which, at, value):
        ref = sums[name][which]
        rows = ref.shape[1]
        count = value.shape[0] // rows
        ref[at : at + count] = value.reshape(count, rows, value.shape[1]).astype(BF16)

    half = D // 2
    for i in range(2):
        value = dot(hid[:, i * half : (i + 1) * half], branch[...], 0, 0)
        keep("down", "grad", 4 * i, value)
    summed["down"].start()
    for i in range(2):
        value = dot(n2[:, i * half : (i + 1) * half], preg[...], 0, 0)
        keep("up", "grad", 4 * i, value)
    summed["up"].start()
    sm[...] = jnp.zeros_like(sm)
    sm[4:5, :] = bias_sum[0] + bias_sum[1] + bias_sum[2] + bias_sum[3]

    def norm_back(grad_of, gain, xh_ref, scale_ref, kept, out_ref, out_start, row):
        gain = gain[...].reshape(1, -1)
        gain_sum = jnp.zeros((1, D), F32)
        bias_total = jnp.zeros((1, D), F32)
        for t in range(3):
            rows = slice(t * step, (t + 1) * step)
            dy, through = grad_of(rows)
            xh = xh_ref[rows, :]
            gain_sum = gain_sum + jnp.sum(dy * xh, axis=0, keepdims=True)
            bias_total = bias_total + jnp.sum(dy, axis=0, keepdims=True)
            dy = dy * gain
            mean_one = jnp.sum(dy, axis=1, keepdims=True) * (1.0 / D)
            mean_two = jnp.sum(dy * xh, axis=1, keepdims=True) * (1.0 / D)
            dx = through + scale_ref[rows, :] * (dy - mean_one - xh * mean_two)
            if kept is not None:
                kept[rows, :] = dx
            out_ref[pl.ds(out_start + t * step, step), :] = dx.astype(BF16)
        sm[row : row + 1, :] = gain_sum
        sm[row + 1 : row + 2, :] = bias_total

    own_part = pl.ds(own_rows, R)
    sg2, eb = res1, mb
    copies = {}
    locals_left = []
    tasks = {}

    def task(function):
        tasks[function.__name__] = function

    @task
    def norm2():
        c_core[1, 0].wait_recv()
        c_far[1].wait_recv()

        def grad_of(rows):
            dy = own[1, rows, :] + crecv[1, 0, rows, :].astype(F32) + xrecv[1, rows, :].astype(F32)
            at = pl.ds(pl.multiple_of(place.m * R, 16) + rows.start, step)
            return dy, branch[at, :].astype(F32)

        norm_back(grad_of, second_gain, xh2, rs2, sg2, mb, own_rows, 2)
        copies["mb"] = net.send(mb.at[own_part], mb.at[own_part], place.sib)

    @task
    def result():
        c_core[0, 0].wait_recv()
        c_far[0].wait_recv()
        net.sent(c_core[0, 0])
        for t in range(3):
            rows = slice(t * step, (t + 1) * step)
            value = (
                res2[rows, :]
                + own[0, rows, :]
                + crecv[0, 0, rows, :].astype(F32)
                + xrecv[0, rows, :].astype(F32)
            )
            csend[0, 0, rows, :] = (value * valid_rows(own_rows + t * step, step)).astype(BF16)
        locals_left.append(net.local(csend.at[0, 0], block_out))

    whole_out = jnp.concatenate([pout[0], pout[1]], axis=0)

    @task
    def mixed_back():
        copies["mb"].wait_recv()
        value = dot(mixed[...], mb[...], 0, 0)
        shard = pout.shape[1]
        for j, which in ((1, "far"), (0, "grad")):
            rows = value[j * shard : (j + 1) * shard]
            for i in range(2):
                keep("pout", which, 4 * i, rows[:, i * half : (i + 1) * half])
        summed["pout"].send_far()
        for at, size in tile_rows:
            value = dot(mb[at : at + size, :], whole_out, 1, 1).astype(BF16)
            for h in range(2 * per_shard):
                heads[h, at : at + size, :] = value[:, h * HEAD_DIM : (h + 1) * HEAD_DIM]

    def head_back(h, carry):
        p = probs[h]
        dp = dot(heads[h], v[h], 1, 1)
        v[h] = dot(p, heads[h], 0, 0).astype(BF16)
        p = p.astype(F32)
        ds = (p * (dp - jnp.sum(p * dp, axis=1, keepdims=True))).astype(BF16)
        dq = (dot(ds, k[h]) * score_scale).astype(BF16)
        k[h] = (dot(ds, q[h], 0, 0) * score_scale).astype(BF16)
        q[h] = dq
        return carry

    def pin_back(j, which):
        lax.fori_loop(per_shard * j, per_shard * (j + 1), head_back, 0)

        def store_pg(lanes, value):
            pg[j, :, lanes] = value

        pieces = [ref[per_shard * j + h] for h in range(per_shard) for ref in (q, k, v)]
        side_by_side(pieces, store_pg)
        value = dot(pg[j], n1[...], 0, 0)
        wide = D // 6
        for i in range(6):
            keep("pin%d" % (i // 2), which, 4 * (i % 2), value[:, i * wide : (i + 1) * wide])

    @task
    def heads_far():
        pin_back(1, "far")
        summed["pin0"].send_far()

    @task
    def heads_own():
        pin_back(0, "grad")

    @task
    def norm1_send():
        def product(start):
            rows = pl.ds(start, R)
            return dot(pg[0, rows, :], pin[0]) + dot(pg[1, rows, :], pin[1])

        width = pl.ds(0, D)
        sbuf[:, width] = product(sib_rows)
        copies["n1"] = net.send(sbuf.at[:, width], rbuf.at[:, width], place.sib)
        xh2[...] = product(own_rows)

    @task
    def norm1():
        copies["n1"].wait_recv()
        net.sent(copies["n1"])

        def grad_of(rows):
            return xh2[rows, :] + rbuf[rows, 0:D], sg2[rows, :]

        net.sent(copies["mb"])
        norm_back(grad_of, first_gain, xh1, rs1, None, eb, own_rows, 0)
        copies["eb"] = net.send(eb.at[own_part], eb.at[own_part], place.sib)

    def embed_back(j, which):
        keep("embed", which, 0, dot(act[j], eb[...], 0, 0))

    cin = feat.shape[1]

    def stem_back(j, which):
        gain_sum = jnp.zeros((1, channels), F32)
        bias_total = jnp.zeros((1, channels), F32)
        for at, size in tile_rows:
            dz = dot(eb[at : at + size, :], embed[j], 1, 1) * dgs[j, at : at + size, :]
            dgs[j, at : at + size, :] = dz
            gain_sum = gain_sum + jnp.sum(dz * xhs[j, at : at + size, :], axis=0, keepdims=True)
            bias_total = bias_total + jnp.sum(dz, axis=0, keepdims=True)
        sm[5 + j : 6 + j, 0:channels] = gain_sum
        sm[5 + j : 6 + j, channels : 2 * channels] = bias_total
        gain = gvec[j, 0:1, :]
        count = 1.0 / (length * GROUP)
        mean_one = group_sum(bias_total * gain) * count
        mean_two = group_sum(gain_sum * gain) * count
        for at, size in tile_rows:
            part = dgs[j, at : at + size, :] * gain - valid_rows(at, size) * (
                mean_one + xhs[j, at : at + size, :] * mean_two
            )
            sg[j, at : at + size, :] = (part * gst[j, 0:1, :]).astype(BF16)
        average, scale = wstat[j, 0:1, :], wstat[j, 1:2, :]
        sum_one = jnp.zeros((1, channels), F32)
        sum_two = jnp.zeros((1, channels), F32)
        quarter = cin // 4
        for t in range(4):
            rows = slice(t * quarter, (t + 1) * quarter)
            grad = dot(feat[:, rows], sg[j], 0, 0)
            gtmp[rows, :] = grad
            xh = (stem[j, rows, :].astype(F32) - average) * scale
            sum_one = sum_one + jnp.sum(grad, axis=0, keepdims=True)
            sum_two = sum_two + jnp.sum(grad * xh, axis=0, keepdims=True)
        sum_one = sum_one * (1.0 / cin)
        sum_two = sum_two * (1.0 / cin)
        for t in range(4):
            rows = slice(t * quarter, (t + 1) * quarter)
            xh = (stem[j, rows, :].astype(F32) - average) * scale
            keep("stem", which, 2 * t, (gtmp[rows, :] - sum_one - xh * sum_two) * scale)

    @task
    def stem_far():
        copies["eb"].wait_recv()
        embed_back(1, "far")
        summed["embed"].send_far()
        stem_back(1, "far")
        for name in ("stem", "pin1", "pin2"):
            summed[name].send_far()

    @task
    def stem_own():
        embed_back(0, "grad")
        stem_back(0, "grad")
        small("core")

    @task
    def features_send():
        def product(start):
            rows = pl.ds(start, R)
            return dot(sg[0, rows, :], std[0], 1, 1) + dot(sg[1, rows, :], std[1], 1, 1)

        sbuf[...] = product(sib_rows)
        copies["feat"] = net.send(sbuf, rbuf, place.sib)
        copies["feat_own"] = product(own_rows)

    @task
    def features_sum():
        copies["feat"].wait_recv()
        net.sent(copies["feat"])
        sbuf[...] = copies["feat_own"] + rbuf[...]
        locals_left.append(net.local(sbuf, features_grad))

    small_at = {"core": place.sib, "x": place.far}
    for name in place.bits:
        small_at[name] = place.partner(name)[1]
    small_order = tuple(small_at)

    def small(name):
        copies["small"] = net.send(sm, smr.at[small_order.index(name)], small_at[name])

    def small_step(i):
        copies["small"].wait_recv()
        net.sent(copies["small"])
        if small_order[i] in ("core", "x"):
            sm[0:4, :] = sm[0:4, :] + smr[i, 0:4, :]
            if small_order[i] == "x":
                sm[5:6, :] = sm[5:6, :] + smr[i, 6:7, :]
        else:
            sm[...] = sm[...] + smr[i]
        if i + 1 < len(small_order):
            small(small_order[i + 1])
        else:
            o_small[...] = sm[...]

    small_next = list(range(len(small_order)))
    for name in ORDER:
        if name in tasks:
            tasks.pop(name)()
        elif name == "small":
            small_step(small_next.pop(0))
        else:
            summed[name].step()
    assert not tasks and not small_next
    for one in summed.values():
        one.step_all()
    for copy in locals_left:
        copy.wait()
    net.finish()


def body(
    features, stem_weight, group_gain, group_bias, embed_weight, first_gain, first_bias,
    project_in, project_out, second_gain, second_bias, up_weight, up_bias, down_weight,
    valid_mask, slot_slice, cotangent, *, dp,
):
    slots = slot_slice.shape[0]
    L = features.shape[0] // slots
    R = cotangent.shape[0]
    cin, channels = stem_weight.shape
    D = cotangent.shape[1]
    wide_in = project_in.shape[1]
    project_in = project_in.T
    out_rows = project_out.shape[0]
    hidden = up_weight.shape[1]
    heads = 2 * wide_in // (3 * HEAD_DIM)
    hbm = pl.BlockSpec(memory_space=pl.ANY)
    vmem = pl.BlockSpec(memory_space=pltpu.VMEM)
    smem = pl.BlockSpec(memory_space=pltpu.SMEM)
    in_specs = dict(
        features=hbm, stem_weight=hbm, group_gain=vmem, group_bias=vmem, embed_weight=hbm,
        first_gain=vmem, first_bias=vmem, project_in=hbm, project_out=hbm, second_gain=vmem,
        second_bias=vmem, up_weight=hbm, up_bias=vmem, down_weight=hbm, valid_mask=vmem,
        slot_slice=smem, cotangent=hbm,
    )
    parts = dict(
        up=(D // 8, hidden),
        down=(hidden // 8, D),
        pout=(out_rows // 4, D // 2),
        pin0=(wide_in // 4, D // 6),
        pin1=(wide_in // 4, D // 6),
        pin2=(wide_in // 4, D // 6),
        embed=(channels // 8, D),
        stem=(cin // 8, channels),
    )
    outs = dict(
        block_out=((R, D), BF16, hbm),
        features_grad=((R, cin), F32, hbm),
        o_small=((8, D), F32, vmem),
    )
    for name in GRADS:
        outs["o_" + name] = ((8,) + parts[name], BF16, hbm)
    scratch = dict(
        feat=((L, cin), BF16), stem=((2, cin, channels), BF16), std=((2, cin, channels), BF16),
        wstat=((2, 8, channels), F32), embed=((2, channels, D), BF16), pin=((2, wide_in, D), BF16),
        pout=((2, out_rows, D), BF16), up=((D, hidden), BF16), down=((hidden, D), BF16),
        gvec=((2, 8, channels), F32), xhs=((2, L, channels), F32), dgs=((2, L, channels), F32),
        act=((2, L, channels), BF16), gst=((2, 8, channels), F32),
        sbuf=((R, cin), F32), rbuf=((R, cin), F32), res1=((R, D), F32), xh1=((R, D), F32),
        rs1=((R, 1), F32), n1=((L, D), BF16), q=((heads, L, HEAD_DIM), BF16),
        k=((heads, L, HEAD_DIM), BF16), v=((heads, L, HEAD_DIM), BF16), probs=((heads, L, L), BF16),
        heads=((heads, L, HEAD_DIM), BF16), mixed=((L, heads * HEAD_DIM), BF16),
        res2=((R, D), F32), xh2=((R, D), F32), rs2=((R, 1), F32), n2=((4 * R, D), BF16),
        hid=((4 * R, hidden), BF16), branch=((4 * R, D), BF16), preg=((4 * R, hidden), BF16),
        own=((2, R, D), F32), csend=((2, 2, R, D), BF16),
        crecv=((2, 2, R, D), BF16), xsend=((2, R, D), BF16), xrecv=((2, R, D), BF16),
        mb=((L, D), BF16), pg=((2, L, wide_in), BF16),
        sg=((2, L, channels), BF16), gtmp=((cin, channels), F32),
    )
    for kind, count, names in (
        ("g_", 8, GRADS), ("f_", 8, BY_SLOT), ("i_", 8, BY_SLOT), ("r_", 7, GRADS), ("p_", 1, GRADS)
    ):
        for name in names:
            scratch[kind + name] = ((count,) + parts[name], BF16)
    scratch.update(sm=((8, D), F32), smr=((5, 8, D), F32))
    copies = 112
    shapes = [pltpu.VMEM(*one) for one in scratch.values()]
    shapes += [pltpu.SemaphoreType.DMA((copies,)) for _ in range(2)]
    shapes += [pltpu.SemaphoreType.DMA((24,))]
    names = tuple(scratch) + ("send_sems", "recv_sems", "local_sems")
    results = pl.pallas_call(
        functools.partial(kernel, tuple(in_specs), tuple(outs), names),
        out_shape=[jax.ShapeDtypeStruct(shape, kind) for shape, kind, _ in outs.values()],
        in_specs=list(in_specs.values()),
        out_specs=[spec for _, _, spec in outs.values()],
        scratch_shapes=shapes,
        compiler_params=pltpu.CompilerParams(
            collective_id=0, has_side_effects=True, vmem_limit_bytes=62 * 2**20
        ),
        name="layer",
    )(
        features, stem_weight, group_gain, group_bias, embed_weight, first_gain, first_bias,
        project_in, project_out, second_gain, second_bias, up_weight, up_bias, down_weight,
        valid_mask, slot_slice, cotangent,
    )
    out = dict(zip(outs, results))

    wide = {name: out["o_" + name].astype(F32) for name in GRADS}
    small = out["o_small"]
    bit = NEAR
    while bit < dp:
        pairs = [(i, i ^ bit) for i in range(dp)]
        wide, small = jax.tree.map(
            lambda part: part + lax.ppermute(part, "dp", pairs), (wide, small)
        )
        bit *= 2

    def rows_of(name):
        return wide[name].reshape(-1, wide[name].shape[-1])

    def side_by_side(part, blocks):
        count, rows, columns = part.shape
        part = part.reshape(blocks, count // blocks * rows, columns)
        return jnp.moveaxis(part, 0, 1).reshape(-1, blocks * columns)

    pin = jnp.concatenate([wide["pin0"], wide["pin1"], wide["pin2"]], axis=0)
    project_in_grad = side_by_side(pin, 6).T
    project_out_grad = side_by_side(wide["pout"], 2)
    return (
        out["block_out"],
        out["features_grad"],
        rows_of("stem"),
        small[5, 0:channels],
        small[5, channels : 2 * channels],
        rows_of("embed"),
        small[0],
        small[1],
        project_in_grad,
        project_out_grad,
        small[2],
        small[3],
        rows_of("up"),
        small[4],
        rows_of("down"),
    )


def solution(mesh):
    return jax.shard_map(
        functools.partial(body, dp=mesh.shape["dp"]),
        mesh=mesh,
        in_specs=(
            P("dp", None), P(None, "mp"), P("mp"), P("mp"), P("mp", None), P(), P(),
            P(None, "mp"), P("mp", None), P(), P(), P(None, "mp"), P("mp"), P("mp", None),
            P(), P("dp"), P(("dp", "mp"), None),
        ),
        out_specs=(
            P(("dp", "mp"), None), P(("dp", "mp"), None), P(None, "mp"), P("mp"), P("mp"),
            P("mp", None), P(), P(), P(None, "mp"), P("mp", None), P(), P(), P(None, "mp"),
            P("mp"), P("mp", None),
        ),
        check_vma=False,
    )
```

```python
import functools
import itertools

import jax
import jax.numpy as jnp
from jax import lax
from jax.experimental import pallas as pl
from jax.experimental.pallas import tpu as pltpu
from jax.sharding import PartitionSpec as P

MESH = pl.DeviceIdType.MESH
F32 = jnp.float32
BF16 = jnp.bfloat16
HEAD_DIM = 64
GROUP = 32
NEAR = 8


def dot(left, right, left_dim=1, right_dim=0, precision=None):
    return lax.dot_general(
        left,
        right,
        (((left_dim,), (right_dim,)), ((), ())),
        precision=precision,
        preferred_element_type=F32,
    )


def gelu_parts(z):
    cdf = 0.5 + 0.5 * lax.erf(z * 0.7071067811865476)
    return z * cdf, cdf + z * (jnp.exp(-0.5 * z * z) * 0.3989422804014327)


class Net:
    def __init__(self, send_sems, recv_sems, local_sems):
        self.send_sems, self.recv_sems, self.local_sems = send_sems, recv_sems, local_sems
        self.count, self.local_count, self.unsent = 0, 0, []

    def send(self, src, dst, device):
        copy = pltpu.make_async_remote_copy(
            src_ref=src,
            dst_ref=dst,
            send_sem=self.send_sems.at[self.count],
            recv_sem=self.recv_sems.at[self.count],
            device_id=device,
            device_id_type=MESH,
        )
        self.count += 1
        copy.start()
        self.unsent.append(copy)
        return copy

    def sent(self, copy):
        self.unsent = [one for one in self.unsent if one is not copy]
        copy.wait_send()

    def local(self, src, dst):
        copy = pltpu.make_async_copy(src, dst, self.local_sems.at[self.local_count])
        self.local_count += 1
        copy.start()
        return copy

    def finish(self):
        for copy in self.unsent:
            copy.wait_send()


class Summed:
    def __init__(self, net, place, away, back, grad, arrive, piece, out):
        self.net, self.place, self.away, self.back = net, place, away, back
        self.grad, self.arrive, self.piece, self.out = grad, arrive, piece, out
        self.dims = "xyab"[4 - (len(grad.shape) - 2) :]
        self.fixed = {}
        self.level, self.gathered = 0, None

    def index(self, dims, **more):
        fixed = {**self.fixed, **more}
        return tuple(pl.ds(fixed[dim], 1) if dim in fixed else pl.ds(0, 2) for dim in dims)

    def start(self):
        dim = self.away[self.level]
        bit, partner = self.place.partner(dim)
        give = self.index(self.dims, **{dim: 1 - bit})
        self.fixed[dim] = bit
        self.copy = self.net.send(self.grad.at[give], self.arrive[self.level], partner)

    def share(self, source):
        dim = self.back[len(self.gathered)]
        bit, partner = self.place.partner(dim)
        held = self.index("yab")
        self.copy = self.net.send(self.out.at[held] if source is None else source, self.out.at[held], partner)
        self.gathered.append(dim)
        del self.fixed[dim]

    def add(self, arrived, store):
        for at in itertools.product((0, 1), repeat=len(self.dims)):
            here = dict(zip(self.dims, at))
            if any(here[dim] for dim in self.fixed):
                continue
            where = tuple(self.fixed.get(dim, here[dim]) for dim in self.dims)
            store(where, self.grad[where].astype(F32) + arrived[at].astype(F32))

    def step(self):
        self.copy.wait_recv()
        if self.gathered is None:
            arrived = self.arrive[self.level]
            self.level += 1
            if self.level < len(self.away):

                def store(where, value):
                    self.grad[where] = value.astype(BF16)

                self.add(arrived, store)
                self.start()
            else:

                def store(where, value):
                    self.piece[0, 0, 0] = value.astype(BF16)

                self.add(arrived, store)
                self.fixed.pop("x", None)
                self.gathered = []
                self.own = self.net.local(self.piece, self.out.at[self.index("yab")])
                self.share(self.piece)
        else:
            if len(self.gathered) == 1:
                self.own.wait()
            if len(self.gathered) < 3:
                self.share(None)
            else:
                self.copy = None

    def step_all(self):
        while self.copy is not None:
            self.step()


class Place:
    def __init__(self):
        self.d = lax.axis_index("dp")
        self.m = lax.axis_index("mp")
        self.x = lax.div(self.m, 2)
        self.c = lax.rem(self.m, 2)
        self.y = lax.rem(self.d, 2)
        self.zi = lax.div(lax.rem(self.d, NEAR), 2)
        self.bits = {"x": (0, None), "y": (self.y, 1), "a": (lax.rem(self.zi, 2), 2), "b": (lax.div(self.zi, 2), 4)}
        self.sib_m = self.m + 1 - 2 * self.c
        self.far_m = lax.rem(self.m + 2, 4)
        self.far_sib_m = lax.rem(self.sib_m + 2, 4)
        self.sib = (self.d, self.sib_m)
        self.far = (self.d, self.far_m)
        self.y_device = (self.d + 1 - 2 * self.y, self.m)

    def partner(self, name):
        bit, stride = self.bits[name]
        if stride is None:
            return bit, self.far
        return bit, (self.d + stride - 2 * stride * bit, self.m)


GRADS = ("up", "down", "pout", "pin0", "pin1", "pin2", "embed", "stem0", "stem1")
BY_SLOT = GRADS[2:]
KINDS = dict(g="grad", p="piece", o="out", r0="arrive0", r1="arrive1", r2="arrive2", r3="arrive3")
AWAY = dict(
    down="yab",
    up="bay",
    pout="yxab",
    pin0="yxab",
    pin1="xyab",
    pin2="xyba",
    embed="xyab",
    stem0="yxab",
    stem1="xyab",
)
BACK = dict(
    down="bay",
    up="bay",
    pout="aby",
    pin0="aby",
    pin1="bya",
    pin2="yba",
    embed="yba",
    stem0="yab",
    stem1="aby",
)
ORDER = (
    "norm2", "+result", "mixed_back", "+pout", "heads_far", "+pin1", "down", "heads_own", "pout",
    "norm1_send", "+pin2", "norm1", "down", "pin1", "stem_far", "+pin0", "up", "pout",
    "stem_own", "+embed", "pin1", "features_send", "small", "pin2", "down", "features_sum",
    "+stem0", "+stem1", "result", "pin0", "up", "pout", "pin2", "pin1", "embed", "small", "down",
    "pout", "stem0", "stem1", "pin2", "up", "pin1", "pin0", "embed", "small", "down", "stem0",
    "pout", "pin2", "stem1", "up", "pin0", "pin1", "embed", "small", "pout", "stem0", "pin0",
    "stem1", "embed", "down", "small", "pin2", "stem0", "pin1", "stem1", "up", "pout", "embed",
    "stem0", "pin2", "pin0", "pin1", "embed", "stem1", "pin0", "stem0", "up", "pin2", "stem1",
    "pin0", "embed", "stem1", "stem0",
)


def kernel(in_names, out_names, scratch_names, *refs):
    names = in_names + out_names + scratch_names
    r = dict(zip(names, refs))
    sums = {name: {} for name in GRADS}
    for name in names:
        kind, _, which = name.partition("_")
        if which in sums and kind in KINDS:
            sums[which][KINDS[kind]] = r.pop(name)
    for refs in sums.values():
        refs["arrive"] = [refs.pop(kind) for kind in sorted(refs) if kind.startswith("arrive")]
    run(sums=sums, **r)


def run(
    features, stem_weight, group_gain, group_bias, embed_weight, first_gain, first_bias,
    project_in, project_out, second_gain, second_bias, up_weight, up_bias, down_weight,
    valid_mask, slot_slice, cotangent,
    block_out, features_grad, o_small,
    feat, stem, std, wstat, embed, pin, pout, up, down, gvec, xhs, dgs, act, gst,
    sbuf, rbuf, res1, xh1, rs1, n1, q, k, v, probs, heads, mixed, res2, xh2, rs2,
    n2, hid, branch, preg, own, csend, crecv, xsend, xrecv, mb, pg, sg, gtmp,
    sm, smr, send_sems, recv_sems, local_sems, sums,
):
    place = Place()
    net = Net(send_sems, recv_sems, local_sems)
    x, c = place.x, place.c
    R = cotangent.shape[0]
    L = feat.shape[0]
    D = up.shape[0]
    own_rows = pl.multiple_of(c * R, 16)
    sib_rows = pl.multiple_of((1 - c) * R, 16)

    def block(m):
        return pl.ds(pl.multiple_of(m * R, 16), R)

    barrier = pltpu.get_barrier_semaphore()
    peers = [place.sib] + [place.partner(name)[1] for name in place.bits]
    for peer in peers:
        pl.semaphore_signal(barrier, inc=1, device_id=peer, device_id_type=MESH)
    l_stem = net.local(stem_weight, stem.at[0])
    l_feat = net.local(features.at[pl.ds(pl.multiple_of(x * L, 16), L)], feat)
    l_embed = net.local(embed_weight, embed.at[0])
    l_cot = net.local(cotangent, branch.at[block(place.m)])
    l_pin = net.local(project_in, pin.at[0])
    l_pout = net.local(project_out, pout.at[0])
    l_up = net.local(up_weight, up)
    l_down = net.local(down_weight, down)
    gvec[0, 0:1, :] = group_gain[...].reshape(1, -1)
    gvec[0, 1:2, :] = group_bias[...].reshape(1, -1)
    pl.semaphore_wait(barrier, len(peers))

    c_gvec = net.send(gvec.at[0], gvec.at[1], place.far)

    def halves(weight, kept, pieces):
        rows = weight.shape[0] // 2 // pieces
        for t in range(pieces):
            at = pl.ds(pl.multiple_of((place.y * pieces + t) * rows, 16), rows)
            yield kept.at[1, at], net.send(weight.at[at], kept.at[1, at], place.far)

    stem_half = list(halves(stem_weight, stem, 2))
    embed_half = list(halves(embed_weight, embed, 1))
    pin_half = list(halves(project_in, pin, 2))
    pout_half = list(halves(project_out, pout, 1))
    c_cot = [
        net.send(cotangent, branch.at[block(place.m)], device) for device in (place.far, place.sib)
    ]

    def pass_on(half):
        ref, copy = half
        copy.wait_recv()
        return net.send(ref, ref, place.y_device)

    slices = valid_mask.shape[0]
    lengths = jnp.sum(valid_mask[...].astype(F32), axis=1, keepdims=True)
    mine = lax.broadcasted_iota(jnp.int32, (slices, 1), 0) == slot_slice[x]
    length = jnp.sum(jnp.where(mine, lengths, 0.0), axis=0, keepdims=True)

    def valid_rows(start, count):
        at = (lax.broadcasted_iota(jnp.int32, (count, 1), 0) + start).astype(F32)
        return jnp.where(at < length, 1.0, 0.0)

    key_valid = jnp.where(
        lax.broadcasted_iota(jnp.int32, (1, L), 1).astype(F32) < length, 1.0, 0.0
    )
    score_scale = HEAD_DIM ** (-0.5)
    key_scale = key_valid * score_scale
    key_shift = (key_valid - 1.0) * 1e9

    channels = stem.shape[2]
    same = (
        lax.div(lax.broadcasted_iota(jnp.int32, (channels, channels), 0), GROUP)
        == lax.div(lax.broadcasted_iota(jnp.int32, (channels, channels), 1), GROUP)
    )
    same = jnp.where(same, 1.0, 0.0)

    def group_sum(values):
        wide = jnp.broadcast_to(values, (8, channels))
        return dot(wide, same, precision=lax.Precision.HIGHEST)[0:1]

    def standardize(j):
        w = stem[j].astype(F32)
        average = jnp.sum(w, axis=0, keepdims=True) * (1.0 / w.shape[0])
        w = w - average
        scale = lax.rsqrt(jnp.sum(w * w, axis=0, keepdims=True) * (1.0 / w.shape[0]) + 1e-5)
        std[j] = (w * scale).astype(BF16)
        wstat[j, 0:1, :] = average
        wstat[j, 1:2, :] = scale

    tile_rows = [(t * R, R) for t in range(L // R)]

    def stem_forward(j):
        count = 1.0 / (length * GROUP)
        total = jnp.zeros((1, channels), F32)
        for at, size in tile_rows:
            s = dot(feat[at : at + size, :], std[j])
            xhs[j, at : at + size, :] = s
            total = total + jnp.sum(s * valid_rows(at, size), axis=0, keepdims=True)
        average = group_sum(total) * count
        total = jnp.zeros((1, channels), F32)
        for at, size in tile_rows:
            s = xhs[j, at : at + size, :] - average
            total = total + jnp.sum(s * s * valid_rows(at, size), axis=0, keepdims=True)
        scale = lax.rsqrt(group_sum(total) * count + 1e-5)
        gst[j, 0:1, :] = scale
        for at, size in tile_rows:
            xh = (xhs[j, at : at + size, :] - average) * scale
            xhs[j, at : at + size, :] = xh
            value, slope = gelu_parts(xh * gvec[j, 0:1, :] + gvec[j, 1:2, :])
            act[j, at : at + size, :] = value.astype(BF16)
            dgs[j, at : at + size, :] = slope

    l_stem.wait()
    standardize(0)
    c_stem = [pass_on(stem_half[0])]
    l_feat.wait()
    stem_forward(0)
    c_stem.append(pass_on(stem_half[1]))
    c_gvec.wait_recv()
    c_embed = pass_on(embed_half[0])
    for copy in c_stem:
        copy.wait_recv()
    standardize(1)
    stem_forward(1)
    l_embed.wait()
    c_embed.wait_recv()

    def core_sum(product):
        width = pl.ds(0, D)
        sbuf[:, width] = product(sib_rows)
        copy = net.send(sbuf.at[:, width], rbuf.at[:, width], place.sib)
        mine = product(own_rows)
        copy.wait_recv()
        net.sent(copy)
        return mine

    def embed_product(start):
        rows = pl.ds(start, R)
        return dot(act[0, rows, :], embed[0]) + dot(act[1, rows, :], embed[1])

    res1[...] = core_sum(embed_product)

    step = R // 3

    def layer_norm(res, other, add, gain, bias, xh_ref, scale_ref, out_ref, out_start):
        gain, bias = gain[...].reshape(1, -1), bias[...].reshape(1, -1)
        for t in range(3):
            rows = slice(t * step, (t + 1) * step)
            value = res[rows, :] + other[rows, 0:D]
            if add is not None:
                value = value + add[rows, :]
            res[rows, :] = value
            average = jnp.sum(value, axis=1, keepdims=True) * (1.0 / D)
            value = value - average
            scale = lax.rsqrt(jnp.sum(value * value, axis=1, keepdims=True) * (1.0 / D) + 1e-6)
            xh = value * scale
            xh_ref[rows, :] = xh
            scale_ref[rows, :] = scale
            out_ref[pl.ds(out_start + t * step, step), :] = (xh * gain + bias).astype(BF16)

    c_pin = [pass_on(pin_half[0])]
    layer_norm(res1, rbuf, None, first_gain, first_bias, xh1, rs1, n1, own_rows)
    c_n1 = net.send(n1.at[pl.ds(own_rows, R)], n1.at[pl.ds(own_rows, R)], place.sib)
    l_pin.wait()
    c_n1.wait_recv()
    c_pin.append(pass_on(pin_half[1]))

    per_shard = pin.shape[1] // (3 * HEAD_DIM)

    def attend(j):
        for at, size in tile_rows:
            packed = dot(n1[at : at + size, :], pin[j], 1, 1).astype(BF16)
            for h in range(per_shard):
                for i, ref in enumerate((q, k, v)):
                    lane = (3 * h + i) * HEAD_DIM
                    ref[per_shard * j + h, at : at + size, :] = packed[:, lane : lane + HEAD_DIM]

        def head(i, carry):
            h = per_shard * j + i
            for at, size in tile_rows:
                s = dot(q[h, at : at + size, :], k[h], 1, 1) * key_scale + key_shift
                s = jnp.exp(s - jnp.max(s, axis=1, keepdims=True))
                p = (s * (1.0 / jnp.sum(s, axis=1, keepdims=True))).astype(BF16)
                probs[h, at : at + size, :] = p
                heads[h, at : at + size, :] = dot(p, v[h]).astype(BF16)
            return carry

        lax.fori_loop(0, per_shard, head, 0)

    attend(0)
    c_pout = pass_on(pout_half[0])
    for copy in c_pin:
        copy.wait_recv()
    attend(1)

    def side_by_side(pieces, store):
        at = 0
        while at < len(pieces):
            pair = pieces[at : at + 2]
            value = pair[0] if len(pair) == 1 else jnp.concatenate(pair, axis=1)
            store(slice(at * HEAD_DIM, at * HEAD_DIM + value.shape[1]), value)
            at += 2

    def store_mixed(lanes, value):
        mixed[:, lanes] = value

    side_by_side([heads[h] for h in range(2 * per_shard)], store_mixed)
    l_pout.wait()
    c_pout.wait_recv()
    out_width = pout.shape[1]

    def out_product(start):
        rows = pl.ds(start, R)
        whole = jnp.concatenate([pout[0], pout[1]], axis=0)
        return dot(mixed[rows, :], whole)

    res2[...] = core_sum(out_product)
    layer_norm(
        res2, rbuf, res1, second_gain, second_bias, xh2, rs2, n2, pl.multiple_of(place.m * R, 16)
    )
    mine = block(place.m)
    c_n2 = [net.send(n2.at[mine], n2.at[mine], device) for device in (place.far, place.sib)]

    l_cot.wait()
    l_up.wait()
    l_down.wait()
    bias_sum = []

    def feed(m):
        rows = block(m)
        pre = dot(n2[rows, :], up[...]) + up_bias[...].reshape(1, -1)
        value, slope = gelu_parts(pre)
        hid[rows, :] = value.astype(BF16)
        grad = (dot(branch[rows, :], down[...], 1, 1) * slope).astype(BF16)
        preg[rows, :] = grad
        bias_sum.append(jnp.sum(grad.astype(F32), axis=0, keepdims=True))

    def back_part(m):
        return dot(preg[block(m), :], up[...], 1, 1)

    def out_part(m):
        return dot(hid[block(m), :], down[...])

    def mask_branch(m, own_slot):
        rows = block(m)
        start = lax.rem(m, 2) * R
        branch[rows, :] = (
            branch[rows, :].astype(F32) * valid_of(own_slot, start)
        ).astype(BF16)

    mine_far = lax.broadcasted_iota(jnp.int32, (slices, 1), 0) == slot_slice[1 - x]
    far_length = jnp.sum(jnp.where(mine_far, lengths, 0.0), axis=0, keepdims=True)

    def valid_of(own_slot, start):
        at = (lax.broadcasted_iota(jnp.int32, (R, 1), 0) + start).astype(F32)
        return jnp.where(at < (length if own_slot else far_length), 1.0, 0.0)

    c_cot[0].wait_recv()
    f_rows = block(place.far_m)
    c_cot_fwd = net.send(branch.at[f_rows], branch.at[f_rows], place.sib)
    mask_done = []

    mask_branch(place.m, True)
    feed(place.m)
    own[1] = back_part(place.m)
    c_cot[1].wait_recv()
    c_n2[1].wait_recv()
    mask_branch(place.sib_m, True)
    feed(place.sib_m)
    csend[1, 0] = back_part(place.sib_m).astype(BF16)
    c_core = {}
    c_core[1, 0] = net.send(csend.at[1, 0], crecv.at[1, 0], place.sib)
    c_n2[0].wait_recv()
    c_n2_fwd = net.send(n2.at[f_rows], n2.at[f_rows], place.sib)
    csend[0, 0] = out_part(place.sib_m).astype(BF16)
    c_core[0, 0] = net.send(csend.at[0, 0], crecv.at[0, 0], place.sib)
    own[0] = out_part(place.m)
    c_cot_fwd.wait_recv()
    c_n2_fwd.wait_recv()
    mask_branch(place.far_sib_m, False)
    feed(place.far_sib_m)
    csend[1, 1] = back_part(place.far_sib_m).astype(BF16)
    c_core[1, 1] = net.send(csend.at[1, 1], crecv.at[1, 1], place.sib)
    net.sent(c_cot_fwd)
    mask_branch(place.far_m, False)
    feed(place.far_m)
    sbuf[:, 0:D] = back_part(place.far_m)
    c_core[1, 1].wait_recv()
    xsend[1] = (sbuf[:, 0:D] + crecv[1, 1].astype(F32)).astype(BF16)
    c_far = {}
    c_far[1] = net.send(xsend.at[1], xrecv.at[1], place.far)
    csend[0, 1] = out_part(place.far_sib_m).astype(BF16)
    c_core[0, 1] = net.send(csend.at[0, 1], crecv.at[0, 1], place.sib)
    sbuf[:, 0:D] = out_part(place.far_m)
    c_core[0, 1].wait_recv()
    xsend[0] = (sbuf[:, 0:D] + crecv[0, 1].astype(F32)).astype(BF16)

    summed = {name: Summed(net, place, AWAY[name], BACK[name], **sums[name]) for name in GRADS}

    def keep(name, slot, at, value):
        ref = sums[name]["grad"]
        rows = ref.shape[-2]
        for t in range(value.shape[0] // rows):
            part = (at + t) // 4, (at + t) // 2 % 2, (at + t) % 2
            ref[part if slot is None else (slot,) + part] = value[
                t * rows : (t + 1) * rows
            ].astype(BF16)

    half = D // 2
    for i in range(2):
        value = dot(hid[:, i * half : (i + 1) * half], branch[...], 0, 0)
        keep("down", None, 4 * i, value)
    summed["down"].start()
    for i in range(2):
        value = dot(n2[:, i * half : (i + 1) * half], preg[...], 0, 0)
        keep("up", None, 4 * i, value)
    summed["up"].start()
    sm[...] = jnp.zeros_like(sm)
    sm[4:5, :] = bias_sum[0] + bias_sum[1] + bias_sum[2] + bias_sum[3]

    def norm_back(grad_of, gain, xh_ref, scale_ref, kept, out_ref, out_start, row):
        gain = gain[...].reshape(1, -1)
        gain_sum = jnp.zeros((1, D), F32)
        bias_total = jnp.zeros((1, D), F32)
        for t in range(3):
            rows = slice(t * step, (t + 1) * step)
            dy, through = grad_of(rows)
            xh = xh_ref[rows, :]
            gain_sum = gain_sum + jnp.sum(dy * xh, axis=0, keepdims=True)
            bias_total = bias_total + jnp.sum(dy, axis=0, keepdims=True)
            dy = dy * gain
            mean_one = jnp.sum(dy, axis=1, keepdims=True) * (1.0 / D)
            mean_two = jnp.sum(dy * xh, axis=1, keepdims=True) * (1.0 / D)
            dx = through + scale_ref[rows, :] * (dy - mean_one - xh * mean_two)
            if kept is not None:
                kept[rows, :] = dx
            out_ref[pl.ds(out_start + t * step, step), :] = dx.astype(BF16)
        sm[row : row + 1, :] = gain_sum
        sm[row + 1 : row + 2, :] = bias_total

    own_part = pl.ds(own_rows, R)
    sg2, eb = res1, mb
    copies = {}
    locals_left = []
    tasks = {}

    def task(function):
        tasks[function.__name__] = function

    @task
    def norm2():
        c_core[1, 0].wait_recv()
        c_far[1].wait_recv()

        def grad_of(rows):
            dy = own[1, rows, :] + crecv[1, 0, rows, :].astype(F32) + xrecv[1, rows, :].astype(F32)
            at = pl.ds(pl.multiple_of(place.m * R, 16) + rows.start, step)
            return dy, branch[at, :].astype(F32)

        norm_back(grad_of, second_gain, xh2, rs2, sg2, mb, own_rows, 2)
        copies["mb"] = net.send(mb.at[own_part], mb.at[own_part], place.sib)

    @task
    def result():
        c_core[0, 0].wait_recv()
        c_far[0].wait_recv()
        net.sent(c_core[0, 0])
        for t in range(3):
            rows = slice(t * step, (t + 1) * step)
            value = (
                res2[rows, :]
                + own[0, rows, :]
                + crecv[0, 0, rows, :].astype(F32)
                + xrecv[0, rows, :].astype(F32)
            )
            csend[0, 0, rows, :] = (value * valid_rows(own_rows + t * step, step)).astype(BF16)
        locals_left.append(net.local(csend.at[0, 0], block_out))

    whole_out = jnp.concatenate([pout[0], pout[1]], axis=0)

    @task
    def mixed_back():
        copies["mb"].wait_recv()
        value = dot(mixed[...], mb[...], 0, 0)
        shard = pout.shape[1]
        for j in range(2):
            rows = value[j * shard : (j + 1) * shard]
            for i in range(2):
                keep("pout", j, 4 * i, rows[:, i * half : (i + 1) * half])
        for at, size in tile_rows:
            value = dot(mb[at : at + size, :], whole_out, 1, 1).astype(BF16)
            for h in range(2 * per_shard):
                heads[h, at : at + size, :] = value[:, h * HEAD_DIM : (h + 1) * HEAD_DIM]

    def head_back(h, carry):
        p = probs[h]
        dp = dot(heads[h], v[h], 1, 1)
        v[h] = dot(p, heads[h], 0, 0).astype(BF16)
        p = p.astype(F32)
        ds = (p * (dp - jnp.sum(p * dp, axis=1, keepdims=True))).astype(BF16)
        dq = (dot(ds, k[h]) * score_scale).astype(BF16)
        k[h] = (dot(ds, q[h], 0, 0) * score_scale).astype(BF16)
        q[h] = dq
        return carry

    def pin_back(j):
        lax.fori_loop(per_shard * j, per_shard * (j + 1), head_back, 0)

        def store_pg(lanes, value):
            pg[j, :, lanes] = value

        pieces = [ref[per_shard * j + h] for h in range(per_shard) for ref in (q, k, v)]
        side_by_side(pieces, store_pg)
        value = dot(pg[j], n1[...], 0, 0)
        wide = D // 6
        for i in range(6):
            keep("pin%d" % (i // 2), j, 4 * (i % 2), value[:, i * wide : (i + 1) * wide])

    @task
    def heads_far():
        pin_back(1)

    @task
    def heads_own():
        pin_back(0)

    @task
    def norm1_send():
        def product(start):
            rows = pl.ds(start, R)
            return dot(pg[0, rows, :], pin[0]) + dot(pg[1, rows, :], pin[1])

        width = pl.ds(0, D)
        sbuf[:, width] = product(sib_rows)
        copies["n1"] = net.send(sbuf.at[:, width], rbuf.at[:, width], place.sib)
        xh2[...] = product(own_rows)

    @task
    def norm1():
        copies["n1"].wait_recv()
        net.sent(copies["n1"])

        def grad_of(rows):
            return xh2[rows, :] + rbuf[rows, 0:D], sg2[rows, :]

        net.sent(copies["mb"])
        norm_back(grad_of, first_gain, xh1, rs1, None, eb, own_rows, 0)
        copies["eb"] = net.send(eb.at[own_part], eb.at[own_part], place.sib)

    def embed_back(j):
        keep("embed", j, 0, dot(act[j], eb[...], 0, 0))

    cin = feat.shape[1]

    def stem_back(j):
        gain_sum = jnp.zeros((1, channels), F32)
        bias_total = jnp.zeros((1, channels), F32)
        for at, size in tile_rows:
            dz = dot(eb[at : at + size, :], embed[j], 1, 1) * dgs[j, at : at + size, :]
            dgs[j, at : at + size, :] = dz
            gain_sum = gain_sum + jnp.sum(dz * xhs[j, at : at + size, :], axis=0, keepdims=True)
            bias_total = bias_total + jnp.sum(dz, axis=0, keepdims=True)
        sm[5 + j : 6 + j, 0:channels] = gain_sum
        sm[5 + j : 6 + j, channels : 2 * channels] = bias_total
        gain = gvec[j, 0:1, :]
        count = 1.0 / (length * GROUP)
        mean_one = group_sum(bias_total * gain) * count
        mean_two = group_sum(gain_sum * gain) * count
        for at, size in tile_rows:
            part = dgs[j, at : at + size, :] * gain - valid_rows(at, size) * (
                mean_one + xhs[j, at : at + size, :] * mean_two
            )
            sg[j, at : at + size, :] = (part * gst[j, 0:1, :]).astype(BF16)
        average, scale = wstat[j, 0:1, :], wstat[j, 1:2, :]
        sum_one = jnp.zeros((1, channels), F32)
        sum_two = jnp.zeros((1, channels), F32)
        quarter = cin // 4
        for t in range(4):
            rows = slice(t * quarter, (t + 1) * quarter)
            grad = dot(feat[:, rows], sg[j], 0, 0)
            gtmp[rows, :] = grad
            xh = (stem[j, rows, :].astype(F32) - average) * scale
            sum_one = sum_one + jnp.sum(grad, axis=0, keepdims=True)
            sum_two = sum_two + jnp.sum(grad * xh, axis=0, keepdims=True)
        sum_one = sum_one * (1.0 / cin)
        sum_two = sum_two * (1.0 / cin)
        for t in range(4):
            rows = slice(t * quarter, (t + 1) * quarter)
            xh = (stem[j, rows, :].astype(F32) - average) * scale
            value = (gtmp[rows, :] - sum_one - xh * sum_two) * scale
            for i in range(2):
                lanes = slice(i * channels // 2, (i + 1) * channels // 2)
                keep("stem%d" % i, j, 2 * t, value[:, lanes])

    @task
    def stem_far():
        copies["eb"].wait_recv()
        embed_back(1)
        stem_back(1)

    @task
    def stem_own():
        embed_back(0)
        stem_back(0)
        small("core")

    @task
    def features_send():
        def product(start):
            rows = pl.ds(start, R)
            return dot(sg[0, rows, :], std[0], 1, 1) + dot(sg[1, rows, :], std[1], 1, 1)

        sbuf[...] = product(sib_rows)
        copies["feat"] = net.send(sbuf, rbuf, place.sib)
        copies["feat_own"] = product(own_rows)

    @task
    def features_sum():
        copies["feat"].wait_recv()
        net.sent(copies["feat"])
        sbuf[...] = copies["feat_own"] + rbuf[...]
        locals_left.append(net.local(sbuf, features_grad))

    small_at = {"core": place.sib}
    for name in place.bits:
        small_at[name] = place.partner(name)[1]
    small_order = tuple(small_at)

    def small(name):
        copies["small"] = net.send(sm, smr.at[small_order.index(name)], small_at[name])

    def small_step(i):
        copies["small"].wait_recv()
        net.sent(copies["small"])
        if small_order[i] in ("core", "x"):
            sm[0:4, :] = sm[0:4, :] + smr[i, 0:4, :]
            if small_order[i] == "x":
                sm[5:6, :] = sm[5:6, :] + smr[i, 6:7, :]
        else:
            sm[...] = sm[...] + smr[i]
        if i + 1 < len(small_order):
            small(small_order[i + 1])
        else:
            o_small[...] = sm[...]

    small_next = list(range(len(small_order)))
    for name in ORDER:
        if name in tasks:
            tasks.pop(name)()
        elif name == "+result":
            c_far[0] = net.send(xsend.at[0], xrecv.at[0], place.far)
        elif name[0] == "+":
            summed[name[1:]].start()
        elif name == "small":
            small_step(small_next.pop(0))
        else:
            summed[name].step()
    assert not tasks and not small_next
    for one in summed.values():
        one.step_all()
    for copy in locals_left:
        copy.wait()
    net.finish()


def finish(in_names, out_names, *refs):
    names = in_names + out_names
    r = dict(zip(names, refs))
    rest = refs[len(names) :]
    sems, passed, rest = rest[0], rest[1:3], rest[3:]
    held, made = rest[: len(GRADS)], rest[len(GRADS) :]
    made = dict(zip(("up", "down", "pout", "pin", "embed", "stem"), made))
    count = [0]
    going = []

    def move(src, dst):
        copy = pltpu.make_async_copy(src, dst, sems.at[count[0]])
        count[0] += 1
        copy.start()
        return copy

    order = ("up", "down", "stem0", "stem1", "embed", "pin0", "pin1", "pin2", "pout")
    held = dict(zip(GRADS, held))
    as_is = ("block_out", "features_grad")
    passing = [move(r["i_" + name], ref) for name, ref in zip(as_is, passed)]
    arriving = {name: move(r["i_" + name], held[name]) for name in order}
    small = r["i_small"]
    for i, name in enumerate(("g1", "b1", "g2", "b2", "ub")):
        r["o_" + name][...] = small[i, :]
    channels = r["o_gain"].shape[0]
    r["o_gain"][...] = small[5, 0:channels]
    r["o_shift"][...] = small[5, channels : 2 * channels]
    for name, ref, copy in zip(as_is, passed, passing):
        copy.wait()
        going.append(move(ref, r["o_" + name]))
    for name in order:
        arriving[name].wait()
        part = held[name]
        rows, columns = part.shape[1:]
        whole = name.rstrip("012")
        down = made[whole].shape[0] // rows
        for t in range(8):
            at = slice(t % down * rows, (t % down + 1) * rows)
            left = t // down * columns
            if whole in ("pin", "stem"):
                left += int(name[-1]) * made[whole].shape[1] // dict(pin=3, stem=2)[whole]
            made[whole][at, left : left + columns] = part[t].astype(F32)
            last = name not in ("pin0", "pin1", "stem0")
            if last and (t == 3 or t == 7) and whole in ("up", "down"):
                half = pl.ds(t // 4 * 4 * rows, 4 * rows)
                going.append(move(made[whole].at[half], r["o_" + whole].at[half]))
            elif last and t == 7:
                going.append(move(made[whole], r["o_" + whole]))
    for copy in going:
        copy.wait()


def body(
    features, stem_weight, group_gain, group_bias, embed_weight, first_gain, first_bias,
    project_in, project_out, second_gain, second_bias, up_weight, up_bias, down_weight,
    valid_mask, slot_slice, cotangent, *, dp,
):
    slots = slot_slice.shape[0]
    L = features.shape[0] // slots
    R = cotangent.shape[0]
    cin, channels = stem_weight.shape
    D = cotangent.shape[1]
    wide_in = project_in.shape[1]
    project_in = project_in.T
    out_rows = project_out.shape[0]
    hidden = up_weight.shape[1]
    heads = 2 * wide_in // (3 * HEAD_DIM)
    hbm = pl.BlockSpec(memory_space=pl.ANY)
    vmem = pl.BlockSpec(memory_space=pltpu.VMEM)
    smem = pl.BlockSpec(memory_space=pltpu.SMEM)
    in_specs = dict(
        features=hbm, stem_weight=hbm, group_gain=vmem, group_bias=vmem, embed_weight=hbm,
        first_gain=vmem, first_bias=vmem, project_in=hbm, project_out=hbm, second_gain=vmem,
        second_bias=vmem, up_weight=hbm, up_bias=vmem, down_weight=hbm, valid_mask=vmem,
        slot_slice=smem, cotangent=hbm,
    )
    parts = dict(
        up=(D // 8, hidden),
        down=(hidden // 8, D),
        pout=(out_rows // 4, D // 2),
        pin0=(wide_in // 4, D // 6),
        pin1=(wide_in // 4, D // 6),
        pin2=(wide_in // 4, D // 6),
        embed=(channels // 8, D),
        stem0=(cin // 8, channels // 2),
        stem1=(cin // 8, channels // 2),
    )
    outs = dict(
        block_out=((R, D), BF16, hbm),
        features_grad=((R, cin), F32, hbm),
        o_small=((8, D), F32, vmem),
    )
    for name in GRADS:
        outs["o_" + name] = ((2, 2, 2) + parts[name], BF16, hbm)
    scratch = dict(
        feat=((L, cin), BF16), stem=((2, cin, channels), BF16), std=((2, cin, channels), BF16),
        wstat=((2, 8, channels), F32), embed=((2, channels, D), BF16), pin=((2, wide_in, D), BF16),
        pout=((2, out_rows, D), BF16), up=((D, hidden), BF16), down=((hidden, D), BF16),
        gvec=((2, 8, channels), F32), xhs=((2, L, channels), F32), dgs=((2, L, channels), F32),
        act=((2, L, channels), BF16), gst=((2, 8, channels), F32),
        sbuf=((R, cin), F32), rbuf=((R, cin), F32), res1=((R, D), F32), xh1=((R, D), F32),
        rs1=((R, 1), F32), n1=((L, D), BF16), q=((heads, L, HEAD_DIM), BF16),
        k=((heads, L, HEAD_DIM), BF16), v=((heads, L, HEAD_DIM), BF16), probs=((heads, L, L), BF16),
        heads=((heads, L, HEAD_DIM), BF16), mixed=((L, heads * HEAD_DIM), BF16),
        res2=((R, D), F32), xh2=((R, D), F32), rs2=((R, 1), F32), n2=((4 * R, D), BF16),
        hid=((4 * R, hidden), BF16), branch=((4 * R, D), BF16), preg=((4 * R, hidden), BF16),
        own=((2, R, D), F32), csend=((2, 2, R, D), BF16),
        crecv=((2, 2, R, D), BF16), xsend=((2, R, D), BF16), xrecv=((2, R, D), BF16),
        mb=((L, D), BF16), pg=((2, L, wide_in), BF16),
        sg=((2, L, channels), BF16), gtmp=((cin, channels), F32),
    )
    for name in GRADS:
        size = dict.fromkeys(sorted(AWAY[name], key="xyab".index), 2)
        scratch["g_" + name] = (tuple(size.values()) + parts[name], BF16)
        for level, dim in enumerate(AWAY[name]):
            size[dim] = 1
            scratch["r%d_" % level + name] = (tuple(size.values()) + parts[name], BF16)
        scratch["p_" + name] = ((1, 1, 1) + parts[name], BF16)
    scratch.update(sm=((8, D), F32), smr=((5, 8, D), F32))
    copies = 128
    shapes = [pltpu.VMEM(*one) for one in scratch.values()]
    shapes += [pltpu.SemaphoreType.DMA((copies,)) for _ in range(2)]
    shapes += [pltpu.SemaphoreType.DMA((24,))]
    names = tuple(scratch) + ("send_sems", "recv_sems", "local_sems")
    results = pl.pallas_call(
        functools.partial(kernel, tuple(in_specs), tuple(outs), names),
        out_shape=[jax.ShapeDtypeStruct(shape, kind) for shape, kind, _ in outs.values()],
        in_specs=list(in_specs.values()),
        out_specs=[spec for _, _, spec in outs.values()],
        scratch_shapes=shapes,
        compiler_params=pltpu.CompilerParams(
            collective_id=0, has_side_effects=True, vmem_limit_bytes=62 * 2**20
        ),
        name="layer",
    )(
        features, stem_weight, group_gain, group_bias, embed_weight, first_gain, first_bias,
        project_in, project_out, second_gain, second_bias, up_weight, up_bias, down_weight,
        valid_mask, slot_slice, cotangent,
    )
    out = dict(zip(outs, results))

    wide = {name: out["o_" + name].reshape((8,) + parts[name]) for name in GRADS}
    small = out["o_small"]
    bit = NEAR
    if bit < dp:
        wide = {name: part.astype(F32) for name, part in wide.items()}
    while bit < dp:
        pairs = [(i, i ^ bit) for i in range(dp)]
        wide, small = jax.tree.map(
            lambda part: part + lax.ppermute(part, "dp", pairs), (wide, small)
        )
        bit *= 2

    inputs = {"i_" + name: wide[name] for name in GRADS}
    inputs.update(i_block_out=out["block_out"], i_features_grad=out["features_grad"], i_small=small)
    whole = dict(
        up=(D, hidden), down=(hidden, D), pout=(out_rows, D), pin=(wide_in, D),
        embed=(channels, D), stem=(cin, channels),
    )
    finals = dict(o_block_out=((R, D), BF16, hbm), o_features_grad=((R, cin), F32, hbm))
    for name, shape in whole.items():
        finals["o_" + name] = (shape, F32, hbm)
    for name in ("g1", "b1", "g2", "b2"):
        finals["o_" + name] = ((D,), F32, vmem)
    finals["o_ub"] = ((hidden,), F32, vmem)
    for name in ("gain", "shift"):
        finals["o_" + name] = ((channels,), F32, vmem)
    moved = pl.pallas_call(
        functools.partial(finish, tuple(inputs), tuple(finals)),
        out_shape=[jax.ShapeDtypeStruct(shape, kind) for shape, kind, _ in finals.values()],
        in_specs=[hbm] * (len(inputs) - 1) + [vmem],
        out_specs=[spec for _, _, spec in finals.values()],
        scratch_shapes=[pltpu.SemaphoreType.DMA((24,))]
        + [pltpu.VMEM((R, D), BF16), pltpu.VMEM((R, cin), F32)]
        + [pltpu.VMEM(wide[name].shape, wide[name].dtype) for name in GRADS]
        + [pltpu.VMEM(shape, F32) for shape in whole.values()],
        compiler_params=pltpu.CompilerParams(vmem_limit_bytes=62 * 2**20),
        name="finish",
    )(*inputs.values())
    done = dict(zip(finals, moved))
    return (
        done["o_block_out"],
        done["o_features_grad"],
        done["o_stem"],
        done["o_gain"],
        done["o_shift"],
        done["o_embed"],
        done["o_g1"],
        done["o_b1"],
        done["o_pin"].T,
        done["o_pout"],
        done["o_g2"],
        done["o_b2"],
        done["o_up"],
        done["o_ub"],
        done["o_down"],
    )


def solution(mesh):
    return jax.shard_map(
        functools.partial(body, dp=mesh.shape["dp"]),
        mesh=mesh,
        in_specs=(
            P("dp", None), P(None, "mp"), P("mp"), P("mp"), P("mp", None), P(), P(),
            P(None, "mp"), P("mp", None), P(), P(), P(None, "mp"), P("mp"), P("mp", None),
            P(), P("dp"), P(("dp", "mp"), None),
        ),
        out_specs=(
            P(("dp", "mp"), None), P(("dp", "mp"), None), P(None, "mp"), P("mp"), P("mp"),
            P("mp", None), P(), P(), P(None, "mp"), P("mp", None), P(), P(), P(None, "mp"),
            P("mp"), P("mp", None),
        ),
        check_vma=False,
    )
```

```python
import functools
import itertools

import jax
import jax.numpy as jnp
from jax import lax
from jax.experimental import pallas as pl
from jax.experimental.pallas import tpu as pltpu
from jax.sharding import PartitionSpec as P

MESH = pl.DeviceIdType.MESH
F32 = jnp.float32
BF16 = jnp.bfloat16
HEAD_DIM = 64
GROUP = 32
NEAR = 8


def dot(left, right, left_dim=1, right_dim=0, precision=None):
    return lax.dot_general(
        left,
        right,
        (((left_dim,), (right_dim,)), ((), ())),
        precision=precision,
        preferred_element_type=F32,
    )


def gelu_parts(z):
    cdf = 0.5 + 0.5 * lax.erf(z * 0.7071067811865476)
    return z * cdf, cdf + z * (jnp.exp(-0.5 * z * z) * 0.3989422804014327)


class Net:
    def __init__(self, place, send_sems, recv_sems, local_sems):
        self.place = place
        self.send_sems, self.recv_sems, self.local_sems = send_sems, recv_sems, local_sems
        self.count, self.local_count, self.unsent = 0, 0, []

    def by(self, who, action):
        if who is None:
            action()
        else:
            pl.when(self.place.inner if who else jnp.logical_not(self.place.inner))(action)

    def plan(self, src, dst, device, who=None):
        copy = pltpu.make_async_remote_copy(
            src_ref=src,
            dst_ref=dst,
            send_sem=self.send_sems.at[self.count],
            recv_sem=self.recv_sems.at[self.count],
            device_id=device,
            device_id_type=MESH,
        )
        self.count += 1
        self.unsent.append((copy, who))
        return copy

    def send(self, src, dst, device, who=None):
        copy = self.plan(src, dst, device, who)
        self.by(who, copy.start)
        return copy

    def sent(self, copy):
        self.unsent = [one for one in self.unsent if one[0] is not copy]
        copy.wait_send()

    def local(self, src, dst, who=None):
        copy = pltpu.make_async_copy(src, dst, self.local_sems.at[self.local_count])
        self.local_count += 1
        self.by(who, copy.start)
        return copy

    def finish(self):
        for copy, who in self.unsent:
            self.by(who, copy.wait_send)


class Summed:
    def __init__(self, net, place, away, back, grad, arrive, out):
        self.net, self.place, self.away, self.back = net, place, away, back
        self.grad, self.arrive, self.out = grad, arrive, out
        self.dims = "xyb"[3 - (len(grad.shape) - 2) :]
        self.fixed = {}
        self.level, self.gathered = 0, None

    def index(self, dims, **more):
        fixed = {**self.fixed, **more}
        return tuple(pl.ds(fixed[dim], 1) if dim in fixed else pl.ds(0, 2) for dim in dims)

    def start(self):
        dim = self.away[self.level]
        bit, partner = self.place.partner(dim)
        inner_only = "a" in self.away[: self.level]
        if dim == "a":
            give, who = self.index(self.dims), False
        else:
            give, who = self.index(self.dims, **{dim: 1 - bit}), True if inner_only else None
            self.fixed[dim] = bit
        self.copy = self.net.send(self.grad.at[give], self.arrive[self.level], partner, who)

    def add(self, arrived):
        for at in itertools.product((0, 1), repeat=len(self.dims)):
            here = dict(zip(self.dims, at))
            if any(here[dim] for dim in self.fixed):
                continue
            where = tuple(self.fixed.get(dim, here[dim]) for dim in self.dims)
            value = self.grad[where].astype(F32) + arrived[at].astype(F32)
            self.grad[where] = value.astype(BF16)

    def held(self):
        return self.out.at[self.index("yb")]

    def share(self):
        dim = self.back[len(self.gathered)]
        _, partner = self.place.partner(dim)
        source = self.held()
        if not self.gathered:
            at = self.index("yb")
            source = self.grad.at[(0,) + at if "x" in self.dims else at]
        self.copy = self.net.send(source, self.held(), partner, True)
        if dim == "a" and len(self.gathered) < 2:
            _, partner = self.place.partner(self.back[2])
            self.last = self.net.plan(self.held(), self.held(), partner)
            self.net.by(True, self.last.start)

    def step(self):
        copy = self.copy
        if self.gathered is None:
            arrived = self.arrive[self.level]

            def take():
                copy.wait_recv()
                self.add(arrived)

            self.net.by(True if "a" in self.away[: self.level + 1] else None, take)
            self.level += 1
            if self.level < len(self.away):
                self.start()
                return
            self.fixed.pop("x", None)
            self.gathered = []
            at = self.index("yb")
            source = self.grad.at[(0,) + at if "x" in self.dims else at]
            self.own = self.net.local(source, self.held(), True)
            self.share()
            return
        dim = self.back[len(self.gathered)]
        if dim == "a":
            self.net.by(False, copy.wait_recv)
        elif "a" in self.gathered:
            copy.wait_recv()
        else:
            self.net.by(True, copy.wait_recv)
        if not self.gathered:
            self.net.by(True, self.own.wait)
        self.gathered.append(dim)
        self.fixed.pop(dim, None)
        if len(self.gathered) == 3:
            self.copy = None
        elif dim == "a":
            self.copy = self.last
            self.net.by(False, self.copy.start)
        else:
            self.share()

    def step_all(self):
        while self.copy is not None:
            self.step()


class Place:
    def __init__(self):
        self.d = lax.axis_index("dp")
        self.m = lax.axis_index("mp")
        self.x = lax.div(self.m, 2)
        self.c = lax.rem(self.m, 2)
        self.y = lax.rem(self.d, 2)
        self.zi = lax.div(lax.rem(self.d, NEAR), 2)
        self.sib_m = self.m + 1 - 2 * self.c
        self.far_m = lax.rem(self.m + 2, 4)
        self.far_sib_m = lax.rem(self.sib_m + 2, 4)
        self.sib = (self.d, self.sib_m)
        self.far = (self.d, self.far_m)
        self.y_device = (self.d + 1 - 2 * self.y, self.m)
        self.inner = jnp.logical_or(self.zi == 1, self.zi == 2)
        self.bits = {
            "y": (self.y, 1),
            "a": (lax.rem(self.zi, 2), 2),
            "b": (lax.div(self.zi, 2), 2),
            "w": (lax.div(self.zi, 2), 4),
        }

    def partner(self, name):
        if name == "x":
            return 0, self.far
        bit, stride = self.bits[name]
        return bit, (self.d + stride - 2 * stride * bit, self.m)


GRADS = ("up0", "up1", "down0", "down1", "pout", "pin0", "pin1", "pin2", "embed", "stem0", "stem1")
UP0, UP1, DOWN0, DOWN1, POUT, PIN0, PIN1, PIN2, EMBED, STEM0, STEM1, SMALL = range(12)
(NORM2, RESULT, MIXED_BACK, HEADS_FAR, HEADS_OWN, NORM1_SEND, NORM1, STEM_FAR, STEM_OWN, FEATURES_SEND,
 FEATURES_SUM) = range(12, 23)
KINDS = dict(g="grad", o="out", r0="arrive0", r1="arrive1", r2="arrive2", r3="arrive3")
AWAY = dict(
    down0="yab",
    down1="aby",
    up0="yab",
    up1="yab",
    pout="xaby",
    pin0="xaby",
    pin1="yxab",
    pin2="yxab",
    embed="xaby",
    stem0="xaby",
    stem1="xyab",
)
BACK = dict(
    down0="bay",
    down1="yba",
    up0="bay",
    up1="bay",
    pout="bay",
    pin0="bay",
    pin1="bay",
    pin2="bya",
    embed="bay",
    stem0="bay",
    stem1="bay",
)
ORDER = (
    NORM2, ~RESULT, DOWN0, MIXED_BACK, HEADS_FAR, ~POUT, DOWN1, UP0, HEADS_OWN, ~PIN1, DOWN0, UP1,
    NORM1_SEND, DOWN1, UP0, NORM1, ~PIN0, ~PIN2, POUT, DOWN0, STEM_FAR, ~STEM0, ~EMBED, PIN1, UP1,
    UP0, STEM_OWN, ~STEM1, DOWN1, DOWN0, FEATURES_SEND, SMALL, PIN0, POUT, UP1, FEATURES_SUM, PIN2,
    RESULT, UP0, STEM0, DOWN1, PIN0, POUT, DOWN0, UP1, STEM0, EMBED, UP0, PIN1, DOWN0, DOWN1, POUT,
    PIN0, UP1, STEM1, SMALL, EMBED, STEM0, UP0, POUT, PIN2, PIN1, PIN0, UP1, PIN2, EMBED, PIN1,
    STEM1, SMALL, DOWN1, STEM0, PIN0, PIN2, POUT, PIN1, EMBED, STEM0, SMALL, STEM1, PIN0, PIN2,
    POUT, PIN1, EMBED, STEM1, STEM0, PIN0, SMALL, STEM1, PIN1, PIN2, EMBED, STEM0, STEM1, EMBED,
    STEM1, PIN2,
)


def kernel(in_names, out_names, scratch_names, *refs):
    names = in_names + out_names + scratch_names
    r = dict(zip(names, refs))
    sums = {name: {} for name in GRADS}
    for name in names:
        kind, _, which = name.partition("_")
        if which in sums and kind in KINDS:
            sums[which][KINDS[kind]] = r.pop(name)
    for refs in sums.values():
        refs["arrive"] = [refs.pop(kind) for kind in sorted(refs) if kind.startswith("arrive")]
    run(sums=sums, **r)


def run(
    features, stem_weight, group_gain, group_bias, embed_weight, first_gain, first_bias,
    project_in, project_out, second_gain, second_bias, up_weight, up_bias, down_weight,
    valid_mask, slot_slice, cotangent,
    block_out, features_grad, o_small,
    feat, stem, std, wstat, embed, pin, pout, up, down, gvec, xhs, dgs, act, gst,
    sbuf, rbuf, res1, xh1, rs1, n1, q, k, v, probs, heads, mixed, res2, xh2, rs2,
    n2, hid, branch, preg, own, csend, crecv, xsend, xrecv, mb, pg,
    sm, smr, send_sems, recv_sems, local_sems, sums,
):
    place = Place()
    net = Net(place, send_sems, recv_sems, local_sems)
    x, c = place.x, place.c
    R = cotangent.shape[0]
    L = feat.shape[0]
    D = up.shape[0]
    own_rows = pl.multiple_of(c * R, 16)
    sib_rows = pl.multiple_of((1 - c) * R, 16)

    def block(m):
        return pl.ds(pl.multiple_of(m * R, 16), R)

    barrier = pltpu.get_barrier_semaphore()
    peers = [place.sib] + [place.partner(name)[1] for name in "xyaw"]
    for peer in peers:
        pl.semaphore_signal(barrier, inc=1, device_id=peer, device_id_type=MESH)

    def greet():
        peer = place.partner("b")[1]
        pl.semaphore_signal(barrier, inc=1, device_id=peer, device_id_type=MESH)

    net.by(True, greet)
    l_stem = net.local(stem_weight, stem.at[0])
    l_feat = net.local(features.at[pl.ds(pl.multiple_of(x * L, 16), L)], feat)
    l_embed = net.local(embed_weight, embed.at[0])
    l_cot = net.local(cotangent, branch.at[block(place.m)])
    l_pin = net.local(project_in, pin.at[0])
    l_pout = net.local(project_out, pout.at[0])
    l_up = net.local(up_weight, up)
    l_down = net.local(down_weight, down)
    gvec[0, 0:1, :] = group_gain[...].reshape(1, -1)
    gvec[0, 1:2, :] = group_bias[...].reshape(1, -1)
    pl.semaphore_wait(barrier, len(peers) + place.inner.astype(jnp.int32))

    c_gvec = net.send(gvec.at[0], gvec.at[1], place.far)

    def halves(weight, kept, pieces):
        rows = weight.shape[0] // pieces // 2
        for t in range(pieces):
            at = pl.ds(pl.multiple_of((2 * t + place.y) * rows, 16), rows)
            yield kept.at[1, at], net.send(weight.at[at], kept.at[1, at], place.far)

    stem_half = list(halves(stem_weight, stem, 2))
    embed_half = list(halves(embed_weight, embed, 1))
    pin_half = list(halves(project_in, pin, pin.shape[1] // (3 * HEAD_DIM)))
    pout_half = list(halves(project_out, pout, 1))
    c_cot = [
        net.send(cotangent, branch.at[block(place.m)], device) for device in (place.far, place.sib)
    ]

    def pass_on(half):
        ref, copy = half
        copy.wait_recv()
        return net.send(ref, ref, place.y_device)

    slices = valid_mask.shape[0]
    lengths = jnp.sum(valid_mask[...].astype(F32), axis=1, keepdims=True)
    mine = lax.broadcasted_iota(jnp.int32, (slices, 1), 0) == slot_slice[x]
    length = jnp.sum(jnp.where(mine, lengths, 0.0), axis=0, keepdims=True)

    def valid_rows(start, count):
        at = (lax.broadcasted_iota(jnp.int32, (count, 1), 0) + start).astype(F32)
        return jnp.where(at < length, 1.0, 0.0)

    key_valid = jnp.where(
        lax.broadcasted_iota(jnp.int32, (1, L), 1).astype(F32) < length, 1.0, 0.0
    )
    score_scale = HEAD_DIM ** (-0.5)
    key_scale = key_valid * score_scale
    key_shift = (key_valid - 1.0) * 1e9

    channels = stem.shape[2]
    same = (
        lax.div(lax.broadcasted_iota(jnp.int32, (channels, channels), 0), GROUP)
        == lax.div(lax.broadcasted_iota(jnp.int32, (channels, channels), 1), GROUP)
    )
    same = jnp.where(same, 1.0, 0.0)

    def group_sum(values):
        wide = jnp.broadcast_to(values, (8, channels))
        return dot(wide, same, precision=lax.Precision.HIGHEST)[0:1]

    def standardize(j):
        w = stem[j].astype(F32)
        average = jnp.sum(w, axis=0, keepdims=True) * (1.0 / w.shape[0])
        w = w - average
        scale = lax.rsqrt(jnp.sum(w * w, axis=0, keepdims=True) * (1.0 / w.shape[0]) + 1e-5)
        std[j] = (w * scale).astype(BF16)
        wstat[j, 0:1, :] = average
        wstat[j, 1:2, :] = scale

    tile_rows = [(t * R, R) for t in range(L // R)]

    def stem_forward(j):
        count = 1.0 / (length * GROUP)
        total = jnp.zeros((1, channels), F32)
        for at, size in tile_rows:
            s = dot(feat[at : at + size, :], std[j])
            xhs[j, at : at + size, :] = s
            total = total + jnp.sum(s * valid_rows(at, size), axis=0, keepdims=True)
        average = group_sum(total) * count
        total = jnp.zeros((1, channels), F32)
        for at, size in tile_rows:
            s = xhs[j, at : at + size, :] - average
            total = total + jnp.sum(s * s * valid_rows(at, size), axis=0, keepdims=True)
        scale = lax.rsqrt(group_sum(total) * count + 1e-5)
        gst[j, 0:1, :] = scale
        for at, size in tile_rows:
            xh = (xhs[j, at : at + size, :] - average) * scale
            xhs[j, at : at + size, :] = xh
            value, slope = gelu_parts(xh * gvec[j, 0:1, :] + gvec[j, 1:2, :])
            act[j, at : at + size, :] = value.astype(BF16)
            dgs[j, at : at + size, :] = slope

    l_stem.wait()
    standardize(0)
    c_stem = [pass_on(stem_half[0])]
    l_feat.wait()
    stem_forward(0)
    c_stem.append(pass_on(stem_half[1]))
    c_gvec.wait_recv()
    c_embed = pass_on(embed_half[0])
    for copy in c_stem:
        copy.wait_recv()
    standardize(1)
    stem_forward(1)
    l_embed.wait()
    c_embed.wait_recv()

    def core_sum(product):
        width = pl.ds(0, D)
        sbuf[:, width] = product(sib_rows)
        copy = net.send(sbuf.at[:, width], rbuf.at[:, width], place.sib)
        mine = product(own_rows)
        copy.wait_recv()
        net.sent(copy)
        return mine

    def embed_product(start):
        rows = pl.ds(start, R)
        return dot(act[0, rows, :], embed[0]) + dot(act[1, rows, :], embed[1])

    res1[...] = core_sum(embed_product)

    step = R // 3

    def layer_norm(res, other, add, gain, bias, xh_ref, scale_ref, out_ref, out_start):
        gain, bias = gain[...].reshape(1, -1), bias[...].reshape(1, -1)
        for t in range(3):
            rows = slice(t * step, (t + 1) * step)
            value = res[rows, :] + other[rows, 0:D]
            if add is not None:
                value = value + add[rows, :]
            res[rows, :] = value
            average = jnp.sum(value, axis=1, keepdims=True) * (1.0 / D)
            value = value - average
            scale = lax.rsqrt(jnp.sum(value * value, axis=1, keepdims=True) * (1.0 / D) + 1e-6)
            xh = value * scale
            xh_ref[rows, :] = xh
            scale_ref[rows, :] = scale
            out_ref[pl.ds(out_start + t * step, step), :] = (xh * gain + bias).astype(BF16)

    c_pin = [pass_on(pin_half[0])]
    layer_norm(res1, rbuf, None, first_gain, first_bias, xh1, rs1, n1, own_rows)
    c_n1 = net.send(n1.at[pl.ds(own_rows, R)], n1.at[pl.ds(own_rows, R)], place.sib)
    l_pin.wait()
    c_n1.wait_recv()
    c_pin.append(pass_on(pin_half[1]))

    per_shard = pin.shape[1] // (3 * HEAD_DIM)

    def attend(j, i):
        h = per_shard * j + i
        width = 3 * HEAD_DIM
        for at, size in tile_rows:
            weight = pin[j, i * width : (i + 1) * width, :]
            packed = dot(n1[at : at + size, :], weight, 1, 1).astype(BF16)
            for t, ref in enumerate((q, k, v)):
                ref[h, at : at + size, :] = packed[:, t * HEAD_DIM : (t + 1) * HEAD_DIM]
        for at, size in tile_rows:
            s = dot(q[h, at : at + size, :], k[h], 1, 1) * key_scale + key_shift
            s = jnp.exp(s - jnp.max(s, axis=1, keepdims=True))
            p = (s * (1.0 / jnp.sum(s, axis=1, keepdims=True))).astype(BF16)
            probs[h, at : at + size, :] = p
            heads[h, at : at + size, :] = dot(p, v[h]).astype(BF16)

    for i in range(per_shard):
        attend(0, i)
        if i + 2 < per_shard:
            c_pin.append(pass_on(pin_half[i + 2]))
    c_pout = pass_on(pout_half[0])
    for i in range(per_shard):
        c_pin[i].wait_recv()
        attend(1, i)

    def side_by_side(pieces, store):
        at = 0
        while at < len(pieces):
            pair = pieces[at : at + 2]
            value = pair[0] if len(pair) == 1 else jnp.concatenate(pair, axis=1)
            store(slice(at * HEAD_DIM, at * HEAD_DIM + value.shape[1]), value)
            at += 2

    def store_mixed(lanes, value):
        mixed[:, lanes] = value

    side_by_side([heads[h] for h in range(2 * per_shard)], store_mixed)
    l_pout.wait()
    c_pout.wait_recv()
    out_width = pout.shape[1]

    def out_product(start):
        rows = pl.ds(start, R)
        return dot(mixed[rows, :], pout[...].reshape(-1, D))

    res2[...] = core_sum(out_product)
    layer_norm(
        res2, rbuf, res1, second_gain, second_bias, xh2, rs2, n2, pl.multiple_of(place.m * R, 16)
    )
    mine = block(place.m)
    c_n2 = [net.send(n2.at[mine], n2.at[mine], device) for device in (place.far, place.sib)]

    l_cot.wait()
    l_up.wait()
    l_down.wait()
    bias_sum = []

    def feed(m):
        rows = block(m)
        pre = dot(n2[rows, :], up[...]) + up_bias[...].reshape(1, -1)
        value, slope = gelu_parts(pre)
        hid[rows, :] = value.astype(BF16)
        grad = (dot(branch[rows, :], down[...], 1, 1) * slope).astype(BF16)
        preg[rows, :] = grad
        bias_sum.append(jnp.sum(grad.astype(F32), axis=0, keepdims=True))

    def back_part(m):
        return dot(preg[block(m), :], up[...], 1, 1)

    def out_part(m):
        return dot(hid[block(m), :], down[...])

    def mask_branch(m, own_slot):
        rows = block(m)
        start = lax.rem(m, 2) * R
        branch[rows, :] = (
            branch[rows, :].astype(F32) * valid_of(own_slot, start)
        ).astype(BF16)

    mine_far = lax.broadcasted_iota(jnp.int32, (slices, 1), 0) == slot_slice[1 - x]
    far_length = jnp.sum(jnp.where(mine_far, lengths, 0.0), axis=0, keepdims=True)

    def valid_of(own_slot, start):
        at = (lax.broadcasted_iota(jnp.int32, (R, 1), 0) + start).astype(F32)
        return jnp.where(at < (length if own_slot else far_length), 1.0, 0.0)

    c_cot[0].wait_recv()
    f_rows = block(place.far_m)
    c_cot_fwd = net.send(branch.at[f_rows], branch.at[f_rows], place.sib)
    mask_done = []

    mask_branch(place.m, True)
    feed(place.m)
    own[1] = back_part(place.m)
    c_cot[1].wait_recv()
    c_n2[1].wait_recv()
    mask_branch(place.sib_m, True)
    feed(place.sib_m)
    csend[1, 0] = back_part(place.sib_m).astype(BF16)
    c_core = {}
    c_core[1, 0] = net.send(csend.at[1, 0], crecv.at[1, 0], place.sib)
    c_n2[0].wait_recv()
    c_n2_fwd = net.send(n2.at[f_rows], n2.at[f_rows], place.sib)
    csend[0, 0] = out_part(place.sib_m).astype(BF16)
    c_core[0, 0] = net.send(csend.at[0, 0], crecv.at[0, 0], place.sib)
    own[0] = out_part(place.m)
    c_cot_fwd.wait_recv()
    c_n2_fwd.wait_recv()
    mask_branch(place.far_sib_m, False)
    feed(place.far_sib_m)
    csend[1, 1] = back_part(place.far_sib_m).astype(BF16)
    c_core[1, 1] = net.send(csend.at[1, 1], crecv.at[1, 1], place.sib)
    net.sent(c_cot_fwd)
    mask_branch(place.far_m, False)
    feed(place.far_m)
    sbuf[:, 0:D] = back_part(place.far_m)
    c_core[1, 1].wait_recv()
    xsend[1] = (sbuf[:, 0:D] + crecv[1, 1].astype(F32)).astype(BF16)
    c_far = {}
    c_far[1] = net.send(xsend.at[1], xrecv.at[1], place.far)

    def result_send():
        csend[0, 1] = out_part(place.far_sib_m).astype(BF16)
        c_core[0, 1] = net.send(csend.at[0, 1], crecv.at[0, 1], place.sib)
        sbuf[:, 0:D] = out_part(place.far_m)
        c_core[0, 1].wait_recv()
        xsend[0] = (sbuf[:, 0:D] + crecv[0, 1].astype(F32)).astype(BF16)
        c_far[0] = net.send(xsend.at[0], xrecv.at[0], place.far)

    summed = {name: Summed(net, place, AWAY[name], BACK[name], **sums[name]) for name in GRADS}

    def keep(name, slot, at, value):
        ref = sums[name]["grad"]
        rows = ref.shape[-2]
        for t in range(value.shape[0] // rows):
            part = (at + t) // 2, (at + t) % 2
            ref[part if slot is None else (slot,) + part] = value[
                t * rows : (t + 1) * rows
            ].astype(BF16)

    half = D // 2
    for i, name in enumerate(("down0", "down1")):
        keep(name, None, 0, dot(hid[:, i * half : (i + 1) * half], branch[...], 0, 0))
        summed[name].start()
    for i, name in enumerate(("up0", "up1")):
        keep(name, None, 0, dot(n2[:, i * half : (i + 1) * half], preg[...], 0, 0))
        summed[name].start()
    sm[...] = jnp.zeros_like(sm)
    sm[4:5, :] = bias_sum[0] + bias_sum[1] + bias_sum[2] + bias_sum[3]

    def norm_back(grad_of, gain, xh_ref, scale_ref, kept, out_ref, out_start, row):
        gain = gain[...].reshape(1, -1)
        gain_sum = jnp.zeros((1, D), F32)
        bias_total = jnp.zeros((1, D), F32)
        for t in range(3):
            rows = slice(t * step, (t + 1) * step)
            dy, through = grad_of(rows)
            xh = xh_ref[rows, :]
            gain_sum = gain_sum + jnp.sum(dy * xh, axis=0, keepdims=True)
            bias_total = bias_total + jnp.sum(dy, axis=0, keepdims=True)
            dy = dy * gain
            mean_one = jnp.sum(dy, axis=1, keepdims=True) * (1.0 / D)
            mean_two = jnp.sum(dy * xh, axis=1, keepdims=True) * (1.0 / D)
            dx = through + scale_ref[rows, :] * (dy - mean_one - xh * mean_two)
            if kept is not None:
                kept[rows, :] = dx
            out_ref[pl.ds(out_start + t * step, step), :] = dx.astype(BF16)
        sm[row : row + 1, :] = gain_sum
        sm[row + 1 : row + 2, :] = bias_total

    own_part = pl.ds(own_rows, R)
    sg2, eb, sg = res1, mb, act
    copies = {}
    locals_left = []
    tasks = {}

    def task(number):
        def enter(function):
            tasks[number] = function

        return enter

    @task(NORM2)
    def norm2():
        c_core[1, 0].wait_recv()
        c_far[1].wait_recv()

        def grad_of(rows):
            dy = own[1, rows, :] + crecv[1, 0, rows, :].astype(F32) + xrecv[1, rows, :].astype(F32)
            at = pl.ds(pl.multiple_of(place.m * R, 16) + rows.start, step)
            return dy, branch[at, :].astype(F32)

        norm_back(grad_of, second_gain, xh2, rs2, sg2, mb, own_rows, 2)
        copies["mb"] = net.send(mb.at[own_part], mb.at[own_part], place.sib)

    @task(RESULT)
    def result():
        c_core[0, 0].wait_recv()
        c_far[0].wait_recv()
        net.sent(c_core[0, 0])
        for t in range(3):
            rows = slice(t * step, (t + 1) * step)
            value = (
                res2[rows, :]
                + own[0, rows, :]
                + crecv[0, 0, rows, :].astype(F32)
                + xrecv[0, rows, :].astype(F32)
            )
            csend[0, 0, rows, :] = (value * valid_rows(own_rows + t * step, step)).astype(BF16)
        locals_left.append(net.local(csend.at[0, 0], block_out))

    @task(MIXED_BACK)
    def mixed_back():
        copies["mb"].wait_recv()
        value = dot(mixed[...], mb[...], 0, 0)
        shard = pout.shape[1]
        for j in range(2):
            rows = value[j * shard : (j + 1) * shard]
            for i in range(2):
                keep("pout", j, 2 * i, rows[:, i * half : (i + 1) * half])
        for at, size in tile_rows:
            value = dot(mb[at : at + size, :], pout[...].reshape(-1, D), 1, 1).astype(BF16)
            for h in range(2 * per_shard):
                heads[h, at : at + size, :] = value[:, h * HEAD_DIM : (h + 1) * HEAD_DIM]

    def head_back(h, carry):
        p = probs[h]
        dp = dot(heads[h], v[h], 1, 1)
        v[h] = dot(p, heads[h], 0, 0).astype(BF16)
        p = p.astype(F32)
        ds = (p * (dp - jnp.sum(p * dp, axis=1, keepdims=True))).astype(BF16)
        dq = (dot(ds, k[h]) * score_scale).astype(BF16)
        k[h] = (dot(ds, q[h], 0, 0) * score_scale).astype(BF16)
        q[h] = dq
        return carry

    def pin_back(j):
        lax.fori_loop(per_shard * j, per_shard * (j + 1), head_back, 0)

        def store_pg(lanes, value):
            pg[j, :, lanes] = value

        pieces = [ref[per_shard * j + h] for h in range(per_shard) for ref in (q, k, v)]
        side_by_side(pieces, store_pg)
        value = dot(pg[j], n1[...], 0, 0)
        wide = D // 6
        for i in range(6):
            keep("pin%d" % (i // 2), j, 2 * (i % 2), value[:, i * wide : (i + 1) * wide])

    @task(HEADS_FAR)
    def heads_far():
        pin_back(1)

    @task(HEADS_OWN)
    def heads_own():
        pin_back(0)

    @task(NORM1_SEND)
    def norm1_send():
        def product(start):
            rows = pl.ds(start, R)
            return dot(pg[0, rows, :], pin[0]) + dot(pg[1, rows, :], pin[1])

        width = pl.ds(0, D)
        sbuf[:, width] = product(sib_rows)
        copies["n1"] = net.send(sbuf.at[:, width], rbuf.at[:, width], place.sib)
        xh2[...] = product(own_rows)

    @task(NORM1)
    def norm1():
        copies["n1"].wait_recv()
        net.sent(copies["n1"])

        def grad_of(rows):
            return xh2[rows, :] + rbuf[rows, 0:D], sg2[rows, :]

        net.sent(copies["mb"])
        norm_back(grad_of, first_gain, xh1, rs1, None, eb, own_rows, 0)
        copies["eb"] = net.send(eb.at[own_part], eb.at[own_part], place.sib)

    def embed_back(j):
        keep("embed", j, 0, dot(act[j], eb[...], 0, 0))

    cin = feat.shape[1]
    square = pl.ds(0, cin // 4), pl.ds(0, channels)
    spares = [ref.at[square] for ref in (xh1, xh2, res1, own.at[1])]

    def stem_back(j):
        gain_sum = jnp.zeros((1, channels), F32)
        bias_total = jnp.zeros((1, channels), F32)
        for at, size in tile_rows:
            dz = dot(eb[at : at + size, :], embed[j], 1, 1) * dgs[j, at : at + size, :]
            dgs[j, at : at + size, :] = dz
            gain_sum = gain_sum + jnp.sum(dz * xhs[j, at : at + size, :], axis=0, keepdims=True)
            bias_total = bias_total + jnp.sum(dz, axis=0, keepdims=True)
        sm[5 + j : 6 + j, 0:channels] = gain_sum
        sm[5 + j : 6 + j, channels : 2 * channels] = bias_total
        gain = gvec[j, 0:1, :]
        count = 1.0 / (length * GROUP)
        mean_one = group_sum(bias_total * gain) * count
        mean_two = group_sum(gain_sum * gain) * count
        for at, size in tile_rows:
            part = dgs[j, at : at + size, :] * gain - valid_rows(at, size) * (
                mean_one + xhs[j, at : at + size, :] * mean_two
            )
            sg[j, at : at + size, :] = (part * gst[j, 0:1, :]).astype(BF16)
        average, scale = wstat[j, 0:1, :], wstat[j, 1:2, :]
        sum_one = jnp.zeros((1, channels), F32)
        sum_two = jnp.zeros((1, channels), F32)
        quarter = cin // 4
        for t in range(4):
            rows = slice(t * quarter, (t + 1) * quarter)
            grad = dot(feat[:, rows], sg[j], 0, 0)
            spare = spares[t]
            spare[...] = grad
            xh = (stem[j, rows, :].astype(F32) - average) * scale
            sum_one = sum_one + jnp.sum(grad, axis=0, keepdims=True)
            sum_two = sum_two + jnp.sum(grad * xh, axis=0, keepdims=True)
        sum_one = sum_one * (1.0 / cin)
        sum_two = sum_two * (1.0 / cin)
        for t in range(4):
            rows = slice(t * quarter, (t + 1) * quarter)
            xh = (stem[j, rows, :].astype(F32) - average) * scale
            value = (spares[t][...] - sum_one - xh * sum_two) * scale
            for i in range(2):
                lanes = slice(i * channels // 2, (i + 1) * channels // 2)
                keep("stem%d" % i, j, t, value[:, lanes])

    @task(STEM_FAR)
    def stem_far():
        copies["eb"].wait_recv()
        embed_back(1)
        stem_back(1)

    @task(STEM_OWN)
    def stem_own():
        embed_back(0)
        stem_back(0)
        small("core")

    def feature_product(start):
        rows = pl.ds(start, R)
        return dot(sg[0, rows, :], std[0], 1, 1) + dot(sg[1, rows, :], std[1], 1, 1)

    @task(FEATURES_SEND)
    def features_send():
        sbuf[...] = feature_product(sib_rows)
        copies["feat"] = net.send(sbuf, rbuf, place.sib)

    @task(FEATURES_SUM)
    def features_sum():
        copies["feat"].wait_recv()
        net.sent(copies["feat"])
        sbuf[...] = feature_product(own_rows) + rbuf[...]
        locals_left.append(net.local(sbuf, features_grad))

    small_at = {"core": place.sib}
    for name in "xyaw":
        small_at[name] = place.partner(name)[1]
    small_order = tuple(small_at)

    def small(name):
        copies["small"] = net.send(sm, smr.at[small_order.index(name)], small_at[name])

    def small_step(i):
        copies["small"].wait_recv()
        net.sent(copies["small"])
        if small_order[i] in ("core", "x"):
            sm[0:4, :] = sm[0:4, :] + smr[i, 0:4, :]
            if small_order[i] == "x":
                sm[5:6, :] = sm[5:6, :] + smr[i, 6:7, :]
        else:
            sm[...] = sm[...] + smr[i]
        if i + 1 < len(small_order):
            small(small_order[i + 1])
        else:
            o_small[...] = sm[...]

    small_next = list(range(len(small_order)))
    for what in ORDER:
        if what in tasks:
            tasks.pop(what)()
        elif what == SMALL:
            small_step(small_next.pop(0))
        elif what == ~RESULT:
            result_send()
        elif what < 0:
            summed[GRADS[~what]].start()
        else:
            summed[GRADS[what]].step()
    assert not tasks and not small_next
    for one in summed.values():
        one.step_all()
    for copy in locals_left:
        copy.wait()
    net.finish()


def finish(in_names, out_names, *refs):
    names = in_names + out_names
    r = dict(zip(names, refs))
    rest = refs[len(names) :]
    sems, passed, rest = rest[0], rest[1:3], rest[3:]
    held, made = rest[: len(GRADS)], rest[len(GRADS) :]
    made = dict(zip(("up", "down", "pout", "pin", "embed", "stem"), made))
    count = [0]
    going = []

    def move(src, dst):
        copy = pltpu.make_async_copy(src, dst, sems.at[count[0]])
        count[0] += 1
        copy.start()
        return copy

    order = GRADS
    held = dict(zip(GRADS, held))
    as_is = ("block_out", "features_grad")
    passing = [move(r["i_" + name], ref) for name, ref in zip(as_is, passed)]
    arriving = {name: move(r["i_" + name], held[name]) for name in order}
    small = r["i_small"]
    for i, name in enumerate(("g1", "b1", "g2", "b2", "ub")):
        r["o_" + name][...] = small[i, :]
    channels = r["o_gain"].shape[0]
    r["o_gain"][...] = small[5, 0:channels]
    r["o_shift"][...] = small[5, channels : 2 * channels]
    for name, ref, copy in zip(as_is, passed, passing):
        copy.wait()
        going.append(move(ref, r["o_" + name]))
    for name in order:
        arriving[name].wait()
        part = held[name]
        parts, rows, columns = part.shape
        name, number = name.rstrip("012"), int(name[-1]) if name[-1] in "012" else 0
        to = made[name]
        top, left = 0, 0
        if name in ("up", "down"):
            top, down = number * parts * rows, parts
        else:
            down = to.shape[0] // rows
            left = number * (parts // down) * columns
        for t in range(parts):
            at = top + t % down * rows
            lane = left + t // down * columns
            to[at : at + rows, lane : lane + columns] = part[t].astype(F32)
        if name in ("up", "down"):
            rows = pl.ds(top, parts * rows)
            going.append(move(to.at[rows], r["o_" + name].at[rows]))
        elif number == dict(pin=2, stem=1).get(name, 0):
            going.append(move(to, r["o_" + name]))
    for copy in going:
        copy.wait()


def body(
    features, stem_weight, group_gain, group_bias, embed_weight, first_gain, first_bias,
    project_in, project_out, second_gain, second_bias, up_weight, up_bias, down_weight,
    valid_mask, slot_slice, cotangent, *, dp,
):
    slots = slot_slice.shape[0]
    L = features.shape[0] // slots
    R = cotangent.shape[0]
    cin, channels = stem_weight.shape
    D = cotangent.shape[1]
    wide_in = project_in.shape[1]
    project_in = project_in.T
    out_rows = project_out.shape[0]
    hidden = up_weight.shape[1]
    heads = 2 * wide_in // (3 * HEAD_DIM)
    hbm = pl.BlockSpec(memory_space=pl.ANY)
    vmem = pl.BlockSpec(memory_space=pltpu.VMEM)
    smem = pl.BlockSpec(memory_space=pltpu.SMEM)
    in_specs = dict(
        features=hbm, stem_weight=hbm, group_gain=vmem, group_bias=vmem, embed_weight=hbm,
        first_gain=vmem, first_bias=vmem, project_in=hbm, project_out=hbm, second_gain=vmem,
        second_bias=vmem, up_weight=hbm, up_bias=vmem, down_weight=hbm, valid_mask=vmem,
        slot_slice=smem, cotangent=hbm,
    )
    parts = dict(
        up0=(D // 8, hidden),
        up1=(D // 8, hidden),
        down0=(hidden // 8, D),
        down1=(hidden // 8, D),
        pout=(out_rows // 2, D // 2),
        pin0=(wide_in // 2, D // 6),
        pin1=(wide_in // 2, D // 6),
        pin2=(wide_in // 2, D // 6),
        embed=(channels // 4, D),
        stem0=(cin // 4, channels // 2),
        stem1=(cin // 4, channels // 2),
    )
    outs = dict(
        block_out=((R, D), BF16, hbm),
        features_grad=((R, cin), F32, hbm),
        o_small=((8, D), F32, vmem),
    )
    for name in GRADS:
        outs["o_" + name] = ((2, 2) + parts[name], BF16, hbm)
    scratch = dict(
        feat=((L, cin), BF16), stem=((2, cin, channels), BF16), std=((2, cin, channels), BF16),
        wstat=((2, 8, channels), F32), embed=((2, channels, D), BF16), pin=((2, wide_in, D), BF16),
        pout=((2, out_rows, D), BF16), up=((D, hidden), BF16), down=((hidden, D), BF16),
        gvec=((2, 8, channels), F32), xhs=((2, L, channels), F32), dgs=((2, L, channels), F32),
        act=((2, L, channels), BF16), gst=((2, 8, channels), F32),
        sbuf=((R, cin), F32), rbuf=((R, cin), F32), res1=((R, D), F32), xh1=((R, D), F32),
        rs1=((R, 1), F32), n1=((L, D), BF16), q=((heads, L, HEAD_DIM), BF16),
        k=((heads, L, HEAD_DIM), BF16), v=((heads, L, HEAD_DIM), BF16), probs=((heads, L, L), BF16),
        heads=((heads, L, HEAD_DIM), BF16), mixed=((L, heads * HEAD_DIM), BF16),
        res2=((R, D), F32), xh2=((R, D), F32), rs2=((R, 1), F32), n2=((4 * R, D), BF16),
        hid=((4 * R, hidden), BF16), branch=((4 * R, D), BF16), preg=((4 * R, hidden), BF16),
        own=((2, R, D), F32), csend=((2, 2, R, D), BF16),
        crecv=((2, 2, R, D), BF16), xsend=((2, R, D), BF16), xrecv=((2, R, D), BF16),
        mb=((L, D), BF16), pg=((2, L, wide_in), BF16),
    )
    for name in GRADS:
        size = {dim: 2 for dim in "xyb" if dim in AWAY[name]}
        scratch["g_" + name] = (tuple(size.values()) + parts[name], BF16)
        for level, dim in enumerate(AWAY[name]):
            if dim != "a":
                size[dim] = 1
            scratch["r%d_" % level + name] = (tuple(size.values()) + parts[name], BF16)
    scratch.update(sm=((8, D), F32), smr=((5, 8, D), F32))
    copies = 144
    shapes = [pltpu.VMEM(*one) for one in scratch.values()]
    shapes += [pltpu.SemaphoreType.DMA((copies,)) for _ in range(2)]
    shapes += [pltpu.SemaphoreType.DMA((24,))]
    names = tuple(scratch) + ("send_sems", "recv_sems", "local_sems")
    results = pl.pallas_call(
        functools.partial(kernel, tuple(in_specs), tuple(outs), names),
        out_shape=[jax.ShapeDtypeStruct(shape, kind) for shape, kind, _ in outs.values()],
        in_specs=list(in_specs.values()),
        out_specs=[spec for _, _, spec in outs.values()],
        scratch_shapes=shapes,
        compiler_params=pltpu.CompilerParams(
            collective_id=0, has_side_effects=True, vmem_limit_bytes=62 * 2**20
        ),
        name="layer",
    )(
        features, stem_weight, group_gain, group_bias, embed_weight, first_gain, first_bias,
        project_in, project_out, second_gain, second_bias, up_weight, up_bias, down_weight,
        valid_mask, slot_slice, cotangent,
    )
    out = dict(zip(outs, results))

    wide = {name: out["o_" + name].reshape((4,) + parts[name]) for name in GRADS}
    small = out["o_small"]
    bit = NEAR
    if bit < dp:
        wide = {name: part.astype(F32) for name, part in wide.items()}
    while bit < dp:
        pairs = [(i, i ^ bit) for i in range(dp)]
        wide, small = jax.tree.map(
            lambda part: part + lax.ppermute(part, "dp", pairs), (wide, small)
        )
        bit *= 2

    inputs = {"i_" + name: wide[name] for name in GRADS}
    inputs.update(i_block_out=out["block_out"], i_features_grad=out["features_grad"], i_small=small)
    whole = dict(
        up=(D, hidden), down=(hidden, D), pout=(out_rows, D), pin=(wide_in, D),
        embed=(channels, D), stem=(cin, channels),
    )
    finals = dict(o_block_out=((R, D), BF16, hbm), o_features_grad=((R, cin), F32, hbm))
    for name, shape in whole.items():
        finals["o_" + name] = (shape, F32, hbm)
    for name in ("g1", "b1", "g2", "b2"):
        finals["o_" + name] = ((D,), F32, vmem)
    finals["o_ub"] = ((hidden,), F32, vmem)
    for name in ("gain", "shift"):
        finals["o_" + name] = ((channels,), F32, vmem)
    moved = pl.pallas_call(
        functools.partial(finish, tuple(inputs), tuple(finals)),
        out_shape=[jax.ShapeDtypeStruct(shape, kind) for shape, kind, _ in finals.values()],
        in_specs=[hbm] * (len(inputs) - 1) + [vmem],
        out_specs=[spec for _, _, spec in finals.values()],
        scratch_shapes=[pltpu.SemaphoreType.DMA((28,))]
        + [pltpu.VMEM((R, D), BF16), pltpu.VMEM((R, cin), F32)]
        + [pltpu.VMEM(wide[name].shape, wide[name].dtype) for name in GRADS]
        + [pltpu.VMEM(shape, F32) for shape in whole.values()],
        compiler_params=pltpu.CompilerParams(vmem_limit_bytes=62 * 2**20),
        name="finish",
    )(*inputs.values())
    done = dict(zip(finals, moved))
    return (
        done["o_block_out"],
        done["o_features_grad"],
        done["o_stem"],
        done["o_gain"],
        done["o_shift"],
        done["o_embed"],
        done["o_g1"],
        done["o_b1"],
        done["o_pin"].T,
        done["o_pout"],
        done["o_g2"],
        done["o_b2"],
        done["o_up"],
        done["o_ub"],
        done["o_down"],
    )


def solution(mesh):
    return jax.shard_map(
        functools.partial(body, dp=mesh.shape["dp"]),
        mesh=mesh,
        in_specs=(
            P("dp", None), P(None, "mp"), P("mp"), P("mp"), P("mp", None), P(), P(),
            P(None, "mp"), P("mp", None), P(), P(), P(None, "mp"), P("mp"), P("mp", None),
            P(), P("dp"), P(("dp", "mp"), None),
        ),
        out_specs=(
            P(("dp", "mp"), None), P(("dp", "mp"), None), P(None, "mp"), P("mp"), P("mp"),
            P("mp", None), P(), P(), P(None, "mp"), P("mp", None), P(), P(), P(None, "mp"),
            P("mp"), P("mp", None),
        ),
        check_vma=False,
    )
```

```python
import functools
import itertools

import jax
import jax.numpy as jnp
from jax import lax
from jax.experimental import pallas as pl
from jax.experimental.pallas import tpu as pltpu
from jax.sharding import PartitionSpec as P

MESH = pl.DeviceIdType.MESH
F32 = jnp.float32
BF16 = jnp.bfloat16
HEAD_DIM = 64
GROUP = 32
NEAR = 8


def dot(left, right, left_dim=1, right_dim=0, precision=None):
    return lax.dot_general(
        left,
        right,
        (((left_dim,), (right_dim,)), ((), ())),
        precision=precision,
        preferred_element_type=F32,
    )


def gelu_parts(z):
    cdf = 0.5 + 0.5 * lax.erf(z * 0.7071067811865476)
    return z * cdf, cdf + z * (jnp.exp(-0.5 * z * z) * 0.3989422804014327)


class Net:
    def __init__(self, place, send_sems, recv_sems, local_sems):
        self.place = place
        self.send_sems, self.recv_sems, self.local_sems = send_sems, recv_sems, local_sems
        self.count, self.local_count, self.unsent = 0, 0, []

    def by(self, who, action):
        if who is None:
            action()
        else:
            pl.when(self.place.inner if who else jnp.logical_not(self.place.inner))(action)

    def plan(self, src, dst, device, who=None):
        copy = pltpu.make_async_remote_copy(
            src_ref=src,
            dst_ref=dst,
            send_sem=self.send_sems.at[self.count],
            recv_sem=self.recv_sems.at[self.count],
            device_id=device,
            device_id_type=MESH,
        )
        self.count += 1
        self.unsent.append((copy, who))
        return copy

    def send(self, src, dst, device, who=None):
        copy = self.plan(src, dst, device, who)
        self.by(who, copy.start)
        return copy

    def sent(self, copy):
        self.unsent = [one for one in self.unsent if one[0] is not copy]
        copy.wait_send()

    def local(self, src, dst, who=None):
        copy = pltpu.make_async_copy(src, dst, self.local_sems.at[self.local_count])
        self.local_count += 1
        self.by(who, copy.start)
        return copy

    def finish(self):
        for copy, who in self.unsent:
            self.by(who, copy.wait_send)


class Summed:
    def __init__(self, net, place, away, back, grad, arrive, out):
        self.net, self.place, self.away, self.back = net, place, away, back
        self.grad, self.arrive, self.out = grad, arrive, out
        self.dims = "xyb"[3 - (len(grad.shape) - 2) :]
        self.fixed = {}
        self.level, self.gathered = 0, None

    def index(self, dims, **more):
        fixed = {**self.fixed, **more}
        return tuple(pl.ds(fixed[dim], 1) if dim in fixed else pl.ds(0, 2) for dim in dims)

    def start(self):
        dim = self.away[self.level]
        bit, partner = self.place.partner(dim)
        inner_only = "a" in self.away[: self.level]
        if dim == "a":
            give, who = self.index(self.dims), False
        else:
            give, who = self.index(self.dims, **{dim: 1 - bit}), True if inner_only else None
            self.fixed[dim] = bit
        self.copy = self.net.send(self.grad.at[give], self.arrive[self.level], partner, who)

    def add(self, arrived):
        for at in itertools.product((0, 1), repeat=len(self.dims)):
            here = dict(zip(self.dims, at))
            if any(here[dim] for dim in self.fixed):
                continue
            where = tuple(self.fixed.get(dim, here[dim]) for dim in self.dims)
            value = self.grad[where].astype(F32) + arrived[at].astype(F32)
            self.grad[where] = value.astype(BF16)

    def held(self):
        return self.out.at[self.index("yb")]

    def share(self):
        dim = self.back[len(self.gathered)]
        _, partner = self.place.partner(dim)
        source = self.held()
        if not self.gathered:
            at = self.index("yb")
            source = self.grad.at[(0,) + at if "x" in self.dims else at]
        self.copy = self.net.send(source, self.held(), partner, True)
        if dim == "a" and len(self.gathered) < 2:
            _, partner = self.place.partner(self.back[2])
            self.last = self.net.plan(self.held(), self.held(), partner)
            self.net.by(True, self.last.start)

    def step(self):
        copy = self.copy
        if self.gathered is None:
            arrived = self.arrive[self.level]

            def take():
                copy.wait_recv()
                self.add(arrived)

            self.net.by(True if "a" in self.away[: self.level + 1] else None, take)
            self.level += 1
            if self.level < len(self.away):
                self.start()
                return
            self.fixed.pop("x", None)
            self.gathered = []
            at = self.index("yb")
            source = self.grad.at[(0,) + at if "x" in self.dims else at]
            self.own = self.net.local(source, self.held(), True)
            self.share()
            return
        dim = self.back[len(self.gathered)]
        if dim == "a":
            self.net.by(False, copy.wait_recv)
        elif "a" in self.gathered:
            copy.wait_recv()
        else:
            self.net.by(True, copy.wait_recv)
        if not self.gathered:
            self.net.by(True, self.own.wait)
        self.gathered.append(dim)
        self.fixed.pop(dim, None)
        if len(self.gathered) == 3:
            self.copy = None
        elif dim == "a":
            self.copy = self.last
            self.net.by(False, self.copy.start)
        else:
            self.share()

    def step_all(self):
        while self.copy is not None:
            self.step()


class Place:
    def __init__(self):
        self.d = lax.axis_index("dp")
        self.m = lax.axis_index("mp")
        self.x = lax.div(self.m, 2)
        self.c = lax.rem(self.m, 2)
        self.y = lax.rem(self.d, 2)
        self.zi = lax.div(lax.rem(self.d, NEAR), 2)
        self.sib_m = self.m + 1 - 2 * self.c
        self.far_m = lax.rem(self.m + 2, 4)
        self.far_sib_m = lax.rem(self.sib_m + 2, 4)
        self.sib = (self.d, self.sib_m)
        self.far = (self.d, self.far_m)
        self.y_device = (self.d + 1 - 2 * self.y, self.m)
        self.inner = jnp.logical_or(self.zi == 1, self.zi == 2)
        self.bits = {
            "y": (self.y, 1),
            "a": (lax.rem(self.zi, 2), 2),
            "b": (lax.div(self.zi, 2), 2),
            "w": (lax.div(self.zi, 2), 4),
        }

    def partner(self, name):
        if name == "x":
            return 0, self.far
        bit, stride = self.bits[name]
        return bit, (self.d + stride - 2 * stride * bit, self.m)


GRADS = ("up0", "up1", "down0", "down1", "pout", "pin0", "pin1", "pin2", "embed", "stem0", "stem1")
UP0, UP1, DOWN0, DOWN1, POUT, PIN0, PIN1, PIN2, EMBED, STEM0, STEM1, SMALL = range(12)
(NORM2, RESULT, MIXED_BACK, HEADS_FAR, HEADS_OWN, NORM1_SEND, NORM1, STEM_FAR, STEM_OWN, FEATURES_SEND,
 FEATURES_SUM) = range(12, 23)
KINDS = dict(g="grad", o="out", r0="arrive0", r1="arrive1", r2="arrive2", r3="arrive3")
AWAY = dict(
    down0="yab",
    down1="aby",
    up0="yab",
    up1="yab",
    pout="xaby",
    pin0="xaby",
    pin1="yxab",
    pin2="yxab",
    embed="xaby",
    stem0="xaby",
    stem1="xyab",
)
BACK = dict(
    down0="bay",
    down1="yba",
    up0="bay",
    up1="bay",
    pout="bay",
    pin0="bay",
    pin1="bay",
    pin2="bya",
    embed="bay",
    stem0="bay",
    stem1="bay",
)
ORDER = (
    NORM2, ~RESULT, DOWN0, MIXED_BACK, HEADS_FAR, ~POUT, DOWN1, UP0, HEADS_OWN, ~PIN1, DOWN0, UP1,
    NORM1_SEND, DOWN1, UP0, NORM1, ~PIN0, ~PIN2, POUT, DOWN0, STEM_FAR, ~STEM0, ~EMBED, PIN1, UP1,
    UP0, STEM_OWN, ~STEM1, DOWN1, DOWN0, FEATURES_SEND, SMALL, PIN0, POUT, UP1, FEATURES_SUM, PIN2,
    RESULT, UP0, STEM0, DOWN1, PIN0, POUT, DOWN0, UP1, STEM0, EMBED, UP0, PIN1, DOWN0, DOWN1, POUT,
    PIN0, UP1, STEM1, SMALL, EMBED, STEM0, UP0, POUT, PIN2, PIN1, PIN0, UP1, PIN2, EMBED, PIN1,
    STEM1, SMALL, DOWN1, STEM0, PIN0, PIN2, POUT, PIN1, EMBED, STEM0, SMALL, STEM1, PIN0, PIN2,
    POUT, PIN1, EMBED, STEM1, STEM0, PIN0, SMALL, STEM1, PIN1, PIN2, EMBED, STEM0, STEM1, EMBED,
    STEM1, PIN2,
)


def kernel(in_names, out_names, scratch_names, *refs):
    names = in_names + out_names + scratch_names
    r = dict(zip(names, refs))
    sums = {name: {} for name in GRADS}
    for name in names:
        kind, _, which = name.partition("_")
        if which in sums and kind in KINDS:
            sums[which][KINDS[kind]] = r.pop(name)
    for refs in sums.values():
        refs["arrive"] = [refs.pop(kind) for kind in sorted(refs) if kind.startswith("arrive")]
    run(sums=sums, **r)


def run(
    features, stem_weight, group_gain, group_bias, embed_weight, first_gain, first_bias,
    project_in, project_out, second_gain, second_bias, up_weight, up_bias, down_weight,
    valid_mask, slot_slice, cotangent,
    block_out, features_grad, o_small,
    feat, stem, std, wstat, embed, pin, pout, up, down, gvec, xhs, dgs, act, gst,
    sbuf, rbuf, res1, xh1, rs1, n1, q, k, v, probs, heads, mixed, res2, xh2, rs2,
    n2, hid, branch, preg, own, csend, crecv, xsend, xrecv, mb, pg,
    sm, smr, send_sems, recv_sems, local_sems, sums,
):
    place = Place()
    net = Net(place, send_sems, recv_sems, local_sems)
    x, c = place.x, place.c
    R = cotangent.shape[0]
    L = feat.shape[0]
    D = up.shape[0]
    own_rows = pl.multiple_of(c * R, 16)
    sib_rows = pl.multiple_of((1 - c) * R, 16)

    def block(m):
        return pl.ds(pl.multiple_of(m * R, 16), R)

    barrier = pltpu.get_barrier_semaphore()
    peers = [place.sib] + [place.partner(name)[1] for name in "xyaw"]
    for peer in peers:
        pl.semaphore_signal(barrier, inc=1, device_id=peer, device_id_type=MESH)

    def greet():
        peer = place.partner("b")[1]
        pl.semaphore_signal(barrier, inc=1, device_id=peer, device_id_type=MESH)

    net.by(True, greet)
    l_stem = net.local(stem_weight, stem.at[0])
    l_feat = net.local(features.at[pl.ds(pl.multiple_of(x * L, 16), L)], feat)
    l_embed = net.local(embed_weight, embed.at[0])
    l_cot = net.local(cotangent, branch.at[block(place.m)])
    l_pin = net.local(project_in, pin.at[0])
    l_pout = net.local(project_out, pout.at[0])
    l_up = net.local(up_weight, up)
    l_down = net.local(down_weight, down)
    gvec[0, 0:1, :] = group_gain[...].reshape(1, -1)
    gvec[0, 1:2, :] = group_bias[...].reshape(1, -1)
    pl.semaphore_wait(barrier, len(peers) + place.inner.astype(jnp.int32))

    c_gvec = net.send(gvec.at[0], gvec.at[1], place.far)

    def halves(weight, kept, pieces):
        rows = weight.shape[0] // pieces // 2
        for t in range(pieces):
            at = pl.ds(pl.multiple_of((2 * t + place.y) * rows, 16), rows)
            yield kept.at[1, at], net.send(weight.at[at], kept.at[1, at], place.far)

    stem_half = list(halves(stem_weight, stem, 2))
    embed_half = list(halves(embed_weight, embed, 1))
    pin_half = list(halves(project_in, pin, pin.shape[1] // (3 * HEAD_DIM)))
    pout_half = list(halves(project_out, pout, 1))
    c_cot = [
        net.send(cotangent, branch.at[block(place.m)], device) for device in (place.far, place.sib)
    ]

    def pass_on(half):
        ref, copy = half
        copy.wait_recv()
        return net.send(ref, ref, place.y_device)

    slices = valid_mask.shape[0]
    lengths = jnp.sum(valid_mask[...].astype(F32), axis=1, keepdims=True)
    mine = lax.broadcasted_iota(jnp.int32, (slices, 1), 0) == slot_slice[x]
    length = jnp.sum(jnp.where(mine, lengths, 0.0), axis=0, keepdims=True)

    def valid_rows(start, count):
        at = (lax.broadcasted_iota(jnp.int32, (count, 1), 0) + start).astype(F32)
        return jnp.where(at < length, 1.0, 0.0)

    key_valid = jnp.where(
        lax.broadcasted_iota(jnp.int32, (1, L), 1).astype(F32) < length, 1.0, 0.0
    )
    score_scale = HEAD_DIM ** (-0.5)
    key_scale = key_valid * score_scale
    key_shift = (key_valid - 1.0) * 1e9

    channels = stem.shape[2]
    same = (
        lax.div(lax.broadcasted_iota(jnp.int32, (channels, channels), 0), GROUP)
        == lax.div(lax.broadcasted_iota(jnp.int32, (channels, channels), 1), GROUP)
    )
    same = jnp.where(same, 1.0, 0.0)

    def group_sum(values):
        wide = jnp.broadcast_to(values, (8, channels))
        return dot(wide, same, precision=lax.Precision.HIGHEST)[0:1]

    def standardize(j):
        w = stem[j].astype(F32)
        average = jnp.sum(w, axis=0, keepdims=True) * (1.0 / w.shape[0])
        w = w - average
        scale = lax.rsqrt(jnp.sum(w * w, axis=0, keepdims=True) * (1.0 / w.shape[0]) + 1e-5)
        std[j] = (w * scale).astype(BF16)
        wstat[j, 0:1, :] = average
        wstat[j, 1:2, :] = scale

    tile_rows = [(t * R, R) for t in range(L // R)]

    def stem_forward(j):
        count = 1.0 / (length * GROUP)
        total = jnp.zeros((1, channels), F32)
        for at, size in tile_rows:
            s = dot(feat[at : at + size, :], std[j])
            xhs[j, at : at + size, :] = s
            total = total + jnp.sum(s * valid_rows(at, size), axis=0, keepdims=True)
        average = group_sum(total) * count
        total = jnp.zeros((1, channels), F32)
        for at, size in tile_rows:
            s = xhs[j, at : at + size, :] - average
            total = total + jnp.sum(s * s * valid_rows(at, size), axis=0, keepdims=True)
        scale = lax.rsqrt(group_sum(total) * count + 1e-5)
        gst[j, 0:1, :] = scale
        for at, size in tile_rows:
            xh = (xhs[j, at : at + size, :] - average) * scale
            xhs[j, at : at + size, :] = xh
            value, slope = gelu_parts(xh * gvec[j, 0:1, :] + gvec[j, 1:2, :])
            act[j, at : at + size, :] = value.astype(BF16)
            dgs[j, at : at + size, :] = slope

    l_stem.wait()
    standardize(0)
    c_stem = [pass_on(stem_half[0])]
    l_feat.wait()
    stem_forward(0)
    c_stem.append(pass_on(stem_half[1]))
    c_gvec.wait_recv()
    c_embed = pass_on(embed_half[0])
    for copy in c_stem:
        copy.wait_recv()
    standardize(1)
    stem_forward(1)
    l_embed.wait()
    c_embed.wait_recv()

    def core_sum(product):
        width = pl.ds(0, D)
        sbuf[:, width] = product(sib_rows)
        copy = net.send(sbuf.at[:, width], rbuf.at[:, width], place.sib)
        mine = product(own_rows)
        copy.wait_recv()
        net.sent(copy)
        return mine

    def embed_product(start):
        rows = pl.ds(start, R)
        return dot(act[0, rows, :], embed[0]) + dot(act[1, rows, :], embed[1])

    res1[...] = core_sum(embed_product)

    step = R // 3

    def layer_norm(res, other, add, gain, bias, xh_ref, scale_ref, out_ref, out_start):
        gain, bias = gain[...].reshape(1, -1), bias[...].reshape(1, -1)
        for t in range(3):
            rows = slice(t * step, (t + 1) * step)
            value = res[rows, :] + other[rows, 0:D]
            if add is not None:
                value = value + add[rows, :]
            res[rows, :] = value
            average = jnp.sum(value, axis=1, keepdims=True) * (1.0 / D)
            value = value - average
            scale = lax.rsqrt(jnp.sum(value * value, axis=1, keepdims=True) * (1.0 / D) + 1e-6)
            xh = value * scale
            xh_ref[rows, :] = xh
            scale_ref[rows, :] = scale
            out_ref[pl.ds(out_start + t * step, step), :] = (xh * gain + bias).astype(BF16)

    layer_norm(res1, rbuf, None, first_gain, first_bias, xh1, rs1, n1, own_rows)
    c_n1 = net.send(n1.at[pl.ds(own_rows, R)], n1.at[pl.ds(own_rows, R)], place.sib)
    l_pin.wait()
    c_n1.wait_recv()

    per_shard = pin.shape[1] // (3 * HEAD_DIM)

    width = 3 * HEAD_DIM
    pin_y = [net.plan(ref, ref, place.y_device) for ref, _ in pin_half]

    def pass_pin(i):
        pin_half[i][1].wait_recv()
        pin_y[i].start()

    def attend(h, carry):
        j, i = lax.div(h, per_shard), lax.rem(h, per_shard)
        for at in range(1, per_shard):

            @pl.when(h == at)
            def _():
                pass_pin(at)

        for at in range(per_shard):

            @pl.when(h == per_shard + at)
            def _():
                pin_y[at].wait_recv()

        @pl.when(h == per_shard + 1)
        def _():
            pout_half[0][1].wait_recv()
            pout_y.start()

        weight = pin[j, pl.ds(pl.multiple_of(i * width, 16), width), :]
        for at, size in tile_rows:
            packed = dot(n1[at : at + size, :], weight, 1, 1).astype(BF16)
            for t, ref in enumerate((q, k, v)):
                ref[h, at : at + size, :] = packed[:, t * HEAD_DIM : (t + 1) * HEAD_DIM]
        for at, size in tile_rows:
            s = dot(q[h, at : at + size, :], k[h], 1, 1) * key_scale + key_shift
            s = jnp.exp(s - jnp.max(s, axis=1, keepdims=True))
            p = (s * (1.0 / jnp.sum(s, axis=1, keepdims=True))).astype(BF16)
            probs[h, at : at + size, :] = p
            heads[h, at : at + size, :] = dot(p, v[h]).astype(BF16)
        return carry

    pass_pin(0)
    pout_y = net.plan(pout_half[0][0], pout_half[0][0], place.y_device)
    lax.fori_loop(0, 2 * per_shard, attend, 0)

    def side_by_side(pieces, store):
        at = 0
        while at < len(pieces):
            pair = pieces[at : at + 2]
            value = pair[0] if len(pair) == 1 else jnp.concatenate(pair, axis=1)
            store(slice(at * HEAD_DIM, at * HEAD_DIM + value.shape[1]), value)
            at += 2

    def store_mixed(lanes, value):
        mixed[:, lanes] = value

    side_by_side([heads[h] for h in range(2 * per_shard)], store_mixed)
    l_pout.wait()
    pout_y.wait_recv()
    out_width = pout.shape[1]

    def out_product(start):
        rows = pl.ds(start, R)
        return dot(mixed[rows, :], pout[...].reshape(-1, D))

    res2[...] = core_sum(out_product)
    layer_norm(
        res2, rbuf, res1, second_gain, second_bias, xh2, rs2, n2, pl.multiple_of(place.m * R, 16)
    )
    mine = block(place.m)
    c_n2 = [net.send(n2.at[mine], n2.at[mine], device) for device in (place.far, place.sib)]

    l_cot.wait()
    l_up.wait()
    l_down.wait()
    bias_sum = []

    def feed(m):
        rows = block(m)
        pre = dot(n2[rows, :], up[...]) + up_bias[...].reshape(1, -1)
        value, slope = gelu_parts(pre)
        hid[rows, :] = value.astype(BF16)
        grad = (dot(branch[rows, :], down[...], 1, 1) * slope).astype(BF16)
        preg[rows, :] = grad
        bias_sum.append(jnp.sum(grad.astype(F32), axis=0, keepdims=True))

    def back_part(m):
        return dot(preg[block(m), :], up[...], 1, 1)

    def out_part(m):
        return dot(hid[block(m), :], down[...])

    def mask_branch(m, own_slot):
        rows = block(m)
        start = lax.rem(m, 2) * R
        branch[rows, :] = (
            branch[rows, :].astype(F32) * valid_of(own_slot, start)
        ).astype(BF16)

    mine_far = lax.broadcasted_iota(jnp.int32, (slices, 1), 0) == slot_slice[1 - x]
    far_length = jnp.sum(jnp.where(mine_far, lengths, 0.0), axis=0, keepdims=True)

    def valid_of(own_slot, start):
        at = (lax.broadcasted_iota(jnp.int32, (R, 1), 0) + start).astype(F32)
        return jnp.where(at < (length if own_slot else far_length), 1.0, 0.0)

    c_cot[0].wait_recv()
    f_rows = block(place.far_m)
    c_cot_fwd = net.send(branch.at[f_rows], branch.at[f_rows], place.sib)
    mask_done = []

    mask_branch(place.m, True)
    feed(place.m)
    own[1] = back_part(place.m)
    c_cot[1].wait_recv()
    c_n2[1].wait_recv()
    mask_branch(place.sib_m, True)
    feed(place.sib_m)
    csend[1, 0] = back_part(place.sib_m).astype(BF16)
    c_core = {}
    c_core[1, 0] = net.send(csend.at[1, 0], crecv.at[1, 0], place.sib)
    c_n2[0].wait_recv()
    c_n2_fwd = net.send(n2.at[f_rows], n2.at[f_rows], place.sib)
    csend[0, 0] = out_part(place.sib_m).astype(BF16)
    c_core[0, 0] = net.send(csend.at[0, 0], crecv.at[0, 0], place.sib)
    own[0] = out_part(place.m)
    c_cot_fwd.wait_recv()
    c_n2_fwd.wait_recv()
    mask_branch(place.far_sib_m, False)
    feed(place.far_sib_m)
    csend[1, 1] = back_part(place.far_sib_m).astype(BF16)
    c_core[1, 1] = net.send(csend.at[1, 1], crecv.at[1, 1], place.sib)
    net.sent(c_cot_fwd)
    mask_branch(place.far_m, False)
    feed(place.far_m)
    sbuf[:, 0:D] = back_part(place.far_m)
    c_core[1, 1].wait_recv()
    xsend[1] = (sbuf[:, 0:D] + crecv[1, 1].astype(F32)).astype(BF16)
    c_far = {}
    c_far[1] = net.send(xsend.at[1], xrecv.at[1], place.far)

    def result_send():
        csend[0, 1] = out_part(place.far_sib_m).astype(BF16)
        c_core[0, 1] = net.send(csend.at[0, 1], crecv.at[0, 1], place.sib)
        sbuf[:, 0:D] = out_part(place.far_m)
        c_core[0, 1].wait_recv()
        xsend[0] = (sbuf[:, 0:D] + crecv[0, 1].astype(F32)).astype(BF16)
        c_far[0] = net.send(xsend.at[0], xrecv.at[0], place.far)

    summed = {name: Summed(net, place, AWAY[name], BACK[name], **sums[name]) for name in GRADS}

    def keep(name, slot, at, value):
        ref = sums[name]["grad"]
        rows = ref.shape[-2]
        for t in range(value.shape[0] // rows):
            part = (at + t) // 2, (at + t) % 2
            ref[part if slot is None else (slot,) + part] = value[
                t * rows : (t + 1) * rows
            ].astype(BF16)

    half = D // 2
    for i, name in enumerate(("down0", "down1")):
        keep(name, None, 0, dot(hid[:, i * half : (i + 1) * half], branch[...], 0, 0))
        summed[name].start()
    for i, name in enumerate(("up0", "up1")):
        keep(name, None, 0, dot(n2[:, i * half : (i + 1) * half], preg[...], 0, 0))
        summed[name].start()
    sm[...] = jnp.zeros_like(sm)
    sm[4:5, :] = bias_sum[0] + bias_sum[1] + bias_sum[2] + bias_sum[3]

    def norm_back(grad_of, gain, xh_ref, scale_ref, kept, out_ref, out_start, row):
        gain = gain[...].reshape(1, -1)
        gain_sum = jnp.zeros((1, D), F32)
        bias_total = jnp.zeros((1, D), F32)
        for t in range(3):
            rows = slice(t * step, (t + 1) * step)
            dy, through = grad_of(rows)
            xh = xh_ref[rows, :]
            gain_sum = gain_sum + jnp.sum(dy * xh, axis=0, keepdims=True)
            bias_total = bias_total + jnp.sum(dy, axis=0, keepdims=True)
            dy = dy * gain
            mean_one = jnp.sum(dy, axis=1, keepdims=True) * (1.0 / D)
            mean_two = jnp.sum(dy * xh, axis=1, keepdims=True) * (1.0 / D)
            dx = through + scale_ref[rows, :] * (dy - mean_one - xh * mean_two)
            if kept is not None:
                kept[rows, :] = dx
            out_ref[pl.ds(out_start + t * step, step), :] = dx.astype(BF16)
        sm[row : row + 1, :] = gain_sum
        sm[row + 1 : row + 2, :] = bias_total

    own_part = pl.ds(own_rows, R)
    sg2, eb, sg = res1, mb, act
    copies = {}
    locals_left = []
    tasks = {}

    def task(number):
        def enter(function):
            tasks[number] = function

        return enter

    @task(NORM2)
    def norm2():
        c_core[1, 0].wait_recv()
        c_far[1].wait_recv()

        def grad_of(rows):
            dy = own[1, rows, :] + crecv[1, 0, rows, :].astype(F32) + xrecv[1, rows, :].astype(F32)
            at = pl.ds(pl.multiple_of(place.m * R, 16) + rows.start, step)
            return dy, branch[at, :].astype(F32)

        norm_back(grad_of, second_gain, xh2, rs2, sg2, mb, own_rows, 2)
        copies["mb"] = net.send(mb.at[own_part], mb.at[own_part], place.sib)

    @task(RESULT)
    def result():
        c_core[0, 0].wait_recv()
        c_far[0].wait_recv()
        net.sent(c_core[0, 0])
        for t in range(3):
            rows = slice(t * step, (t + 1) * step)
            value = (
                res2[rows, :]
                + own[0, rows, :]
                + crecv[0, 0, rows, :].astype(F32)
                + xrecv[0, rows, :].astype(F32)
            )
            csend[0, 0, rows, :] = (value * valid_rows(own_rows + t * step, step)).astype(BF16)
        locals_left.append(net.local(csend.at[0, 0], block_out))

    @task(MIXED_BACK)
    def mixed_back():
        copies["mb"].wait_recv()
        value = dot(mixed[...], mb[...], 0, 0)
        shard = pout.shape[1]
        for j in range(2):
            rows = value[j * shard : (j + 1) * shard]
            for i in range(2):
                keep("pout", j, 2 * i, rows[:, i * half : (i + 1) * half])
        for at, size in tile_rows:
            value = dot(mb[at : at + size, :], pout[...].reshape(-1, D), 1, 1).astype(BF16)
            for h in range(2 * per_shard):
                heads[h, at : at + size, :] = value[:, h * HEAD_DIM : (h + 1) * HEAD_DIM]

    def head_back(h, carry):
        p = probs[h]
        dp = dot(heads[h], v[h], 1, 1)
        v[h] = dot(p, heads[h], 0, 0).astype(BF16)
        p = p.astype(F32)
        ds = (p * (dp - jnp.sum(p * dp, axis=1, keepdims=True))).astype(BF16)
        dq = (dot(ds, k[h]) * score_scale).astype(BF16)
        k[h] = (dot(ds, q[h], 0, 0) * score_scale).astype(BF16)
        q[h] = dq
        return carry

    def pin_back(j):
        lax.fori_loop(per_shard * j, per_shard * (j + 1), head_back, 0)

        def store_pg(lanes, value):
            pg[j, :, lanes] = value

        pieces = [ref[per_shard * j + h] for h in range(per_shard) for ref in (q, k, v)]
        side_by_side(pieces, store_pg)
        value = dot(pg[j], n1[...], 0, 0)
        wide = D // 6
        for i in range(6):
            keep("pin%d" % (i // 2), j, 2 * (i % 2), value[:, i * wide : (i + 1) * wide])

    @task(HEADS_FAR)
    def heads_far():
        pin_back(1)

    @task(HEADS_OWN)
    def heads_own():
        pin_back(0)

    @task(NORM1_SEND)
    def norm1_send():
        def product(start):
            rows = pl.ds(start, R)
            return dot(pg[0, rows, :], pin[0]) + dot(pg[1, rows, :], pin[1])

        width = pl.ds(0, D)
        sbuf[:, width] = product(sib_rows)
        copies["n1"] = net.send(sbuf.at[:, width], rbuf.at[:, width], place.sib)
        xh2[...] = product(own_rows)

    @task(NORM1)
    def norm1():
        copies["n1"].wait_recv()
        net.sent(copies["n1"])

        def grad_of(rows):
            return xh2[rows, :] + rbuf[rows, 0:D], sg2[rows, :]

        net.sent(copies["mb"])
        norm_back(grad_of, first_gain, xh1, rs1, None, eb, own_rows, 0)
        copies["eb"] = net.send(eb.at[own_part], eb.at[own_part], place.sib)

    def embed_back(j):
        keep("embed", j, 0, dot(act[j], eb[...], 0, 0))

    cin = feat.shape[1]
    square = pl.ds(0, cin // 4), pl.ds(0, channels)
    spares = [ref.at[square] for ref in (xh1, xh2, res1, own.at[1])]

    def stem_back(j):
        gain_sum = jnp.zeros((1, channels), F32)
        bias_total = jnp.zeros((1, channels), F32)
        for at, size in tile_rows:
            dz = dot(eb[at : at + size, :], embed[j], 1, 1) * dgs[j, at : at + size, :]
            dgs[j, at : at + size, :] = dz
            gain_sum = gain_sum + jnp.sum(dz * xhs[j, at : at + size, :], axis=0, keepdims=True)
            bias_total = bias_total + jnp.sum(dz, axis=0, keepdims=True)
        sm[5 + j : 6 + j, 0:channels] = gain_sum
        sm[5 + j : 6 + j, channels : 2 * channels] = bias_total
        gain = gvec[j, 0:1, :]
        count = 1.0 / (length * GROUP)
        mean_one = group_sum(bias_total * gain) * count
        mean_two = group_sum(gain_sum * gain) * count
        for at, size in tile_rows:
            part = dgs[j, at : at + size, :] * gain - valid_rows(at, size) * (
                mean_one + xhs[j, at : at + size, :] * mean_two
            )
            sg[j, at : at + size, :] = (part * gst[j, 0:1, :]).astype(BF16)
        average, scale = wstat[j, 0:1, :], wstat[j, 1:2, :]
        sum_one = jnp.zeros((1, channels), F32)
        sum_two = jnp.zeros((1, channels), F32)
        quarter = cin // 4
        for t in range(4):
            rows = slice(t * quarter, (t + 1) * quarter)
            grad = dot(feat[:, rows], sg[j], 0, 0)
            spare = spares[t]
            spare[...] = grad
            xh = (stem[j, rows, :].astype(F32) - average) * scale
            sum_one = sum_one + jnp.sum(grad, axis=0, keepdims=True)
            sum_two = sum_two + jnp.sum(grad * xh, axis=0, keepdims=True)
        sum_one = sum_one * (1.0 / cin)
        sum_two = sum_two * (1.0 / cin)
        for t in range(4):
            rows = slice(t * quarter, (t + 1) * quarter)
            xh = (stem[j, rows, :].astype(F32) - average) * scale
            value = (spares[t][...] - sum_one - xh * sum_two) * scale
            for i in range(2):
                lanes = slice(i * channels // 2, (i + 1) * channels // 2)
                keep("stem%d" % i, j, t, value[:, lanes])

    @task(STEM_FAR)
    def stem_far():
        copies["eb"].wait_recv()
        embed_back(1)
        stem_back(1)

    @task(STEM_OWN)
    def stem_own():
        embed_back(0)
        stem_back(0)
        small("core")

    def feature_product(start):
        rows = pl.ds(start, R)
        return dot(sg[0, rows, :], std[0], 1, 1) + dot(sg[1, rows, :], std[1], 1, 1)

    @task(FEATURES_SEND)
    def features_send():
        sbuf[...] = feature_product(sib_rows)
        copies["feat"] = net.send(sbuf, rbuf, place.sib)

    @task(FEATURES_SUM)
    def features_sum():
        copies["feat"].wait_recv()
        net.sent(copies["feat"])
        sbuf[...] = feature_product(own_rows) + rbuf[...]
        locals_left.append(net.local(sbuf, features_grad))

    small_at = {"core": place.sib}
    for name in "xyaw":
        small_at[name] = place.partner(name)[1]
    small_order = tuple(small_at)

    def small(name):
        copies["small"] = net.send(sm, smr.at[small_order.index(name)], small_at[name])

    def small_step(i):
        copies["small"].wait_recv()
        net.sent(copies["small"])
        if small_order[i] in ("core", "x"):
            sm[0:4, :] = sm[0:4, :] + smr[i, 0:4, :]
            if small_order[i] == "x":
                sm[5:6, :] = sm[5:6, :] + smr[i, 6:7, :]
        else:
            sm[...] = sm[...] + smr[i]
        if i + 1 < len(small_order):
            small(small_order[i + 1])
        else:
            o_small[...] = sm[...]

    small_next = list(range(len(small_order)))
    for what in ORDER:
        if what in tasks:
            tasks.pop(what)()
        elif what == SMALL:
            small_step(small_next.pop(0))
        elif what == ~RESULT:
            result_send()
        elif what < 0:
            summed[GRADS[~what]].start()
        else:
            summed[GRADS[what]].step()
    assert not tasks and not small_next
    for one in summed.values():
        one.step_all()
    for copy in locals_left:
        copy.wait()
    net.finish()


def finish(in_names, out_names, *refs):
    names = in_names + out_names
    r = dict(zip(names, refs))
    rest = refs[len(names) :]
    sems, passed, rest = rest[0], rest[1:3], rest[3:]
    held, made = rest[: len(GRADS)], rest[len(GRADS) :]
    made = dict(zip(("up", "down", "pout", "pin", "embed", "stem"), made))
    count = [0]
    going = []

    def move(src, dst):
        copy = pltpu.make_async_copy(src, dst, sems.at[count[0]])
        count[0] += 1
        copy.start()
        return copy

    order = GRADS
    held = dict(zip(GRADS, held))
    as_is = ("block_out", "features_grad")
    passing = [move(r["i_" + name], ref) for name, ref in zip(as_is, passed)]
    arriving = {name: move(r["i_" + name], held[name]) for name in order}
    small = r["i_small"]
    for i, name in enumerate(("g1", "b1", "g2", "b2", "ub")):
        r["o_" + name][...] = small[i, :]
    channels = r["o_gain"].shape[0]
    r["o_gain"][...] = small[5, 0:channels]
    r["o_shift"][...] = small[5, channels : 2 * channels]
    for name, ref, copy in zip(as_is, passed, passing):
        copy.wait()
        going.append(move(ref, r["o_" + name]))
    for name in order:
        arriving[name].wait()
        part = held[name]
        parts, rows, columns = part.shape
        name, number = name.rstrip("012"), int(name[-1]) if name[-1] in "012" else 0
        to = made[name]
        top, left = 0, 0
        if name in ("up", "down"):
            top, down = number * parts * rows, parts
        else:
            down = to.shape[0] // rows
            left = number * (parts // down) * columns
        for t in range(parts):
            at = top + t % down * rows
            lane = left + t // down * columns
            to[at : at + rows, lane : lane + columns] = part[t].astype(F32)
        if name in ("up", "down"):
            rows = pl.ds(top, parts * rows)
            going.append(move(to.at[rows], r["o_" + name].at[rows]))
        elif number == dict(pin=2, stem=1).get(name, 0):
            going.append(move(to, r["o_" + name]))
    for copy in going:
        copy.wait()


def body(
    features, stem_weight, group_gain, group_bias, embed_weight, first_gain, first_bias,
    project_in, project_out, second_gain, second_bias, up_weight, up_bias, down_weight,
    valid_mask, slot_slice, cotangent, *, dp,
):
    slots = slot_slice.shape[0]
    L = features.shape[0] // slots
    R = cotangent.shape[0]
    cin, channels = stem_weight.shape
    D = cotangent.shape[1]
    wide_in = project_in.shape[1]
    project_in = project_in.T
    out_rows = project_out.shape[0]
    hidden = up_weight.shape[1]
    heads = 2 * wide_in // (3 * HEAD_DIM)
    hbm = pl.BlockSpec(memory_space=pl.ANY)
    vmem = pl.BlockSpec(memory_space=pltpu.VMEM)
    smem = pl.BlockSpec(memory_space=pltpu.SMEM)
    in_specs = dict(
        features=hbm, stem_weight=hbm, group_gain=vmem, group_bias=vmem, embed_weight=hbm,
        first_gain=vmem, first_bias=vmem, project_in=hbm, project_out=hbm, second_gain=vmem,
        second_bias=vmem, up_weight=hbm, up_bias=vmem, down_weight=hbm, valid_mask=vmem,
        slot_slice=smem, cotangent=hbm,
    )
    parts = dict(
        up0=(D // 8, hidden),
        up1=(D // 8, hidden),
        down0=(hidden // 8, D),
        down1=(hidden // 8, D),
        pout=(out_rows // 2, D // 2),
        pin0=(wide_in // 2, D // 6),
        pin1=(wide_in // 2, D // 6),
        pin2=(wide_in // 2, D // 6),
        embed=(channels // 4, D),
        stem0=(cin // 4, channels // 2),
        stem1=(cin // 4, channels // 2),
    )
    outs = dict(
        block_out=((R, D), BF16, hbm),
        features_grad=((R, cin), F32, hbm),
        o_small=((8, D), F32, vmem),
    )
    for name in GRADS:
        outs["o_" + name] = ((2, 2) + parts[name], BF16, hbm)
    scratch = dict(
        feat=((L, cin), BF16), stem=((2, cin, channels), BF16), std=((2, cin, channels), BF16),
        wstat=((2, 8, channels), F32), embed=((2, channels, D), BF16), pin=((2, wide_in, D), BF16),
        pout=((2, out_rows, D), BF16), up=((D, hidden), BF16), down=((hidden, D), BF16),
        gvec=((2, 8, channels), F32), xhs=((2, L, channels), F32), dgs=((2, L, channels), F32),
        act=((2, L, channels), BF16), gst=((2, 8, channels), F32),
        sbuf=((R, cin), F32), rbuf=((R, cin), F32), res1=((R, D), F32), xh1=((R, D), F32),
        rs1=((R, 1), F32), n1=((L, D), BF16), q=((heads, L, HEAD_DIM), BF16),
        k=((heads, L, HEAD_DIM), BF16), v=((heads, L, HEAD_DIM), BF16), probs=((heads, L, L), BF16),
        heads=((heads, L, HEAD_DIM), BF16), mixed=((L, heads * HEAD_DIM), BF16),
        res2=((R, D), F32), xh2=((R, D), F32), rs2=((R, 1), F32), n2=((4 * R, D), BF16),
        hid=((4 * R, hidden), BF16), branch=((4 * R, D), BF16), preg=((4 * R, hidden), BF16),
        own=((2, R, D), F32), csend=((2, 2, R, D), BF16),
        crecv=((2, 2, R, D), BF16), xsend=((2, R, D), BF16), xrecv=((2, R, D), BF16),
        mb=((L, D), BF16), pg=((2, L, wide_in), BF16),
    )
    for name in GRADS:
        size = {dim: 2 for dim in "xyb" if dim in AWAY[name]}
        scratch["g_" + name] = (tuple(size.values()) + parts[name], BF16)
        for level, dim in enumerate(AWAY[name]):
            if dim != "a":
                size[dim] = 1
            scratch["r%d_" % level + name] = (tuple(size.values()) + parts[name], BF16)
    scratch.update(sm=((8, D), F32), smr=((5, 8, D), F32))
    copies = 144
    shapes = [pltpu.VMEM(*one) for one in scratch.values()]
    shapes += [pltpu.SemaphoreType.DMA((copies,)) for _ in range(2)]
    shapes += [pltpu.SemaphoreType.DMA((24,))]
    names = tuple(scratch) + ("send_sems", "recv_sems", "local_sems")
    results = pl.pallas_call(
        functools.partial(kernel, tuple(in_specs), tuple(outs), names),
        out_shape=[jax.ShapeDtypeStruct(shape, kind) for shape, kind, _ in outs.values()],
        in_specs=list(in_specs.values()),
        out_specs=[spec for _, _, spec in outs.values()],
        scratch_shapes=shapes,
        compiler_params=pltpu.CompilerParams(
            collective_id=0, has_side_effects=True, vmem_limit_bytes=62 * 2**20
        ),
        name="layer",
    )(
        features, stem_weight, group_gain, group_bias, embed_weight, first_gain, first_bias,
        project_in, project_out, second_gain, second_bias, up_weight, up_bias, down_weight,
        valid_mask, slot_slice, cotangent,
    )
    out = dict(zip(outs, results))

    wide = {name: out["o_" + name].reshape((4,) + parts[name]) for name in GRADS}
    small = out["o_small"]
    bit = NEAR
    if bit < dp:
        wide = {name: part.astype(F32) for name, part in wide.items()}
    while bit < dp:
        pairs = [(i, i ^ bit) for i in range(dp)]
        wide, small = jax.tree.map(
            lambda part: part + lax.ppermute(part, "dp", pairs), (wide, small)
        )
        bit *= 2

    inputs = {"i_" + name: wide[name] for name in GRADS}
    inputs.update(i_block_out=out["block_out"], i_features_grad=out["features_grad"], i_small=small)
    whole = dict(
        up=(D, hidden), down=(hidden, D), pout=(out_rows, D), pin=(wide_in, D),
        embed=(channels, D), stem=(cin, channels),
    )
    finals = dict(o_block_out=((R, D), BF16, hbm), o_features_grad=((R, cin), F32, hbm))
    for name, shape in whole.items():
        finals["o_" + name] = (shape, F32, hbm)
    for name in ("g1", "b1", "g2", "b2"):
        finals["o_" + name] = ((D,), F32, vmem)
    finals["o_ub"] = ((hidden,), F32, vmem)
    for name in ("gain", "shift"):
        finals["o_" + name] = ((channels,), F32, vmem)
    moved = pl.pallas_call(
        functools.partial(finish, tuple(inputs), tuple(finals)),
        out_shape=[jax.ShapeDtypeStruct(shape, kind) for shape, kind, _ in finals.values()],
        in_specs=[hbm] * (len(inputs) - 1) + [vmem],
        out_specs=[spec for _, _, spec in finals.values()],
        scratch_shapes=[pltpu.SemaphoreType.DMA((28,))]
        + [pltpu.VMEM((R, D), BF16), pltpu.VMEM((R, cin), F32)]
        + [pltpu.VMEM(wide[name].shape, wide[name].dtype) for name in GRADS]
        + [pltpu.VMEM(shape, F32) for shape in whole.values()],
        compiler_params=pltpu.CompilerParams(vmem_limit_bytes=62 * 2**20),
        name="finish",
    )(*inputs.values())
    done = dict(zip(finals, moved))
    return (
        done["o_block_out"],
        done["o_features_grad"],
        done["o_stem"],
        done["o_gain"],
        done["o_shift"],
        done["o_embed"],
        done["o_g1"],
        done["o_b1"],
        done["o_pin"].T,
        done["o_pout"],
        done["o_g2"],
        done["o_b2"],
        done["o_up"],
        done["o_ub"],
        done["o_down"],
    )


def solution(mesh):
    return jax.shard_map(
        functools.partial(body, dp=mesh.shape["dp"]),
        mesh=mesh,
        in_specs=(
            P("dp", None), P(None, "mp"), P("mp"), P("mp"), P("mp", None), P(), P(),
            P(None, "mp"), P("mp", None), P(), P(), P(None, "mp"), P("mp"), P("mp", None),
            P(), P("dp"), P(("dp", "mp"), None),
        ),
        out_specs=(
            P(("dp", "mp"), None), P(("dp", "mp"), None), P(None, "mp"), P("mp"), P("mp"),
            P("mp", None), P(), P(), P(None, "mp"), P("mp", None), P(), P(), P(None, "mp"),
            P("mp"), P("mp", None),
        ),
        check_vma=False,
    )
```

```python
import functools
import itertools

import jax
import jax.numpy as jnp
from jax import lax
from jax.experimental import pallas as pl
from jax.experimental.pallas import tpu as pltpu
from jax.sharding import PartitionSpec as P

MESH = pl.DeviceIdType.MESH
F32 = jnp.float32
BF16 = jnp.bfloat16
HEAD_DIM = 64
GROUP = 32
NEAR = 8


def dot(left, right, left_dim=1, right_dim=0, precision=None):
    return lax.dot_general(
        left,
        right,
        (((left_dim,), (right_dim,)), ((), ())),
        precision=precision,
        preferred_element_type=F32,
    )


def gelu_parts(z):
    cdf = 0.5 + 0.5 * lax.erf(z * 0.7071067811865476)
    return z * cdf, cdf + z * (jnp.exp(-0.5 * z * z) * 0.3989422804014327)


class Net:
    def __init__(self, place, send_sems, recv_sems, local_sems):
        self.place = place
        self.send_sems, self.recv_sems, self.local_sems = send_sems, recv_sems, local_sems
        self.count, self.local_count, self.unsent = 0, 0, []

    def by(self, who, action):
        if who is None:
            action()
        else:
            pl.when(self.place.inner if who else jnp.logical_not(self.place.inner))(action)

    def plan(self, src, dst, device, who=None):
        copy = pltpu.make_async_remote_copy(
            src_ref=src,
            dst_ref=dst,
            send_sem=self.send_sems.at[self.count],
            recv_sem=self.recv_sems.at[self.count],
            device_id=device,
            device_id_type=MESH,
        )
        self.count += 1
        self.unsent.append((copy, who))
        return copy

    def send(self, src, dst, device, who=None):
        copy = self.plan(src, dst, device, who)
        self.by(who, copy.start)
        return copy

    def sent(self, copy):
        self.unsent = [one for one in self.unsent if one[0] is not copy]
        copy.wait_send()

    def local(self, src, dst, who=None):
        copy = pltpu.make_async_copy(src, dst, self.local_sems.at[self.local_count])
        self.local_count += 1
        self.by(who, copy.start)
        return copy

    def finish(self):
        for copy, who in self.unsent:
            self.by(who, copy.wait_send)


class Summed:
    def __init__(self, net, place, away, back, grad, arrive, out):
        self.net, self.place, self.away, self.back = net, place, away, back
        self.grad, self.arrive, self.out = grad, arrive, out
        self.dims = "xyb"[3 - (len(grad.shape) - 2) :]
        self.fixed = {}
        self.level, self.gathered = 0, None

    def index(self, dims, **more):
        fixed = {**self.fixed, **more}
        return tuple(pl.ds(fixed[dim], 1) if dim in fixed else pl.ds(0, 2) for dim in dims)

    def start(self):
        dim = self.away[self.level]
        bit, partner = self.place.partner(dim)
        inner_only = "a" in self.away[: self.level]
        if dim == "a":
            give, who = self.index(self.dims), False
        else:
            give, who = self.index(self.dims, **{dim: 1 - bit}), True if inner_only else None
            self.fixed[dim] = bit
        self.copy = self.net.send(self.grad.at[give], self.arrive[self.level], partner, who)

    def add(self, arrived):
        for at in itertools.product((0, 1), repeat=len(self.dims)):
            here = dict(zip(self.dims, at))
            if any(here[dim] for dim in self.fixed):
                continue
            where = tuple(self.fixed.get(dim, here[dim]) for dim in self.dims)
            value = self.grad[where].astype(F32) + arrived[at].astype(F32)
            self.grad[where] = value.astype(BF16)

    def held(self):
        return self.out.at[self.index("yb")]

    def share(self):
        dim = self.back[len(self.gathered)]
        _, partner = self.place.partner(dim)
        source = self.held()
        if not self.gathered:
            at = self.index("yb")
            source = self.grad.at[(0,) + at if "x" in self.dims else at]
        self.copy = self.net.send(source, self.held(), partner, True)
        if dim == "a" and len(self.gathered) < 2:
            _, partner = self.place.partner(self.back[2])
            self.last = self.net.plan(self.held(), self.held(), partner)
            self.net.by(True, self.last.start)

    def step(self):
        copy = self.copy
        if self.gathered is None:
            arrived = self.arrive[self.level]

            def take():
                copy.wait_recv()
                self.add(arrived)

            self.net.by(True if "a" in self.away[: self.level + 1] else None, take)
            self.level += 1
            if self.level < len(self.away):
                self.start()
                return
            self.fixed.pop("x", None)
            self.gathered = []
            at = self.index("yb")
            source = self.grad.at[(0,) + at if "x" in self.dims else at]
            self.own = self.net.local(source, self.held(), True)
            self.share()
            return
        dim = self.back[len(self.gathered)]
        if dim == "a":
            self.net.by(False, copy.wait_recv)
        elif "a" in self.gathered:
            copy.wait_recv()
        else:
            self.net.by(True, copy.wait_recv)
        if not self.gathered:
            self.net.by(True, self.own.wait)
        self.gathered.append(dim)
        self.fixed.pop(dim, None)
        if len(self.gathered) == 3:
            self.copy = None
        elif dim == "a":
            self.copy = self.last
            self.net.by(False, self.copy.start)
        else:
            self.share()

    def step_all(self):
        while self.copy is not None:
            self.step()


class Place:
    def __init__(self):
        self.d = lax.axis_index("dp")
        self.m = lax.axis_index("mp")
        self.x = lax.div(self.m, 2)
        self.c = lax.rem(self.m, 2)
        self.y = lax.rem(self.d, 2)
        self.zi = lax.div(lax.rem(self.d, NEAR), 2)
        self.sib_m = self.m + 1 - 2 * self.c
        self.far_m = lax.rem(self.m + 2, 4)
        self.far_sib_m = lax.rem(self.sib_m + 2, 4)
        self.sib = (self.d, self.sib_m)
        self.far = (self.d, self.far_m)
        self.y_device = (self.d + 1 - 2 * self.y, self.m)
        self.inner = jnp.logical_or(self.zi == 1, self.zi == 2)
        self.bits = {
            "y": (self.y, 1),
            "a": (lax.rem(self.zi, 2), 2),
            "b": (lax.div(self.zi, 2), 2),
            "w": (lax.div(self.zi, 2), 4),
        }

    def partner(self, name):
        if name == "x":
            return 0, self.far
        bit, stride = self.bits[name]
        return bit, (self.d + stride - 2 * stride * bit, self.m)


GRADS = ("up0", "up1", "down0", "down1", "pout", "pin0", "pin1", "pin2", "embed", "stem0", "stem1")
UP0, UP1, DOWN0, DOWN1, POUT, PIN0, PIN1, PIN2, EMBED, STEM0, STEM1, SMALL = range(12)
(NORM2, RESULT, MIXED_BACK, HEADS_FAR, HEADS_OWN, NORM1_SEND, NORM1, STEM_FAR, STEM_OWN, FEATURES_SEND,
 FEATURES_SUM) = range(12, 23)
KINDS = dict(g="grad", o="out", r0="arrive0", r1="arrive1", r2="arrive2", r3="arrive3")
AWAY = dict(
    down0="yab",
    down1="aby",
    up0="yab",
    up1="yab",
    pout="xaby",
    pin0="xaby",
    pin1="yxab",
    pin2="yxab",
    embed="xaby",
    stem0="xaby",
    stem1="xyab",
)
BACK = dict(
    down0="bay",
    down1="yba",
    up0="bay",
    up1="bay",
    pout="bay",
    pin0="bay",
    pin1="bay",
    pin2="bya",
    embed="bay",
    stem0="bay",
    stem1="bay",
)
ORDER = (
    NORM2, ~RESULT, DOWN0, MIXED_BACK, HEADS_FAR, ~POUT, DOWN1, UP0, HEADS_OWN, ~PIN1, DOWN0, UP1,
    NORM1_SEND, DOWN1, UP0, NORM1, ~PIN0, ~PIN2, POUT, DOWN0, STEM_FAR, ~STEM0, ~EMBED, PIN1, UP1,
    UP0, STEM_OWN, ~STEM1, DOWN1, DOWN0, FEATURES_SEND, SMALL, PIN0, POUT, UP1, FEATURES_SUM, PIN2,
    RESULT, UP0, STEM0, DOWN1, PIN0, POUT, DOWN0, UP1, STEM0, EMBED, UP0, PIN1, DOWN0, DOWN1, POUT,
    PIN0, UP1, STEM1, SMALL, EMBED, STEM0, UP0, POUT, PIN2, PIN1, PIN0, UP1, PIN2, EMBED, PIN1,
    STEM1, SMALL, DOWN1, STEM0, PIN0, PIN2, POUT, PIN1, EMBED, STEM0, SMALL, STEM1, PIN0, PIN2,
    POUT, PIN1, EMBED, STEM1, STEM0, PIN0, SMALL, STEM1, PIN1, PIN2, EMBED, STEM0, STEM1, EMBED,
    STEM1, PIN2,
)


def kernel(in_names, out_names, scratch_names, *refs):
    names = in_names + out_names + scratch_names
    r = dict(zip(names, refs))
    sums = {name: {} for name in GRADS}
    for name in names:
        kind, _, which = name.partition("_")
        if which in sums and kind in KINDS:
            sums[which][KINDS[kind]] = r.pop(name)
    for refs in sums.values():
        refs["arrive"] = [refs.pop(kind) for kind in sorted(refs) if kind.startswith("arrive")]
    run(sums=sums, **r)


def run(
    features, stem_weight, group_gain, group_bias, embed_weight, first_gain, first_bias,
    project_in, project_out, second_gain, second_bias, up_weight, up_bias, down_weight,
    valid_mask, slot_slice, cotangent,
    block_out, features_grad, o_small,
    feat, stem, std, wstat, embed, pin, pout, up, down, gvec, xhs, dgs, act, gst,
    sbuf, rbuf, res1, xh1, rs1, n1, q, k, v, probs, heads, mixed, res2, xh2, rs2,
    n2, hid, branch, preg, own, csend, crecv, xsend, xrecv, mb, pg,
    sm, smr, send_sems, recv_sems, local_sems, sums,
):
    place = Place()
    net = Net(place, send_sems, recv_sems, local_sems)
    x, c = place.x, place.c
    R = cotangent.shape[0]
    L = feat.shape[0]
    D = up.shape[0]
    own_rows = pl.multiple_of(c * R, 16)
    sib_rows = pl.multiple_of((1 - c) * R, 16)

    def block(m):
        return pl.ds(pl.multiple_of(m * R, 16), R)

    barrier = pltpu.get_barrier_semaphore()
    peers = [place.sib] + [place.partner(name)[1] for name in "xyaw"]
    for peer in peers:
        pl.semaphore_signal(barrier, inc=1, device_id=peer, device_id_type=MESH)

    def greet():
        peer = place.partner("b")[1]
        pl.semaphore_signal(barrier, inc=1, device_id=peer, device_id_type=MESH)

    net.by(True, greet)
    l_stem = net.local(stem_weight, stem.at[0])
    l_feat = net.local(features.at[pl.ds(pl.multiple_of(x * L, 16), L)], feat)
    l_embed = net.local(embed_weight, embed.at[0])
    l_cot = net.local(cotangent, branch.at[block(place.m)])
    l_pin = net.local(project_in, pin.at[0])
    l_pout = net.local(project_out, pout.at[0])
    l_up = net.local(up_weight, up)
    l_down = net.local(down_weight, down)
    gvec[0, 0:1, :] = group_gain[...].reshape(1, -1)
    gvec[0, 1:2, :] = group_bias[...].reshape(1, -1)
    pl.semaphore_wait(barrier, len(peers) + place.inner.astype(jnp.int32))

    c_gvec = net.send(gvec.at[0], gvec.at[1], place.far)

    def halves(weight, kept, pieces):
        rows = weight.shape[0] // pieces // 2
        for t in range(pieces):
            at = pl.ds(pl.multiple_of((2 * t + place.y) * rows, 16), rows)
            yield kept.at[1, at], net.send(weight.at[at], kept.at[1, at], place.far)

    stem_half = list(halves(stem_weight, stem, 2))
    embed_half = list(halves(embed_weight, embed, 1))
    pin_half = list(halves(project_in, pin, pin.shape[1] // (3 * HEAD_DIM)))
    pout_half = list(halves(project_out, pout, 1))
    c_cot = [
        net.send(cotangent, branch.at[block(place.m)], device) for device in (place.far, place.sib)
    ]

    def pass_on(half):
        ref, copy = half
        copy.wait_recv()
        return net.send(ref, ref, place.y_device)

    slices = valid_mask.shape[0]
    lengths = jnp.sum(valid_mask[...].astype(F32), axis=1, keepdims=True)
    mine = lax.broadcasted_iota(jnp.int32, (slices, 1), 0) == slot_slice[x]
    length = jnp.sum(jnp.where(mine, lengths, 0.0), axis=0, keepdims=True)

    def valid_rows(start, count):
        at = (lax.broadcasted_iota(jnp.int32, (count, 1), 0) + start).astype(F32)
        return jnp.where(at < length, 1.0, 0.0)

    key_valid = jnp.where(
        lax.broadcasted_iota(jnp.int32, (1, L), 1).astype(F32) < length, 1.0, 0.0
    )
    score_scale = HEAD_DIM ** (-0.5)
    key_scale = key_valid * score_scale
    key_shift = (key_valid - 1.0) * 1e9

    channels = stem.shape[2]
    same = (
        lax.div(lax.broadcasted_iota(jnp.int32, (channels, channels), 0), GROUP)
        == lax.div(lax.broadcasted_iota(jnp.int32, (channels, channels), 1), GROUP)
    )
    same = jnp.where(same, 1.0, 0.0)

    def group_sum(values):
        wide = jnp.broadcast_to(values, (8, channels))
        return dot(wide, same, precision=lax.Precision.HIGHEST)[0:1]

    def standardize(j):
        w = stem[j].astype(F32)
        average = jnp.sum(w, axis=0, keepdims=True) * (1.0 / w.shape[0])
        w = w - average
        scale = lax.rsqrt(jnp.sum(w * w, axis=0, keepdims=True) * (1.0 / w.shape[0]) + 1e-5)
        std[j] = (w * scale).astype(BF16)
        wstat[j, 0:1, :] = average
        wstat[j, 1:2, :] = scale

    tile_rows = [(t * R, R) for t in range(L // R)]

    def stem_forward(j):
        count = 1.0 / (length * GROUP)
        total = jnp.zeros((1, channels), F32)
        for at, size in tile_rows:
            s = dot(feat[at : at + size, :], std[j])
            xhs[j, at : at + size, :] = s
            total = total + jnp.sum(s * valid_rows(at, size), axis=0, keepdims=True)
        average = group_sum(total) * count
        total = jnp.zeros((1, channels), F32)
        for at, size in tile_rows:
            s = xhs[j, at : at + size, :] - average
            total = total + jnp.sum(s * s * valid_rows(at, size), axis=0, keepdims=True)
        scale = lax.rsqrt(group_sum(total) * count + 1e-5)
        gst[j, 0:1, :] = scale
        for at, size in tile_rows:
            xh = (xhs[j, at : at + size, :] - average) * scale
            xhs[j, at : at + size, :] = xh
            value, slope = gelu_parts(xh * gvec[j, 0:1, :] + gvec[j, 1:2, :])
            act[j, at : at + size, :] = value.astype(BF16)
            dgs[j, at : at + size, :] = slope

    l_stem.wait()
    standardize(0)
    c_stem = [pass_on(stem_half[0])]
    l_feat.wait()
    stem_forward(0)
    c_stem.append(pass_on(stem_half[1]))
    c_gvec.wait_recv()
    c_embed = pass_on(embed_half[0])
    for copy in c_stem:
        copy.wait_recv()
    standardize(1)
    stem_forward(1)
    l_embed.wait()
    c_embed.wait_recv()

    def core_sum(product):
        xsend[0] = product(sib_rows).astype(BF16)
        copy = net.send(xsend.at[0], xrecv.at[0], place.sib)
        mine = product(own_rows)
        copy.wait_recv()
        net.sent(copy)
        return mine

    def embed_product(start):
        rows = pl.ds(start, R)
        return dot(act[0, rows, :], embed[0]) + dot(act[1, rows, :], embed[1])

    res1[...] = core_sum(embed_product)

    step = R // 2

    def layer_norm(res, other, add, gain, bias, xh_ref, scale_ref, out_ref, out_start, made):
        gain, bias = gain[...].reshape(1, -1), bias[...].reshape(1, -1)
        for t in range(2):
            rows = slice(t * step, (t + 1) * step)
            value = res[rows, :] + other[rows, :].astype(F32)
            if add is not None:
                value = value + add[rows, :]
            res[rows, :] = value
            average = jnp.sum(value, axis=1, keepdims=True) * (1.0 / D)
            value = value - average
            scale = lax.rsqrt(jnp.sum(value * value, axis=1, keepdims=True) * (1.0 / D) + 1e-6)
            xh = value * scale
            xh_ref[rows, :] = xh
            scale_ref[rows, :] = scale
            at = pl.ds(out_start + t * step, step)
            out_ref[at, :] = (xh * gain + bias).astype(BF16)
            made(at)

    layer_norm(
        res1, xrecv.at[0], None, first_gain, first_bias, xh1, rs1, n1, own_rows, lambda at: None
    )
    c_n1 = net.send(n1.at[pl.ds(own_rows, R)], n1.at[pl.ds(own_rows, R)], place.sib)
    l_pin.wait()
    c_n1.wait_recv()

    per_shard = pin.shape[1] // (3 * HEAD_DIM)

    width = 3 * HEAD_DIM
    pin_y = [net.plan(ref, ref, place.y_device) for ref, _ in pin_half]

    def pass_pin(i):
        pin_half[i][1].wait_recv()
        pin_y[i].start()

    def attend(h, carry):
        j, i = lax.div(h, per_shard), lax.rem(h, per_shard)
        for at in range(1, per_shard):

            @pl.when(h == at)
            def _():
                pass_pin(at)

        for at in range(per_shard):

            @pl.when(h == per_shard + at)
            def _():
                pin_y[at].wait_recv()

        @pl.when(h == per_shard + 1)
        def _():
            pout_half[0][1].wait_recv()
            pout_y.start()

        weight = pin[j, pl.ds(pl.multiple_of(i * width, 16), width), :]
        for at, size in tile_rows:
            packed = dot(n1[at : at + size, :], weight, 1, 1).astype(BF16)
            for t, ref in enumerate((q, k, v)):
                ref[h, at : at + size, :] = packed[:, t * HEAD_DIM : (t + 1) * HEAD_DIM]
        for at, size in tile_rows:
            s = dot(q[h, at : at + size, :], k[h], 1, 1) * key_scale + key_shift
            s = jnp.exp(s - jnp.max(s, axis=1, keepdims=True))
            p = (s * (1.0 / jnp.sum(s, axis=1, keepdims=True))).astype(BF16)
            probs[h, at : at + size, :] = p
            heads[h, at : at + size, :] = dot(p, v[h]).astype(BF16)
        return carry

    pass_pin(0)
    pout_y = net.plan(pout_half[0][0], pout_half[0][0], place.y_device)
    lax.fori_loop(0, 2 * per_shard, attend, 0)

    def side_by_side(pieces, store):
        at = 0
        while at < len(pieces):
            pair = pieces[at : at + 2]
            value = pair[0] if len(pair) == 1 else jnp.concatenate(pair, axis=1)
            store(slice(at * HEAD_DIM, at * HEAD_DIM + value.shape[1]), value)
            at += 2

    def store_mixed(lanes, value):
        mixed[:, lanes] = value

    side_by_side([heads[h] for h in range(2 * per_shard)], store_mixed)
    l_pout.wait()
    pout_y.wait_recv()
    out_width = pout.shape[1]

    def out_product(start):
        rows = pl.ds(start, R)
        return dot(mixed[rows, :], pout[...].reshape(-1, D))

    res2[...] = core_sum(out_product)
    c_n2 = []
    layer_norm(
        res2, xrecv.at[0], res1, second_gain, second_bias, xh2, rs2, n2,
        pl.multiple_of(place.m * R, 16),
        lambda at: c_n2.append(net.send(n2.at[at], n2.at[at], place.far)),
    )
    mine = block(place.m)
    c_n2_sib = net.send(n2.at[mine], n2.at[mine], place.sib)

    l_cot.wait()
    l_up.wait()
    l_down.wait()
    sm[...] = jnp.zeros_like(sm)

    def part(m, t):
        return pl.ds(pl.multiple_of(m * R + t * step, 16), step)

    def feed(m, t):
        rows = part(m, t)
        pre = dot(n2[rows, :], up[...]) + up_bias[...].reshape(1, -1)
        value, slope = gelu_parts(pre)
        hid[rows, :] = value.astype(BF16)
        grad = (dot(branch[rows, :], down[...], 1, 1) * slope).astype(BF16)
        preg[rows, :] = grad
        sm[4:5, :] = sm[4:5, :] + jnp.sum(grad.astype(F32), axis=0, keepdims=True)
        return dot(grad, up[...], 1, 1)

    def out_part(m):
        return dot(hid[block(m), :], down[...])

    def mask_branch(m, own_slot):
        rows = block(m)
        start = lax.rem(m, 2) * R
        branch[rows, :] = (
            branch[rows, :].astype(F32) * valid_of(own_slot, start)
        ).astype(BF16)

    mine_far = lax.broadcasted_iota(jnp.int32, (slices, 1), 0) == slot_slice[1 - x]
    far_length = jnp.sum(jnp.where(mine_far, lengths, 0.0), axis=0, keepdims=True)

    def valid_of(own_slot, start):
        at = (lax.broadcasted_iota(jnp.int32, (R, 1), 0) + start).astype(F32)
        return jnp.where(at < (length if own_slot else far_length), 1.0, 0.0)

    c_cot[0].wait_recv()
    f_rows = block(place.far_m)
    c_cot_fwd = net.send(branch.at[f_rows], branch.at[f_rows], place.sib)
    mask_branch(place.m, True)

    def feed_near(i, carry):
        t = lax.rem(i, 2)

        @pl.when(i == 2)
        def _():
            c_cot[1].wait_recv()
            c_n2_sib.wait_recv()
            mask_branch(place.sib_m, True)

        term = feed(jnp.where(i < 2, place.m, place.sib_m), t)
        rows = pl.ds(pl.multiple_of(t * step, 16), step)

        @pl.when(i < 2)
        def _():
            own[1, rows, :] = term

        @pl.when(i >= 2)
        def _():
            csend[1, 0, rows, :] = term.astype(BF16)

        return carry

    lax.fori_loop(0, 4, feed_near, 0)
    c_core = {}
    c_core[1, 0] = net.send(csend.at[1, 0], crecv.at[1, 0], place.sib)
    csend[0, 0] = out_part(place.sib_m).astype(BF16)
    c_core[0, 0] = net.send(csend.at[0, 0], crecv.at[0, 0], place.sib)
    own[0] = out_part(place.m)
    c_cot_fwd.wait_recv()
    net.sent(c_cot_fwd)
    mask_branch(place.far_sib_m, False)
    mask_branch(place.far_m, False)
    c_far = {}

    def feed_far(t):
        rows = pl.ds(t * step, step)
        c_n2[t].wait_recv()
        passed = n2.at[part(place.far_m, t)]
        passing = net.send(passed, passed, place.sib)
        sbuf[rows, 0:D] = feed(place.far_m, t)
        passing.wait_recv()
        csend[1, 1, rows, :] = feed(place.far_sib_m, t).astype(BF16)
        c_core[1, 1, t] = net.send(csend.at[1, 1, rows], crecv.at[1, 1, rows], place.sib)

    def feed_return(t):
        rows = pl.ds(t * step, step)
        c_core[1, 1, t].wait_recv()
        xsend[1, rows, :] = (sbuf[rows, 0:D] + crecv[1, 1, rows, :].astype(F32)).astype(BF16)
        c_far[1, t] = net.send(xsend.at[1, rows], xrecv.at[1, rows], place.far)

    feed_far(0)
    feed_return(0)
    feed_far(1)

    def result_send():
        csend[0, 1] = out_part(place.far_sib_m).astype(BF16)
        c_core[0, 1] = net.send(csend.at[0, 1], crecv.at[0, 1], place.sib)
        sbuf[:, 0:D] = out_part(place.far_m)
        c_core[0, 1].wait_recv()
        xsend[0] = (sbuf[:, 0:D] + crecv[0, 1].astype(F32)).astype(BF16)
        c_far[0] = net.send(xsend.at[0], xrecv.at[0], place.far)

    summed = {name: Summed(net, place, AWAY[name], BACK[name], **sums[name]) for name in GRADS}

    def keep(name, slot, at, value):
        ref = sums[name]["grad"]
        rows = ref.shape[-2]
        for t in range(value.shape[0] // rows):
            part = (at + t) // 2, (at + t) % 2
            ref[part if slot is None else (slot,) + part] = value[
                t * rows : (t + 1) * rows
            ].astype(BF16)

    half = D // 2
    for i, name in enumerate(("down0", "down1")):
        keep(name, None, 0, dot(hid[:, i * half : (i + 1) * half], branch[...], 0, 0))
        summed[name].start()
        if i == 0:
            feed_return(1)
    for i, name in enumerate(("up0", "up1")):
        keep(name, None, 0, dot(n2[:, i * half : (i + 1) * half], preg[...], 0, 0))
        summed[name].start()

    def norm_back(grad_of, gain, xh_ref, scale_ref, kept, out_ref, out_start, row):
        gain = gain[...].reshape(1, -1)
        gain_sum = jnp.zeros((1, D), F32)
        bias_total = jnp.zeros((1, D), F32)
        for t in range(2):
            rows = slice(t * step, (t + 1) * step)
            dy, through = grad_of(rows)
            xh = xh_ref[rows, :]
            gain_sum = gain_sum + jnp.sum(dy * xh, axis=0, keepdims=True)
            bias_total = bias_total + jnp.sum(dy, axis=0, keepdims=True)
            dy = dy * gain
            mean_one = jnp.sum(dy, axis=1, keepdims=True) * (1.0 / D)
            mean_two = jnp.sum(dy * xh, axis=1, keepdims=True) * (1.0 / D)
            dx = through + scale_ref[rows, :] * (dy - mean_one - xh * mean_two)
            if kept is not None:
                kept[rows, :] = dx
            out_ref[pl.ds(out_start + t * step, step), :] = dx.astype(BF16)
        sm[row : row + 1, :] = gain_sum
        sm[row + 1 : row + 2, :] = bias_total

    own_part = pl.ds(own_rows, R)
    sg2, eb, sg = res1, mb, act
    copies = {}
    locals_left = []
    tasks = {}

    def task(number):
        def enter(function):
            tasks[number] = function

        return enter

    @task(NORM2)
    def norm2():
        c_core[1, 0].wait_recv()

        def grad_of(rows):
            c_far[1, rows.start // step].wait_recv()
            dy = own[1, rows, :] + crecv[1, 0, rows, :].astype(F32) + xrecv[1, rows, :].astype(F32)
            at = pl.ds(pl.multiple_of(place.m * R, 16) + rows.start, step)
            return dy, branch[at, :].astype(F32)

        norm_back(grad_of, second_gain, xh2, rs2, sg2, mb, own_rows, 2)
        copies["mb"] = net.send(mb.at[own_part], mb.at[own_part], place.sib)

    @task(RESULT)
    def result():
        c_core[0, 0].wait_recv()
        c_far[0].wait_recv()
        net.sent(c_core[0, 0])
        for t in range(2):
            rows = slice(t * step, (t + 1) * step)
            value = (
                res2[rows, :]
                + own[0, rows, :]
                + crecv[0, 0, rows, :].astype(F32)
                + xrecv[0, rows, :].astype(F32)
            )
            csend[0, 0, rows, :] = (value * valid_rows(own_rows + t * step, step)).astype(BF16)
        locals_left.append(net.local(csend.at[0, 0], block_out))

    @task(MIXED_BACK)
    def mixed_back():
        copies["mb"].wait_recv()
        value = dot(mixed[...], mb[...], 0, 0)
        shard = pout.shape[1]
        for j in range(2):
            rows = value[j * shard : (j + 1) * shard]
            for i in range(2):
                keep("pout", j, 2 * i, rows[:, i * half : (i + 1) * half])
        for at, size in tile_rows:
            value = dot(mb[at : at + size, :], pout[...].reshape(-1, D), 1, 1).astype(BF16)
            for h in range(2 * per_shard):
                heads[h, at : at + size, :] = value[:, h * HEAD_DIM : (h + 1) * HEAD_DIM]

    def head_back(h, carry):
        p = probs[h]
        dp = dot(heads[h], v[h], 1, 1)
        v[h] = dot(p, heads[h], 0, 0).astype(BF16)
        p = p.astype(F32)
        ds = (p * (dp - jnp.sum(p * dp, axis=1, keepdims=True))).astype(BF16)
        dq = (dot(ds, k[h]) * score_scale).astype(BF16)
        k[h] = (dot(ds, q[h], 0, 0) * score_scale).astype(BF16)
        q[h] = dq
        return carry

    def pin_back(j):
        lax.fori_loop(per_shard * j, per_shard * (j + 1), head_back, 0)

        def store_pg(lanes, value):
            pg[j, :, lanes] = value

        pieces = [ref[per_shard * j + h] for h in range(per_shard) for ref in (q, k, v)]
        side_by_side(pieces, store_pg)
        value = dot(pg[j], n1[...], 0, 0)
        wide = D // 6
        for i in range(6):
            keep("pin%d" % (i // 2), j, 2 * (i % 2), value[:, i * wide : (i + 1) * wide])

    @task(HEADS_FAR)
    def heads_far():
        pin_back(1)

    @task(HEADS_OWN)
    def heads_own():
        pin_back(0)

    @task(NORM1_SEND)
    def norm1_send():
        def product(start):
            rows = pl.ds(start, R)
            return dot(pg[0, rows, :], pin[0]) + dot(pg[1, rows, :], pin[1])

        width = pl.ds(0, D)
        sbuf[:, width] = product(sib_rows)
        copies["n1"] = net.send(sbuf.at[:, width], rbuf.at[:, width], place.sib)
        xh2[...] = product(own_rows)

    @task(NORM1)
    def norm1():
        copies["n1"].wait_recv()
        net.sent(copies["n1"])

        def grad_of(rows):
            return xh2[rows, :] + rbuf[rows, 0:D], sg2[rows, :]

        net.sent(copies["mb"])
        norm_back(grad_of, first_gain, xh1, rs1, None, eb, own_rows, 0)
        copies["eb"] = net.send(eb.at[own_part], eb.at[own_part], place.sib)

    def embed_back(j):
        keep("embed", j, 0, dot(act[j], eb[...], 0, 0))

    cin = feat.shape[1]
    square = pl.ds(0, cin // 4), pl.ds(0, channels)
    spares = [ref.at[square] for ref in (xh1, xh2, res1, own.at[1])]

    def stem_back(j):
        gain_sum = jnp.zeros((1, channels), F32)
        bias_total = jnp.zeros((1, channels), F32)
        for at, size in tile_rows:
            dz = dot(eb[at : at + size, :], embed[j], 1, 1) * dgs[j, at : at + size, :]
            dgs[j, at : at + size, :] = dz
            gain_sum = gain_sum + jnp.sum(dz * xhs[j, at : at + size, :], axis=0, keepdims=True)
            bias_total = bias_total + jnp.sum(dz, axis=0, keepdims=True)
        sm[5 + j : 6 + j, 0:channels] = gain_sum
        sm[5 + j : 6 + j, channels : 2 * channels] = bias_total
        gain = gvec[j, 0:1, :]
        count = 1.0 / (length * GROUP)
        mean_one = group_sum(bias_total * gain) * count
        mean_two = group_sum(gain_sum * gain) * count
        for at, size in tile_rows:
            part = dgs[j, at : at + size, :] * gain - valid_rows(at, size) * (
                mean_one + xhs[j, at : at + size, :] * mean_two
            )
            sg[j, at : at + size, :] = (part * gst[j, 0:1, :]).astype(BF16)
        average, scale = wstat[j, 0:1, :], wstat[j, 1:2, :]
        sum_one = jnp.zeros((1, channels), F32)
        sum_two = jnp.zeros((1, channels), F32)
        quarter = cin // 4
        for t in range(4):
            rows = slice(t * quarter, (t + 1) * quarter)
            grad = dot(feat[:, rows], sg[j], 0, 0)
            spare = spares[t]
            spare[...] = grad
            xh = (stem[j, rows, :].astype(F32) - average) * scale
            sum_one = sum_one + jnp.sum(grad, axis=0, keepdims=True)
            sum_two = sum_two + jnp.sum(grad * xh, axis=0, keepdims=True)
        sum_one = sum_one * (1.0 / cin)
        sum_two = sum_two * (1.0 / cin)
        for t in range(4):
            rows = slice(t * quarter, (t + 1) * quarter)
            xh = (stem[j, rows, :].astype(F32) - average) * scale
            value = (spares[t][...] - sum_one - xh * sum_two) * scale
            for i in range(2):
                lanes = slice(i * channels // 2, (i + 1) * channels // 2)
                keep("stem%d" % i, j, t, value[:, lanes])

    @task(STEM_FAR)
    def stem_far():
        copies["eb"].wait_recv()
        embed_back(1)
        stem_back(1)

    @task(STEM_OWN)
    def stem_own():
        embed_back(0)
        stem_back(0)
        small("core")

    def feature_product(start):
        rows = pl.ds(start, R)
        return dot(sg[0, rows, :], std[0], 1, 1) + dot(sg[1, rows, :], std[1], 1, 1)

    @task(FEATURES_SEND)
    def features_send():
        sbuf[...] = feature_product(sib_rows)
        copies["feat"] = net.send(sbuf, rbuf, place.sib)

    @task(FEATURES_SUM)
    def features_sum():
        copies["feat"].wait_recv()
        net.sent(copies["feat"])
        sbuf[...] = feature_product(own_rows) + rbuf[...]
        locals_left.append(net.local(sbuf, features_grad))

    small_at = {"core": place.sib}
    for name in "xyaw":
        small_at[name] = place.partner(name)[1]
    small_order = tuple(small_at)

    def small(name):
        copies["small"] = net.send(sm, smr.at[small_order.index(name)], small_at[name])

    def small_step(i):
        copies["small"].wait_recv()
        net.sent(copies["small"])
        if small_order[i] in ("core", "x"):
            sm[0:4, :] = sm[0:4, :] + smr[i, 0:4, :]
            if small_order[i] == "x":
                sm[5:6, :] = sm[5:6, :] + smr[i, 6:7, :]
        else:
            sm[...] = sm[...] + smr[i]
        if i + 1 < len(small_order):
            small(small_order[i + 1])
        else:
            o_small[...] = sm[...]

    small_next = list(range(len(small_order)))
    for what in ORDER:
        if what in tasks:
            tasks.pop(what)()
        elif what == SMALL:
            small_step(small_next.pop(0))
        elif what == ~RESULT:
            result_send()
        elif what < 0:
            summed[GRADS[~what]].start()
        else:
            summed[GRADS[what]].step()
    assert not tasks and not small_next
    for one in summed.values():
        one.step_all()
    for copy in locals_left:
        copy.wait()
    net.finish()


def finish(in_names, out_names, *refs):
    names = in_names + out_names
    r = dict(zip(names, refs))
    rest = refs[len(names) :]
    sems, passed, rest = rest[0], rest[1:3], rest[3:]
    held, made = rest[: len(GRADS)], rest[len(GRADS) :]
    made = dict(zip(("up", "down", "pout", "pin", "embed", "stem"), made))
    count = [0]
    going = []

    def move(src, dst):
        copy = pltpu.make_async_copy(src, dst, sems.at[count[0]])
        count[0] += 1
        copy.start()
        return copy

    order = GRADS
    held = dict(zip(GRADS, held))
    as_is = ("block_out", "features_grad")
    passing = [move(r["i_" + name], ref) for name, ref in zip(as_is, passed)]
    arriving = {name: move(r["i_" + name], held[name]) for name in order}
    small = r["i_small"]
    for i, name in enumerate(("g1", "b1", "g2", "b2", "ub")):
        r["o_" + name][...] = small[i, :]
    channels = r["o_gain"].shape[0]
    r["o_gain"][...] = small[5, 0:channels]
    r["o_shift"][...] = small[5, channels : 2 * channels]
    for name, ref, copy in zip(as_is, passed, passing):
        copy.wait()
        going.append(move(ref, r["o_" + name]))
    for name in order:
        arriving[name].wait()
        part = held[name]
        parts, rows, columns = part.shape
        name, number = name.rstrip("012"), int(name[-1]) if name[-1] in "012" else 0
        to = made[name]
        top, left = 0, 0
        if name in ("up", "down"):
            top, down = number * parts * rows, parts
        else:
            down = to.shape[0] // rows
            left = number * (parts // down) * columns
        for t in range(parts):
            at = top + t % down * rows
            lane = left + t // down * columns
            to[at : at + rows, lane : lane + columns] = part[t].astype(F32)
        if name in ("up", "down"):
            rows = pl.ds(top, parts * rows)
            going.append(move(to.at[rows], r["o_" + name].at[rows]))
        elif number == dict(pin=2, stem=1).get(name, 0):
            going.append(move(to, r["o_" + name]))
    for copy in going:
        copy.wait()


def body(
    features, stem_weight, group_gain, group_bias, embed_weight, first_gain, first_bias,
    project_in, project_out, second_gain, second_bias, up_weight, up_bias, down_weight,
    valid_mask, slot_slice, cotangent, *, dp,
):
    slots = slot_slice.shape[0]
    L = features.shape[0] // slots
    R = cotangent.shape[0]
    cin, channels = stem_weight.shape
    D = cotangent.shape[1]
    wide_in = project_in.shape[1]
    project_in = project_in.T
    out_rows = project_out.shape[0]
    hidden = up_weight.shape[1]
    heads = 2 * wide_in // (3 * HEAD_DIM)
    hbm = pl.BlockSpec(memory_space=pl.ANY)
    vmem = pl.BlockSpec(memory_space=pltpu.VMEM)
    smem = pl.BlockSpec(memory_space=pltpu.SMEM)
    in_specs = dict(
        features=hbm, stem_weight=hbm, group_gain=vmem, group_bias=vmem, embed_weight=hbm,
        first_gain=vmem, first_bias=vmem, project_in=hbm, project_out=hbm, second_gain=vmem,
        second_bias=vmem, up_weight=hbm, up_bias=vmem, down_weight=hbm, valid_mask=vmem,
        slot_slice=smem, cotangent=hbm,
    )
    parts = dict(
        up0=(D // 8, hidden),
        up1=(D // 8, hidden),
        down0=(hidden // 8, D),
        down1=(hidden // 8, D),
        pout=(out_rows // 2, D // 2),
        pin0=(wide_in // 2, D // 6),
        pin1=(wide_in // 2, D // 6),
        pin2=(wide_in // 2, D // 6),
        embed=(channels // 4, D),
        stem0=(cin // 4, channels // 2),
        stem1=(cin // 4, channels // 2),
    )
    outs = dict(
        block_out=((R, D), BF16, hbm),
        features_grad=((R, cin), F32, hbm),
        o_small=((8, D), F32, vmem),
    )
    for name in GRADS:
        outs["o_" + name] = ((2, 2) + parts[name], BF16, hbm)
    scratch = dict(
        feat=((L, cin), BF16), stem=((2, cin, channels), BF16), std=((2, cin, channels), BF16),
        wstat=((2, 8, channels), F32), embed=((2, channels, D), BF16), pin=((2, wide_in, D), BF16),
        pout=((2, out_rows, D), BF16), up=((D, hidden), BF16), down=((hidden, D), BF16),
        gvec=((2, 8, channels), F32), xhs=((2, L, channels), F32), dgs=((2, L, channels), F32),
        act=((2, L, channels), BF16), gst=((2, 8, channels), F32),
        sbuf=((R, cin), F32), rbuf=((R, cin), F32), res1=((R, D), F32), xh1=((R, D), F32),
        rs1=((R, 1), F32), n1=((L, D), BF16), q=((heads, L, HEAD_DIM), BF16),
        k=((heads, L, HEAD_DIM), BF16), v=((heads, L, HEAD_DIM), BF16), probs=((heads, L, L), BF16),
        heads=((heads, L, HEAD_DIM), BF16), mixed=((L, heads * HEAD_DIM), BF16),
        res2=((R, D), F32), xh2=((R, D), F32), rs2=((R, 1), F32), n2=((4 * R, D), BF16),
        hid=((4 * R, hidden), BF16), branch=((4 * R, D), BF16), preg=((4 * R, hidden), BF16),
        own=((2, R, D), F32), csend=((2, 2, R, D), BF16),
        crecv=((2, 2, R, D), BF16), xsend=((2, R, D), BF16), xrecv=((2, R, D), BF16),
        mb=((L, D), BF16), pg=((2, L, wide_in), BF16),
    )
    for name in GRADS:
        size = {dim: 2 for dim in "xyb" if dim in AWAY[name]}
        scratch["g_" + name] = (tuple(size.values()) + parts[name], BF16)
        for level, dim in enumerate(AWAY[name]):
            if dim != "a":
                size[dim] = 1
            scratch["r%d_" % level + name] = (tuple(size.values()) + parts[name], BF16)
    scratch.update(sm=((8, D), F32), smr=((5, 8, D), F32))
    copies = 144
    shapes = [pltpu.VMEM(*one) for one in scratch.values()]
    shapes += [pltpu.SemaphoreType.DMA((copies,)) for _ in range(2)]
    shapes += [pltpu.SemaphoreType.DMA((24,))]
    names = tuple(scratch) + ("send_sems", "recv_sems", "local_sems")
    results = pl.pallas_call(
        functools.partial(kernel, tuple(in_specs), tuple(outs), names),
        out_shape=[jax.ShapeDtypeStruct(shape, kind) for shape, kind, _ in outs.values()],
        in_specs=list(in_specs.values()),
        out_specs=[spec for _, _, spec in outs.values()],
        scratch_shapes=shapes,
        compiler_params=pltpu.CompilerParams(
            collective_id=0, has_side_effects=True, vmem_limit_bytes=62 * 2**20
        ),
        name="layer",
    )(
        features, stem_weight, group_gain, group_bias, embed_weight, first_gain, first_bias,
        project_in, project_out, second_gain, second_bias, up_weight, up_bias, down_weight,
        valid_mask, slot_slice, cotangent,
    )
    out = dict(zip(outs, results))

    wide = {name: out["o_" + name].reshape((4,) + parts[name]) for name in GRADS}
    small = out["o_small"]
    bit = NEAR
    if bit < dp:
        wide = {name: part.astype(F32) for name, part in wide.items()}
    while bit < dp:
        pairs = [(i, i ^ bit) for i in range(dp)]
        wide, small = jax.tree.map(
            lambda part: part + lax.ppermute(part, "dp", pairs), (wide, small)
        )
        bit *= 2

    inputs = {"i_" + name: wide[name] for name in GRADS}
    inputs.update(i_block_out=out["block_out"], i_features_grad=out["features_grad"], i_small=small)
    whole = dict(
        up=(D, hidden), down=(hidden, D), pout=(out_rows, D), pin=(wide_in, D),
        embed=(channels, D), stem=(cin, channels),
    )
    finals = dict(o_block_out=((R, D), BF16, hbm), o_features_grad=((R, cin), F32, hbm))
    for name, shape in whole.items():
        finals["o_" + name] = (shape, F32, hbm)
    for name in ("g1", "b1", "g2", "b2"):
        finals["o_" + name] = ((D,), F32, vmem)
    finals["o_ub"] = ((hidden,), F32, vmem)
    for name in ("gain", "shift"):
        finals["o_" + name] = ((channels,), F32, vmem)
    moved = pl.pallas_call(
        functools.partial(finish, tuple(inputs), tuple(finals)),
        out_shape=[jax.ShapeDtypeStruct(shape, kind) for shape, kind, _ in finals.values()],
        in_specs=[hbm] * (len(inputs) - 1) + [vmem],
        out_specs=[spec for _, _, spec in finals.values()],
        scratch_shapes=[pltpu.SemaphoreType.DMA((28,))]
        + [pltpu.VMEM((R, D), BF16), pltpu.VMEM((R, cin), F32)]
        + [pltpu.VMEM(wide[name].shape, wide[name].dtype) for name in GRADS]
        + [pltpu.VMEM(shape, F32) for shape in whole.values()],
        compiler_params=pltpu.CompilerParams(vmem_limit_bytes=62 * 2**20),
        name="finish",
    )(*inputs.values())
    done = dict(zip(finals, moved))
    return (
        done["o_block_out"],
        done["o_features_grad"],
        done["o_stem"],
        done["o_gain"],
        done["o_shift"],
        done["o_embed"],
        done["o_g1"],
        done["o_b1"],
        done["o_pin"].T,
        done["o_pout"],
        done["o_g2"],
        done["o_b2"],
        done["o_up"],
        done["o_ub"],
        done["o_down"],
    )


def solution(mesh):
    return jax.shard_map(
        functools.partial(body, dp=mesh.shape["dp"]),
        mesh=mesh,
        in_specs=(
            P("dp", None), P(None, "mp"), P("mp"), P("mp"), P("mp", None), P(), P(),
            P(None, "mp"), P("mp", None), P(), P(), P(None, "mp"), P("mp"), P("mp", None),
            P(), P("dp"), P(("dp", "mp"), None),
        ),
        out_specs=(
            P(("dp", "mp"), None), P(("dp", "mp"), None), P(None, "mp"), P("mp"), P("mp"),
            P("mp", None), P(), P(), P(None, "mp"), P("mp", None), P(), P(), P(None, "mp"),
            P("mp"), P("mp", None),
        ),
        check_vma=False,
    )
```

```python
import functools
import itertools

import jax
import jax.numpy as jnp
from jax import lax
from jax.experimental import pallas as pl
from jax.experimental.pallas import tpu as pltpu
from jax.sharding import PartitionSpec as P

MESH = pl.DeviceIdType.MESH
F32 = jnp.float32
BF16 = jnp.bfloat16
HEAD_DIM = 64
GROUP = 32
NEAR = 8


def dot(left, right, left_dim=1, right_dim=0, precision=None):
    return lax.dot_general(
        left,
        right,
        (((left_dim,), (right_dim,)), ((), ())),
        precision=precision,
        preferred_element_type=F32,
    )


def gelu_parts(z):
    cdf = 0.5 + 0.5 * lax.erf(z * 0.7071067811865476)
    return z * cdf, cdf + z * (jnp.exp(-0.5 * z * z) * 0.3989422804014327)


class Net:
    def __init__(self, place, send_sems, recv_sems, local_sems):
        self.place = place
        self.send_sems, self.recv_sems, self.local_sems = send_sems, recv_sems, local_sems
        self.count, self.local_count, self.unsent = 0, 0, []

    def by(self, who, action):
        if who is None:
            action()
        else:
            pl.when(self.place.inner if who else jnp.logical_not(self.place.inner))(action)

    def plan(self, src, dst, device, who=None):
        copy = pltpu.make_async_remote_copy(
            src_ref=src,
            dst_ref=dst,
            send_sem=self.send_sems.at[self.count],
            recv_sem=self.recv_sems.at[self.count],
            device_id=device,
            device_id_type=MESH,
        )
        self.count += 1
        self.unsent.append((copy, who))
        return copy

    def send(self, src, dst, device, who=None):
        copy = self.plan(src, dst, device, who)
        self.by(who, copy.start)
        return copy

    def sent(self, copy):
        self.unsent = [one for one in self.unsent if one[0] is not copy]
        copy.wait_send()

    def local(self, src, dst, who=None):
        copy = pltpu.make_async_copy(src, dst, self.local_sems.at[self.local_count])
        self.local_count += 1
        self.by(who, copy.start)
        return copy

    def finish(self):
        for copy, who in self.unsent:
            self.by(who, copy.wait_send)


class Summed:
    def __init__(self, net, place, away, back, grad, arrive, out):
        self.net, self.place, self.away, self.back = net, place, away, back
        self.grad, self.arrive, self.out = grad, arrive, out
        self.dims = "xyb"[3 - (len(grad.shape) - 2) :]
        self.fixed = {}
        self.level, self.gathered = 0, None

    def index(self, dims, **more):
        fixed = {**self.fixed, **more}
        return tuple(pl.ds(fixed[dim], 1) if dim in fixed else pl.ds(0, 2) for dim in dims)

    def start(self):
        dim = self.away[self.level]
        bit, partner = self.place.partner(dim)
        inner_only = "a" in self.away[: self.level]
        if dim == "a":
            give, who = self.index(self.dims), False
        else:
            give, who = self.index(self.dims, **{dim: 1 - bit}), True if inner_only else None
            self.fixed[dim] = bit
        self.copy = self.net.send(self.grad.at[give], self.arrive[self.level], partner, who)

    def add(self, arrived):
        for at in itertools.product((0, 1), repeat=len(self.dims)):
            here = dict(zip(self.dims, at))
            if any(here[dim] for dim in self.fixed):
                continue
            where = tuple(self.fixed.get(dim, here[dim]) for dim in self.dims)
            value = self.grad[where].astype(F32) + arrived[at].astype(F32)
            self.grad[where] = value.astype(BF16)

    def held(self):
        return self.out.at[self.index("yb")]

    def share(self):
        dim = self.back[len(self.gathered)]
        _, partner = self.place.partner(dim)
        source = self.held()
        if not self.gathered:
            at = self.index("yb")
            source = self.grad.at[(0,) + at if "x" in self.dims else at]
        self.copy = self.net.send(source, self.held(), partner, True)
        if dim == "a" and len(self.gathered) < 2:
            _, partner = self.place.partner(self.back[2])
            self.last = self.net.plan(self.held(), self.held(), partner)
            self.net.by(True, self.last.start)

    def step(self):
        copy = self.copy
        if self.gathered is None:
            arrived = self.arrive[self.level]

            def take():
                copy.wait_recv()
                self.add(arrived)

            self.net.by(True if "a" in self.away[: self.level + 1] else None, take)
            self.level += 1
            if self.level < len(self.away):
                self.start()
                return
            self.fixed.pop("x", None)
            self.gathered = []
            at = self.index("yb")
            source = self.grad.at[(0,) + at if "x" in self.dims else at]
            self.own = self.net.local(source, self.held(), True)
            self.share()
            return
        dim = self.back[len(self.gathered)]
        if dim == "a":
            self.net.by(False, copy.wait_recv)
        elif "a" in self.gathered:
            copy.wait_recv()
        else:
            self.net.by(True, copy.wait_recv)
        if not self.gathered:
            self.net.by(True, self.own.wait)
        self.gathered.append(dim)
        self.fixed.pop(dim, None)
        if len(self.gathered) == 3:
            self.copy = None
        elif dim == "a":
            self.copy = self.last
            self.net.by(False, self.copy.start)
        else:
            self.share()

    def step_all(self):
        while self.copy is not None:
            self.step()


class Place:
    def __init__(self):
        self.d = lax.axis_index("dp")
        self.m = lax.axis_index("mp")
        self.x = lax.div(self.m, 2)
        self.c = lax.rem(self.m, 2)
        self.y = lax.rem(self.d, 2)
        self.zi = lax.div(lax.rem(self.d, NEAR), 2)
        self.sib_m = self.m + 1 - 2 * self.c
        self.far_m = lax.rem(self.m + 2, 4)
        self.far_sib_m = lax.rem(self.sib_m + 2, 4)
        self.sib = (self.d, self.sib_m)
        self.far = (self.d, self.far_m)
        self.y_device = (self.d + 1 - 2 * self.y, self.m)
        self.inner = jnp.logical_or(self.zi == 1, self.zi == 2)
        self.bits = {
            "y": (self.y, 1),
            "a": (lax.rem(self.zi, 2), 2),
            "b": (lax.div(self.zi, 2), 2),
            "w": (lax.div(self.zi, 2), 4),
        }

    def partner(self, name):
        if name == "x":
            return 0, self.far
        bit, stride = self.bits[name]
        return bit, (self.d + stride - 2 * stride * bit, self.m)


GRADS = ("up0", "up1", "up2", "down0", "down1", "down2", "pout", "pin0", "pin1", "pin2", "embed", "stem0", "stem1")
UP0, UP1, UP2, DOWN0, DOWN1, DOWN2, POUT, PIN0, PIN1, PIN2, EMBED, STEM0, STEM1, SMALL = range(14)
(NORM2, RESULT, MIXED_BACK, HEADS_FAR, HEADS_OWN, NORM1_SEND, NORM1, STEM_FAR, STEM_OWN, FEATURES_SEND,
 FEATURES_SUM) = range(14, 25)
KINDS = dict(g="grad", o="out", r0="arrive0", r1="arrive1", r2="arrive2", r3="arrive3")
AWAY = dict(
    down0="yab",
    down1="yab",
    down2="yab",
    up0="aby",
    up1="yab",
    up2="yab",
    pout="yxab",
    pin0="xaby",
    pin1="xaby",
    pin2="xyab",
    embed="xyab",
    stem0="xyab",
    stem1="xyab",
)
BACK = dict(
    down0="bay",
    down1="bay",
    down2="bay",
    up0="yba",
    up1="yba",
    up2="bay",
    pout="bay",
    pin0="bay",
    pin1="bay",
    pin2="bay",
    embed="bay",
    stem0="yba",
    stem1="bay",
)
ORDER = (
    NORM2, ~RESULT, DOWN0, MIXED_BACK, ~POUT, DOWN1, UP0, HEADS_FAR, ~PIN2, DOWN2, DOWN0,
    HEADS_OWN, ~PIN0, UP1, UP0, DOWN1, UP2, DOWN0, DOWN2, NORM1_SEND, ~PIN1, PIN2, POUT, DOWN1,
    UP1, NORM1, UP0, DOWN0, STEM_FAR, ~EMBED, DOWN2, UP2, PIN0, PIN2, DOWN1, UP0, UP1, STEM_OWN,
    ~STEM0, DOWN0, PIN1, DOWN2, SMALL, FEATURES_SEND, UP2, POUT, PIN0, DOWN1, FEATURES_SUM, ~STEM1,
    RESULT, DOWN0, UP0, PIN2, UP1, DOWN2, UP2, DOWN1, EMBED, PIN0, PIN1, PIN2, DOWN2, POUT, STEM0,
    SMALL, UP1, UP0, EMBED, PIN1, PIN0, UP2, PIN2, STEM1, POUT, STEM0, SMALL, PIN0, PIN1, EMBED,
    POUT, UP2, STEM0, UP1, PIN1, STEM1, EMBED, PIN2, SMALL, STEM0, PIN0, STEM1, EMBED, PIN2, POUT,
    STEM1, STEM0, PIN0, PIN1, SMALL, POUT, STEM1, EMBED, STEM0, PIN1, STEM1, EMBED, STEM0, STEM1,
)


def kernel(in_names, out_names, scratch_names, *refs):
    names = in_names + out_names + scratch_names
    r = dict(zip(names, refs))
    sums = {name: {} for name in GRADS}
    for name in names:
        kind, _, which = name.partition("_")
        if which in sums and kind in KINDS:
            sums[which][KINDS[kind]] = r.pop(name)
    for refs in sums.values():
        refs["arrive"] = [refs.pop(kind) for kind in sorted(refs) if kind.startswith("arrive")]
    run(sums=sums, **r)


def run(
    features, stem_weight, group_gain, group_bias, embed_weight, first_gain, first_bias,
    project_in, project_out, second_gain, second_bias, up_weight, up_bias, down_weight,
    valid_mask, slot_slice, cotangent,
    block_out, features_grad, o_small,
    feat, stem, std, wstat, embed, pin, pout, up, down, gvec, xhs, dgs, act, gst,
    sbuf, rbuf, res1, xh1, rs1, n1, q, k, v, probs, heads, mixed, res2, xh2, rs2,
    n2, hid, branch, preg, own, csend, crecv, xsend, xrecv, mb, pg,
    sm, smr, send_sems, recv_sems, local_sems, sums,
):
    place = Place()
    net = Net(place, send_sems, recv_sems, local_sems)
    x, c = place.x, place.c
    R = cotangent.shape[0]
    L = feat.shape[0]
    D = up.shape[0]
    own_rows = pl.multiple_of(c * R, 16)
    sib_rows = pl.multiple_of((1 - c) * R, 16)

    def block(m):
        return pl.ds(pl.multiple_of(m * R, 16), R)

    barrier = pltpu.get_barrier_semaphore()
    peers = [place.sib] + [place.partner(name)[1] for name in "xyaw"]
    for peer in peers:
        pl.semaphore_signal(barrier, inc=1, device_id=peer, device_id_type=MESH)

    def greet():
        peer = place.partner("b")[1]
        pl.semaphore_signal(barrier, inc=1, device_id=peer, device_id_type=MESH)

    net.by(True, greet)
    l_stem = net.local(stem_weight, stem.at[0])
    l_feat = net.local(features.at[pl.ds(pl.multiple_of(x * L, 16), L)], feat)
    l_embed = net.local(embed_weight, embed.at[0])
    l_cot = net.local(cotangent, branch.at[block(place.m)])
    l_pin = net.local(project_in, pin.at[0])
    l_pout = net.local(project_out, pout.at[0])
    l_up = net.local(up_weight, up)
    l_down = net.local(down_weight, down)
    gvec[0, 0:1, :] = group_gain[...].reshape(1, -1)
    gvec[0, 1:2, :] = group_bias[...].reshape(1, -1)
    pl.semaphore_wait(barrier, len(peers) + place.inner.astype(jnp.int32))

    c_gvec = net.send(gvec.at[0], gvec.at[1], place.far)

    def halves(weight, kept, pieces):
        rows = weight.shape[0] // pieces // 2
        for t in range(pieces):
            at = pl.ds(pl.multiple_of((2 * t + place.y) * rows, 16), rows)
            yield kept.at[1, at], net.send(weight.at[at], kept.at[1, at], place.far)

    stem_half = list(halves(stem_weight, stem, 2))
    embed_half = list(halves(embed_weight, embed, 1))
    pin_half = list(halves(project_in, pin, pin.shape[1] // (3 * HEAD_DIM)))
    pout_half = list(halves(project_out, pout, 1))
    c_cot = [
        net.send(cotangent, branch.at[block(place.m)], device) for device in (place.far, place.sib)
    ]

    def pass_on(half):
        ref, copy = half
        copy.wait_recv()
        return net.send(ref, ref, place.y_device)

    slices = valid_mask.shape[0]
    lengths = jnp.sum(valid_mask[...].astype(F32), axis=1, keepdims=True)
    mine = lax.broadcasted_iota(jnp.int32, (slices, 1), 0) == slot_slice[x]
    length = jnp.sum(jnp.where(mine, lengths, 0.0), axis=0, keepdims=True)

    def valid_rows(start, count):
        at = (lax.broadcasted_iota(jnp.int32, (count, 1), 0) + start).astype(F32)
        return jnp.where(at < length, 1.0, 0.0)

    key_valid = jnp.where(
        lax.broadcasted_iota(jnp.int32, (1, L), 1).astype(F32) < length, 1.0, 0.0
    )
    score_scale = HEAD_DIM ** (-0.5)
    key_scale = key_valid * score_scale
    key_shift = (key_valid - 1.0) * 1e9

    channels = stem.shape[2]
    same = (
        lax.div(lax.broadcasted_iota(jnp.int32, (channels, channels), 0), GROUP)
        == lax.div(lax.broadcasted_iota(jnp.int32, (channels, channels), 1), GROUP)
    )
    same = jnp.where(same, 1.0, 0.0)

    def group_sum(values):
        wide = jnp.broadcast_to(values, (8, channels))
        return dot(wide, same, precision=lax.Precision.HIGHEST)[0:1]

    def standardize(j):
        w = stem[j].astype(F32)
        average = jnp.sum(w, axis=0, keepdims=True) * (1.0 / w.shape[0])
        w = w - average
        scale = lax.rsqrt(jnp.sum(w * w, axis=0, keepdims=True) * (1.0 / w.shape[0]) + 1e-5)
        std[j] = (w * scale).astype(BF16)
        wstat[j, 0:1, :] = average
        wstat[j, 1:2, :] = scale

    tile_rows = [(t * R, R) for t in range(L // R)]

    def stem_forward(j):
        count = 1.0 / (length * GROUP)
        total = jnp.zeros((1, channels), F32)
        for at, size in tile_rows:
            s = dot(feat[at : at + size, :], std[j])
            xhs[j, at : at + size, :] = s
            total = total + jnp.sum(s * valid_rows(at, size), axis=0, keepdims=True)
        average = group_sum(total) * count
        total = jnp.zeros((1, channels), F32)
        for at, size in tile_rows:
            s = xhs[j, at : at + size, :] - average
            total = total + jnp.sum(s * s * valid_rows(at, size), axis=0, keepdims=True)
        scale = lax.rsqrt(group_sum(total) * count + 1e-5)
        gst[j, 0:1, :] = scale
        for at, size in tile_rows:
            xh = (xhs[j, at : at + size, :] - average) * scale
            xhs[j, at : at + size, :] = xh
            value, slope = gelu_parts(xh * gvec[j, 0:1, :] + gvec[j, 1:2, :])
            act[j, at : at + size, :] = value.astype(BF16)
            dgs[j, at : at + size, :] = slope

    l_stem.wait()
    standardize(0)
    c_stem = [pass_on(stem_half[0])]
    l_feat.wait()
    stem_forward(0)
    c_stem.append(pass_on(stem_half[1]))
    c_gvec.wait_recv()
    c_embed = pass_on(embed_half[0])
    for copy in c_stem:
        copy.wait_recv()
    standardize(1)
    stem_forward(1)
    l_embed.wait()
    c_embed.wait_recv()

    def core_sum(product):
        xsend[0] = product(sib_rows).astype(BF16)
        copy = net.send(xsend.at[0], xrecv.at[0], place.sib)
        mine = product(own_rows)
        copy.wait_recv()
        net.sent(copy)
        return mine

    def embed_product(start):
        rows = pl.ds(start, R)
        return dot(act[0, rows, :], embed[0]) + dot(act[1, rows, :], embed[1])

    res1[...] = core_sum(embed_product)

    step = R // 2

    def layer_norm(res, other, add, gain, bias, xh_ref, scale_ref, out_ref, out_start, made):
        gain, bias = gain[...].reshape(1, -1), bias[...].reshape(1, -1)
        for t in range(2):
            rows = slice(t * step, (t + 1) * step)
            value = res[rows, :] + other[rows, :].astype(F32)
            if add is not None:
                value = value + add[rows, :]
            res[rows, :] = value
            average = jnp.sum(value, axis=1, keepdims=True) * (1.0 / D)
            value = value - average
            scale = lax.rsqrt(jnp.sum(value * value, axis=1, keepdims=True) * (1.0 / D) + 1e-6)
            xh = value * scale
            xh_ref[rows, :] = xh
            scale_ref[rows, :] = scale
            at = pl.ds(out_start + t * step, step)
            out_ref[at, :] = (xh * gain + bias).astype(BF16)
            made(at)

    layer_norm(
        res1, xrecv.at[0], None, first_gain, first_bias, xh1, rs1, n1, own_rows, lambda at: None
    )
    c_n1 = net.send(n1.at[pl.ds(own_rows, R)], n1.at[pl.ds(own_rows, R)], place.sib)
    l_pin.wait()
    c_n1.wait_recv()

    per_shard = pin.shape[1] // (3 * HEAD_DIM)

    width = 3 * HEAD_DIM
    pin_y = [net.plan(ref, ref, place.y_device) for ref, _ in pin_half]

    def pass_pin(i):
        pin_half[i][1].wait_recv()
        pin_y[i].start()

    def attend(h, carry):
        j, i = lax.div(h, per_shard), lax.rem(h, per_shard)
        for at in range(1, per_shard):

            @pl.when(h == at)
            def _():
                pass_pin(at)

        for at in range(per_shard):

            @pl.when(h == per_shard + at)
            def _():
                pin_y[at].wait_recv()

        @pl.when(h == per_shard + 1)
        def _():
            pout_half[0][1].wait_recv()
            pout_y.start()

        weight = pin[j, pl.ds(pl.multiple_of(i * width, 16), width), :]
        for at, size in tile_rows:
            packed = dot(n1[at : at + size, :], weight, 1, 1).astype(BF16)
            for t, ref in enumerate((q, k, v)):
                ref[h, at : at + size, :] = packed[:, t * HEAD_DIM : (t + 1) * HEAD_DIM]
        for at, size in tile_rows:
            s = dot(q[h, at : at + size, :], k[h], 1, 1) * key_scale + key_shift
            s = jnp.exp(s - jnp.max(s, axis=1, keepdims=True))
            p = (s * (1.0 / jnp.sum(s, axis=1, keepdims=True))).astype(BF16)
            probs[h, at : at + size, :] = p
            heads[h, at : at + size, :] = dot(p, v[h]).astype(BF16)
        return carry

    pass_pin(0)
    pout_y = net.plan(pout_half[0][0], pout_half[0][0], place.y_device)
    lax.fori_loop(0, 2 * per_shard, attend, 0)

    def side_by_side(pieces, store):
        at = 0
        while at < len(pieces):
            pair = pieces[at : at + 2]
            value = pair[0] if len(pair) == 1 else jnp.concatenate(pair, axis=1)
            store(slice(at * HEAD_DIM, at * HEAD_DIM + value.shape[1]), value)
            at += 2

    def store_mixed(lanes, value):
        mixed[:, lanes] = value

    side_by_side([heads[h] for h in range(2 * per_shard)], store_mixed)
    l_pout.wait()
    pout_y.wait_recv()
    out_width = pout.shape[1]

    def out_product(start):
        rows = pl.ds(start, R)
        return dot(mixed[rows, :], pout[...].reshape(-1, D))

    res2[...] = core_sum(out_product)
    c_n2 = []
    layer_norm(
        res2, xrecv.at[0], res1, second_gain, second_bias, xh2, rs2, n2,
        pl.multiple_of(place.m * R, 16),
        lambda at: c_n2.append(net.send(n2.at[at], n2.at[at], place.far)),
    )
    mine = block(place.m)
    c_n2_sib = net.send(n2.at[mine], n2.at[mine], place.sib)

    l_cot.wait()
    l_up.wait()
    l_down.wait()
    sm[...] = jnp.zeros_like(sm)

    def part(m, t):
        return pl.ds(pl.multiple_of(m * R + t * step, 16), step)

    def feed(m, t):
        rows = part(m, t)
        pre = dot(n2[rows, :], up[...]) + up_bias[...].reshape(1, -1)
        value, slope = gelu_parts(pre)
        hid[rows, :] = value.astype(BF16)
        grad = (dot(branch[rows, :], down[...], 1, 1) * slope).astype(BF16)
        preg[rows, :] = grad
        sm[4:5, :] = sm[4:5, :] + jnp.sum(grad.astype(F32), axis=0, keepdims=True)
        return dot(grad, up[...], 1, 1)

    def out_part(m):
        return dot(hid[block(m), :], down[...])

    def mask_branch(m, own_slot):
        rows = block(m)
        start = lax.rem(m, 2) * R
        branch[rows, :] = (
            branch[rows, :].astype(F32) * valid_of(own_slot, start)
        ).astype(BF16)

    mine_far = lax.broadcasted_iota(jnp.int32, (slices, 1), 0) == slot_slice[1 - x]
    far_length = jnp.sum(jnp.where(mine_far, lengths, 0.0), axis=0, keepdims=True)

    def valid_of(own_slot, start):
        at = (lax.broadcasted_iota(jnp.int32, (R, 1), 0) + start).astype(F32)
        return jnp.where(at < (length if own_slot else far_length), 1.0, 0.0)

    c_cot[0].wait_recv()
    f_rows = block(place.far_m)
    c_cot_fwd = net.send(branch.at[f_rows], branch.at[f_rows], place.sib)
    mask_branch(place.m, True)

    def feed_near(i, carry):
        t = lax.rem(i, 2)

        @pl.when(i == 2)
        def _():
            c_cot[1].wait_recv()
            c_n2_sib.wait_recv()
            mask_branch(place.sib_m, True)

        term = feed(jnp.where(i < 2, place.m, place.sib_m), t)
        rows = pl.ds(pl.multiple_of(t * step, 16), step)

        @pl.when(i < 2)
        def _():
            own[1, rows, :] = term

        @pl.when(i >= 2)
        def _():
            csend[1, 0, rows, :] = term.astype(BF16)

        return carry

    lax.fori_loop(0, 4, feed_near, 0)
    c_core = {}
    c_core[1, 0] = net.send(csend.at[1, 0], crecv.at[1, 0], place.sib)
    csend[0, 0] = out_part(place.sib_m).astype(BF16)
    c_core[0, 0] = net.send(csend.at[0, 0], crecv.at[0, 0], place.sib)
    own[0] = out_part(place.m)
    c_cot_fwd.wait_recv()
    net.sent(c_cot_fwd)
    mask_branch(place.far_sib_m, False)
    mask_branch(place.far_m, False)
    c_far = {}

    def feed_far(t):
        rows = pl.ds(t * step, step)
        c_n2[t].wait_recv()
        passed = n2.at[part(place.far_m, t)]
        passing = net.send(passed, passed, place.sib)
        sbuf[rows, 0:D] = feed(place.far_m, t)
        passing.wait_recv()
        csend[1, 1, rows, :] = feed(place.far_sib_m, t).astype(BF16)
        c_core[1, 1, t] = net.send(csend.at[1, 1, rows], crecv.at[1, 1, rows], place.sib)

    def feed_return(t):
        rows = pl.ds(t * step, step)
        c_core[1, 1, t].wait_recv()
        xsend[1, rows, :] = (sbuf[rows, 0:D] + crecv[1, 1, rows, :].astype(F32)).astype(BF16)
        c_far[1, t] = net.send(xsend.at[1, rows], xrecv.at[1, rows], place.far)

    feed_far(0)
    feed_return(0)
    feed_far(1)

    def result_send():
        csend[0, 1] = out_part(place.far_sib_m).astype(BF16)
        c_core[0, 1] = net.send(csend.at[0, 1], crecv.at[0, 1], place.sib)
        sbuf[:, 0:D] = out_part(place.far_m)
        c_core[0, 1].wait_recv()
        xsend[0] = (sbuf[:, 0:D] + crecv[0, 1].astype(F32)).astype(BF16)
        c_far[0] = net.send(xsend.at[0], xrecv.at[0], place.far)

    summed = {name: Summed(net, place, AWAY[name], BACK[name], **sums[name]) for name in GRADS}

    def keep(name, slot, at, value):
        ref = sums[name]["grad"]
        rows = ref.shape[-2]
        for t in range(value.shape[0] // rows):
            part = (at + t) // 2, (at + t) % 2
            ref[part if slot is None else (slot,) + part] = value[
                t * rows : (t + 1) * rows
            ].astype(BF16)

    half = D // 2
    third = hid.shape[1] // 3
    for i, name in enumerate(("down0", "down1", "down2")):
        keep(name, None, 0, dot(hid[:, i * third : (i + 1) * third], branch[...], 0, 0))
        summed[name].start()
        if i == 0:
            feed_return(1)
    third = D // 3
    for i, name in enumerate(("up0", "up1", "up2")):
        keep(name, None, 0, dot(n2[:, i * third : (i + 1) * third], preg[...], 0, 0))
        summed[name].start()

    def norm_back(grad_of, gain, xh_ref, scale_ref, kept, out_ref, out_start, row):
        gain = gain[...].reshape(1, -1)
        gain_sum = jnp.zeros((1, D), F32)
        bias_total = jnp.zeros((1, D), F32)
        for t in range(2):
            rows = slice(t * step, (t + 1) * step)
            dy, through = grad_of(rows)
            xh = xh_ref[rows, :]
            gain_sum = gain_sum + jnp.sum(dy * xh, axis=0, keepdims=True)
            bias_total = bias_total + jnp.sum(dy, axis=0, keepdims=True)
            dy = dy * gain
            mean_one = jnp.sum(dy, axis=1, keepdims=True) * (1.0 / D)
            mean_two = jnp.sum(dy * xh, axis=1, keepdims=True) * (1.0 / D)
            dx = through + scale_ref[rows, :] * (dy - mean_one - xh * mean_two)
            if kept is not None:
                kept[rows, :] = dx
            out_ref[pl.ds(out_start + t * step, step), :] = dx.astype(BF16)
        sm[row : row + 1, :] = gain_sum
        sm[row + 1 : row + 2, :] = bias_total

    own_part = pl.ds(own_rows, R)
    sg2, eb, sg = res1, mb, act
    copies = {}
    locals_left = []
    tasks = {}

    def task(number):
        def enter(function):
            tasks[number] = function

        return enter

    @task(NORM2)
    def norm2():
        c_core[1, 0].wait_recv()

        def grad_of(rows):
            c_far[1, rows.start // step].wait_recv()
            dy = own[1, rows, :] + crecv[1, 0, rows, :].astype(F32) + xrecv[1, rows, :].astype(F32)
            at = pl.ds(pl.multiple_of(place.m * R, 16) + rows.start, step)
            return dy, branch[at, :].astype(F32)

        norm_back(grad_of, second_gain, xh2, rs2, sg2, mb, own_rows, 2)
        copies["mb"] = net.send(mb.at[own_part], mb.at[own_part], place.sib)

    @task(RESULT)
    def result():
        c_core[0, 0].wait_recv()
        c_far[0].wait_recv()
        net.sent(c_core[0, 0])
        for t in range(2):
            rows = slice(t * step, (t + 1) * step)
            value = (
                res2[rows, :]
                + own[0, rows, :]
                + crecv[0, 0, rows, :].astype(F32)
                + xrecv[0, rows, :].astype(F32)
            )
            csend[0, 0, rows, :] = (value * valid_rows(own_rows + t * step, step)).astype(BF16)
        locals_left.append(net.local(csend.at[0, 0], block_out))

    @task(MIXED_BACK)
    def mixed_back():
        copies["mb"].wait_recv()
        value = dot(mixed[...], mb[...], 0, 0)
        shard = pout.shape[1]
        for j in range(2):
            rows = value[j * shard : (j + 1) * shard]
            for i in range(2):
                keep("pout", j, 2 * i, rows[:, i * half : (i + 1) * half])
        for at, size in tile_rows:
            value = dot(mb[at : at + size, :], pout[...].reshape(-1, D), 1, 1).astype(BF16)
            for h in range(2 * per_shard):
                heads[h, at : at + size, :] = value[:, h * HEAD_DIM : (h + 1) * HEAD_DIM]

    def head_back(h, carry):
        p = probs[h]
        dp = dot(heads[h], v[h], 1, 1)
        v[h] = dot(p, heads[h], 0, 0).astype(BF16)
        p = p.astype(F32)
        ds = (p * (dp - jnp.sum(p * dp, axis=1, keepdims=True))).astype(BF16)
        dq = (dot(ds, k[h]) * score_scale).astype(BF16)
        k[h] = (dot(ds, q[h], 0, 0) * score_scale).astype(BF16)
        q[h] = dq
        return carry

    def pin_back(j):
        lax.fori_loop(per_shard * j, per_shard * (j + 1), head_back, 0)

        def store_pg(lanes, value):
            pg[j, :, lanes] = value

        pieces = [ref[per_shard * j + h] for h in range(per_shard) for ref in (q, k, v)]
        side_by_side(pieces, store_pg)
        value = dot(pg[j], n1[...], 0, 0)
        wide = D // 6
        for i in range(6):
            keep("pin%d" % (i // 2), j, 2 * (i % 2), value[:, i * wide : (i + 1) * wide])

    @task(HEADS_FAR)
    def heads_far():
        pin_back(1)

    @task(HEADS_OWN)
    def heads_own():
        pin_back(0)

    @task(NORM1_SEND)
    def norm1_send():
        def product(start):
            rows = pl.ds(start, R)
            return dot(pg[0, rows, :], pin[0]) + dot(pg[1, rows, :], pin[1])

        width = pl.ds(0, D)
        sbuf[:, width] = product(sib_rows)
        copies["n1"] = net.send(sbuf.at[:, width], rbuf.at[:, width], place.sib)
        xh2[...] = product(own_rows)

    @task(NORM1)
    def norm1():
        copies["n1"].wait_recv()
        net.sent(copies["n1"])

        def grad_of(rows):
            return xh2[rows, :] + rbuf[rows, 0:D], sg2[rows, :]

        net.sent(copies["mb"])
        norm_back(grad_of, first_gain, xh1, rs1, None, eb, own_rows, 0)
        copies["eb"] = net.send(eb.at[own_part], eb.at[own_part], place.sib)

    def embed_back(j):
        keep("embed", j, 0, dot(act[j], eb[...], 0, 0))

    cin = feat.shape[1]
    square = pl.ds(0, cin // 4), pl.ds(0, channels)
    spares = [ref.at[square] for ref in (xh1, xh2, res1, own.at[1])]

    def stem_back(j):
        gain_sum = jnp.zeros((1, channels), F32)
        bias_total = jnp.zeros((1, channels), F32)
        for at, size in tile_rows:
            dz = dot(eb[at : at + size, :], embed[j], 1, 1) * dgs[j, at : at + size, :]
            dgs[j, at : at + size, :] = dz
            gain_sum = gain_sum + jnp.sum(dz * xhs[j, at : at + size, :], axis=0, keepdims=True)
            bias_total = bias_total + jnp.sum(dz, axis=0, keepdims=True)
        sm[5 + j : 6 + j, 0:channels] = gain_sum
        sm[5 + j : 6 + j, channels : 2 * channels] = bias_total
        gain = gvec[j, 0:1, :]
        count = 1.0 / (length * GROUP)
        mean_one = group_sum(bias_total * gain) * count
        mean_two = group_sum(gain_sum * gain) * count
        for at, size in tile_rows:
            part = dgs[j, at : at + size, :] * gain - valid_rows(at, size) * (
                mean_one + xhs[j, at : at + size, :] * mean_two
            )
            sg[j, at : at + size, :] = (part * gst[j, 0:1, :]).astype(BF16)
        average, scale = wstat[j, 0:1, :], wstat[j, 1:2, :]
        sum_one = jnp.zeros((1, channels), F32)
        sum_two = jnp.zeros((1, channels), F32)
        quarter = cin // 4
        for t in range(4):
            rows = slice(t * quarter, (t + 1) * quarter)
            grad = dot(feat[:, rows], sg[j], 0, 0)
            spare = spares[t]
            spare[...] = grad
            xh = (stem[j, rows, :].astype(F32) - average) * scale
            sum_one = sum_one + jnp.sum(grad, axis=0, keepdims=True)
            sum_two = sum_two + jnp.sum(grad * xh, axis=0, keepdims=True)
        sum_one = sum_one * (1.0 / cin)
        sum_two = sum_two * (1.0 / cin)
        for t in range(4):
            rows = slice(t * quarter, (t + 1) * quarter)
            xh = (stem[j, rows, :].astype(F32) - average) * scale
            value = (spares[t][...] - sum_one - xh * sum_two) * scale
            for i in range(2):
                lanes = slice(i * channels // 2, (i + 1) * channels // 2)
                keep("stem%d" % i, j, t, value[:, lanes])

    @task(STEM_FAR)
    def stem_far():
        copies["eb"].wait_recv()
        embed_back(1)
        stem_back(1)

    @task(STEM_OWN)
    def stem_own():
        embed_back(0)
        stem_back(0)
        small("core")

    def feature_product(start):
        rows = pl.ds(start, R)
        return dot(sg[0, rows, :], std[0], 1, 1) + dot(sg[1, rows, :], std[1], 1, 1)

    @task(FEATURES_SEND)
    def features_send():
        sbuf[...] = feature_product(sib_rows)
        copies["feat"] = net.send(sbuf, rbuf, place.sib)

    @task(FEATURES_SUM)
    def features_sum():
        copies["feat"].wait_recv()
        net.sent(copies["feat"])
        sbuf[...] = feature_product(own_rows) + rbuf[...]
        locals_left.append(net.local(sbuf, features_grad))

    small_at = {"core": place.sib}
    for name in "xyaw":
        small_at[name] = place.partner(name)[1]
    small_order = tuple(small_at)

    def small(name):
        copies["small"] = net.send(sm, smr.at[small_order.index(name)], small_at[name])

    def small_step(i):
        copies["small"].wait_recv()
        net.sent(copies["small"])
        if small_order[i] in ("core", "x"):
            sm[0:4, :] = sm[0:4, :] + smr[i, 0:4, :]
            if small_order[i] == "x":
                sm[5:6, :] = sm[5:6, :] + smr[i, 6:7, :]
        else:
            sm[...] = sm[...] + smr[i]
        if i + 1 < len(small_order):
            small(small_order[i + 1])
        else:
            o_small[...] = sm[...]

    small_next = list(range(len(small_order)))
    for what in ORDER:
        if what in tasks:
            tasks.pop(what)()
        elif what == SMALL:
            small_step(small_next.pop(0))
        elif what == ~RESULT:
            result_send()
        elif what < 0:
            summed[GRADS[~what]].start()
        else:
            summed[GRADS[what]].step()
    assert not tasks and not small_next
    for one in summed.values():
        one.step_all()
    for copy in locals_left:
        copy.wait()
    net.finish()


def finish(in_names, out_names, *refs):
    names = in_names + out_names
    r = dict(zip(names, refs))
    rest = refs[len(names) :]
    sems, passed, rest = rest[0], rest[1:3], rest[3:]
    held, made = rest[: len(GRADS)], rest[len(GRADS) :]
    made = dict(zip(("up", "down", "pout", "pin", "embed", "stem"), made))
    count = [0]
    going = []

    def move(src, dst):
        copy = pltpu.make_async_copy(src, dst, sems.at[count[0]])
        count[0] += 1
        copy.start()
        return copy

    order = GRADS
    held = dict(zip(GRADS, held))
    as_is = ("block_out", "features_grad")
    passing = [move(r["i_" + name], ref) for name, ref in zip(as_is, passed)]
    arriving = {name: move(r["i_" + name], held[name]) for name in order}
    small = r["i_small"]
    for i, name in enumerate(("g1", "b1", "g2", "b2", "ub")):
        r["o_" + name][...] = small[i, :]
    channels = r["o_gain"].shape[0]
    r["o_gain"][...] = small[5, 0:channels]
    r["o_shift"][...] = small[5, channels : 2 * channels]
    for name, ref, copy in zip(as_is, passed, passing):
        copy.wait()
        going.append(move(ref, r["o_" + name]))
    for name in order:
        arriving[name].wait()
        part = held[name]
        parts, rows, columns = part.shape
        name, number = name.rstrip("012"), int(name[-1]) if name[-1] in "012" else 0
        to = made[name]
        top, left = 0, 0
        if name in ("up", "down"):
            top, down = number * parts * rows, parts
        else:
            down = to.shape[0] // rows
            left = number * (parts // down) * columns
        for t in range(parts):
            at = top + t % down * rows
            lane = left + t // down * columns
            to[at : at + rows, lane : lane + columns] = part[t].astype(F32)
        if name in ("up", "down"):
            rows = pl.ds(top, parts * rows)
            going.append(move(to.at[rows], r["o_" + name].at[rows]))
        elif number == dict(pin=2, stem=1).get(name, 0):
            going.append(move(to, r["o_" + name]))
    for copy in going:
        copy.wait()


def body(
    features, stem_weight, group_gain, group_bias, embed_weight, first_gain, first_bias,
    project_in, project_out, second_gain, second_bias, up_weight, up_bias, down_weight,
    valid_mask, slot_slice, cotangent, *, dp,
):
    slots = slot_slice.shape[0]
    L = features.shape[0] // slots
    R = cotangent.shape[0]
    cin, channels = stem_weight.shape
    D = cotangent.shape[1]
    wide_in = project_in.shape[1]
    project_in = project_in.T
    out_rows = project_out.shape[0]
    hidden = up_weight.shape[1]
    heads = 2 * wide_in // (3 * HEAD_DIM)
    hbm = pl.BlockSpec(memory_space=pl.ANY)
    vmem = pl.BlockSpec(memory_space=pltpu.VMEM)
    smem = pl.BlockSpec(memory_space=pltpu.SMEM)
    in_specs = dict(
        features=hbm, stem_weight=hbm, group_gain=vmem, group_bias=vmem, embed_weight=hbm,
        first_gain=vmem, first_bias=vmem, project_in=hbm, project_out=hbm, second_gain=vmem,
        second_bias=vmem, up_weight=hbm, up_bias=vmem, down_weight=hbm, valid_mask=vmem,
        slot_slice=smem, cotangent=hbm,
    )
    parts = dict(
        up0=(D // 12, hidden),
        up1=(D // 12, hidden),
        up2=(D // 12, hidden),
        down0=(hidden // 12, D),
        down1=(hidden // 12, D),
        down2=(hidden // 12, D),
        pout=(out_rows // 2, D // 2),
        pin0=(wide_in // 2, D // 6),
        pin1=(wide_in // 2, D // 6),
        pin2=(wide_in // 2, D // 6),
        embed=(channels // 4, D),
        stem0=(cin // 4, channels // 2),
        stem1=(cin // 4, channels // 2),
    )
    outs = dict(
        block_out=((R, D), BF16, hbm),
        features_grad=((R, cin), F32, hbm),
        o_small=((8, D), F32, vmem),
    )
    for name in GRADS:
        outs["o_" + name] = ((2, 2) + parts[name], BF16, hbm)
    scratch = dict(
        feat=((L, cin), BF16), stem=((2, cin, channels), BF16), std=((2, cin, channels), BF16),
        wstat=((2, 8, channels), F32), embed=((2, channels, D), BF16), pin=((2, wide_in, D), BF16),
        pout=((2, out_rows, D), BF16), up=((D, hidden), BF16), down=((hidden, D), BF16),
        gvec=((2, 8, channels), F32), xhs=((2, L, channels), F32), dgs=((2, L, channels), F32),
        act=((2, L, channels), BF16), gst=((2, 8, channels), F32),
        sbuf=((R, cin), F32), rbuf=((R, cin), F32), res1=((R, D), F32), xh1=((R, D), F32),
        rs1=((R, 1), F32), n1=((L, D), BF16), q=((heads, L, HEAD_DIM), BF16),
        k=((heads, L, HEAD_DIM), BF16), v=((heads, L, HEAD_DIM), BF16), probs=((heads, L, L), BF16),
        heads=((heads, L, HEAD_DIM), BF16), mixed=((L, heads * HEAD_DIM), BF16),
        res2=((R, D), F32), xh2=((R, D), F32), rs2=((R, 1), F32), n2=((4 * R, D), BF16),
        hid=((4 * R, hidden), BF16), branch=((4 * R, D), BF16), preg=((4 * R, hidden), BF16),
        own=((2, R, D), F32), csend=((2, 2, R, D), BF16),
        crecv=((2, 2, R, D), BF16), xsend=((2, R, D), BF16), xrecv=((2, R, D), BF16),
        mb=((L, D), BF16), pg=((2, L, wide_in), BF16),
    )
    for name in GRADS:
        size = {dim: 2 for dim in "xyb" if dim in AWAY[name]}
        scratch["g_" + name] = (tuple(size.values()) + parts[name], BF16)
        for level, dim in enumerate(AWAY[name]):
            if dim != "a":
                size[dim] = 1
            scratch["r%d_" % level + name] = (tuple(size.values()) + parts[name], BF16)
    scratch.update(sm=((8, D), F32), smr=((5, 8, D), F32))
    copies = 168
    shapes = [pltpu.VMEM(*one) for one in scratch.values()]
    shapes += [pltpu.SemaphoreType.DMA((copies,)) for _ in range(2)]
    shapes += [pltpu.SemaphoreType.DMA((32,))]
    names = tuple(scratch) + ("send_sems", "recv_sems", "local_sems")
    results = pl.pallas_call(
        functools.partial(kernel, tuple(in_specs), tuple(outs), names),
        out_shape=[jax.ShapeDtypeStruct(shape, kind) for shape, kind, _ in outs.values()],
        in_specs=list(in_specs.values()),
        out_specs=[spec for _, _, spec in outs.values()],
        scratch_shapes=shapes,
        compiler_params=pltpu.CompilerParams(
            collective_id=0, has_side_effects=True, vmem_limit_bytes=62 * 2**20
        ),
        name="layer",
    )(
        features, stem_weight, group_gain, group_bias, embed_weight, first_gain, first_bias,
        project_in, project_out, second_gain, second_bias, up_weight, up_bias, down_weight,
        valid_mask, slot_slice, cotangent,
    )
    out = dict(zip(outs, results))

    wide = {name: out["o_" + name].reshape((4,) + parts[name]) for name in GRADS}
    small = out["o_small"]
    bit = NEAR
    if bit < dp:
        wide = {name: part.astype(F32) for name, part in wide.items()}
    while bit < dp:
        pairs = [(i, i ^ bit) for i in range(dp)]
        wide, small = jax.tree.map(
            lambda part: part + lax.ppermute(part, "dp", pairs), (wide, small)
        )
        bit *= 2

    inputs = {"i_" + name: wide[name] for name in GRADS}
    inputs.update(i_block_out=out["block_out"], i_features_grad=out["features_grad"], i_small=small)
    whole = dict(
        up=(D, hidden), down=(hidden, D), pout=(out_rows, D), pin=(wide_in, D),
        embed=(channels, D), stem=(cin, channels),
    )
    finals = dict(o_block_out=((R, D), BF16, hbm), o_features_grad=((R, cin), F32, hbm))
    for name, shape in whole.items():
        finals["o_" + name] = (shape, F32, hbm)
    for name in ("g1", "b1", "g2", "b2"):
        finals["o_" + name] = ((D,), F32, vmem)
    finals["o_ub"] = ((hidden,), F32, vmem)
    for name in ("gain", "shift"):
        finals["o_" + name] = ((channels,), F32, vmem)
    moved = pl.pallas_call(
        functools.partial(finish, tuple(inputs), tuple(finals)),
        out_shape=[jax.ShapeDtypeStruct(shape, kind) for shape, kind, _ in finals.values()],
        in_specs=[hbm] * (len(inputs) - 1) + [vmem],
        out_specs=[spec for _, _, spec in finals.values()],
        scratch_shapes=[pltpu.SemaphoreType.DMA((40,))]
        + [pltpu.VMEM((R, D), BF16), pltpu.VMEM((R, cin), F32)]
        + [pltpu.VMEM(wide[name].shape, wide[name].dtype) for name in GRADS]
        + [pltpu.VMEM(shape, F32) for shape in whole.values()],
        compiler_params=pltpu.CompilerParams(vmem_limit_bytes=62 * 2**20),
        name="finish",
    )(*inputs.values())
    done = dict(zip(finals, moved))
    return (
        done["o_block_out"],
        done["o_features_grad"],
        done["o_stem"],
        done["o_gain"],
        done["o_shift"],
        done["o_embed"],
        done["o_g1"],
        done["o_b1"],
        done["o_pin"].T,
        done["o_pout"],
        done["o_g2"],
        done["o_b2"],
        done["o_up"],
        done["o_ub"],
        done["o_down"],
    )


def solution(mesh):
    return jax.shard_map(
        functools.partial(body, dp=mesh.shape["dp"]),
        mesh=mesh,
        in_specs=(
            P("dp", None), P(None, "mp"), P("mp"), P("mp"), P("mp", None), P(), P(),
            P(None, "mp"), P("mp", None), P(), P(), P(None, "mp"), P("mp"), P("mp", None),
            P(), P("dp"), P(("dp", "mp"), None),
        ),
        out_specs=(
            P(("dp", "mp"), None), P(("dp", "mp"), None), P(None, "mp"), P("mp"), P("mp"),
            P("mp", None), P(), P(), P(None, "mp"), P("mp", None), P(), P(), P(None, "mp"),
            P("mp"), P("mp", None),
        ),
        check_vma=False,
    )
```
